128 devices in a mesh: section: 2 (over x_lo), tensor: 2 (over core), dp: 32 (over y, z, x_hi).
Axes of the slice: x: 4 (x_hi: 2, x_lo: 2; x = x_hi * 2 + x_lo), y: 4, z: 4, core: 2. Of those that a mesh axis runs over, the one named last changes fastest.
Arguments:
- tokens: bfloat16 [16384, 1024], P('dp'), may hold values from -6 to 6
- segments: int32 [16384], P('dp'), may hold values from 0 to 383, never falling along the last dimension, each value on 1 to 128 neighbouring positions
- cotangent: bfloat16 [16384, 1024], P('dp'), may hold values from -6 to 6
- gain_one: bfloat16 [2, 1024], P('section', ('tensor', 'dp')), may hold values from 0.5 to 1.5
- gain_two: bfloat16 [2, 1024], P('section', ('tensor', 'dp')), may hold values from 0.5 to 1.5
- w_query: bfloat16 [2, 1024, 512], P('section', 'dp', 'tensor'), may hold values from -0.1875 to 0.1875
- key_weight: bfloat16 [2, 1024, 128], P('section', 'dp', 'tensor'), may hold values from -0.1875 to 0.1875
- value_weight: bfloat16 [2, 1024, 128], P('section', 'dp', 'tensor'), may hold values from -0.1875 to 0.1875
- w_attn_out: bfloat16 [2, 512, 1024], P('section', 'tensor', 'dp'), may hold values from -0.5 to 0.5
- w_gate_ssm: bfloat16 [2, 1024, 1536], P('section', 'dp', 'tensor'), may hold values from -0.1875 to 0.1875
- w_ssm_in: bfloat16 [2, 1024, 1536], P('section', 'dp', 'tensor'), may hold values from -0.1875 to 0.1875
- w_step: bfloat16 [2, 1024, 24], P('section', 'dp', 'tensor'), may hold values from -0.1875 to 0.1875
- conv_ssm: bfloat16 [2, 4, 1536], P('section', None, ('tensor', 'dp')), may hold values from -3 to 3
- w_state: bfloat16 [2, 1024, 256], P('section', ('tensor', 'dp')), may hold values from -0.09375 to 0.09375
- conv_state: bfloat16 [2, 4, 256], P('section', None, ('tensor', 'dp')), may hold values from -3 to 3
- step_bias: float32 [2, 24], P('section', 'tensor'), may hold values from -6 to -2
- decay_log: float32 [2, 24], P('section', 'tensor'), may hold values from 0 to 2.7
- skip_gain: float32 [2, 24], P('section', 'tensor'), may hold values from 0.5 to 1.5
- w_ssm_out: bfloat16 [2, 1536, 1024], P('section', 'tensor', 'dp'), may hold values from -0.15625 to 0.15625
- w_ffn_gate: bfloat16 [2, 1024, 2048], P('section', 'dp', 'tensor'), may hold values from -0.1875 to 0.1875
- w_ffn_up: bfloat16 [2, 1024, 2048], P('section', 'dp', 'tensor'), may hold values from -0.1875 to 0.1875
- w_ffn_down: bfloat16 [2, 2048, 1024], P('section', 'tensor', 'dp'), may hold values from -0.125 to 0.125
Outputs:
- final: bfloat16 [16384, 1024], P('dp', 'section')
- input_grad: float32 [16384, 1024], P('dp', 'section')
- grad_gain_one: float32 [2, 1024], P('section', ('tensor', 'dp'))
- grad_gain_two: float32 [2, 1024], P('section', ('tensor', 'dp'))
- grad_query: float32 [2, 1024, 512], P('section', 'dp', 'tensor')
- grad_key: float32 [2, 1024, 128], P('section', 'dp', 'tensor')
- grad_value: float32 [2, 1024, 128], P('section', 'dp', 'tensor')
- grad_attn_out: float32 [2, 512, 1024], P('section', 'tensor', 'dp')
- grad_gate_ssm: float32 [2, 1024, 1536], P('section', 'dp', 'tensor')
- grad_ssm_in: float32 [2, 1024, 1536], P('section', 'dp', 'tensor')
- grad_step: float32 [2, 1024, 24], P('section', 'dp', 'tensor')
- grad_conv_ssm: float32 [2, 4, 1536], P('section', None, ('tensor', 'dp'))
- grad_state: float32 [2, 1024, 256], P('section', ('tensor', 'dp'))
- grad_conv_state: float32 [2, 4, 256], P('section', None, ('tensor', 'dp'))
- grad_step_bias: float32 [2, 24], P('section', 'tensor')
- grad_decay_log: float32 [2, 24], P('section', 'tensor')
- grad_skip: float32 [2, 24], P('section', 'tensor')
- grad_ssm_out: float32 [2, 1536, 1024], P('section', 'tensor', 'dp')
- grad_ffn_gate: float32 [2, 1024, 2048], P('section', 'dp', 'tensor')
- grad_ffn_up: float32 [2, 1024, 2048], P('section', 'dp', 'tensor')
- grad_ffn_down: float32 [2, 2048, 1024], P('section', 'tensor', 'dp')
The draws below stay inside these ranges and needn't reach their ends.
Inputs may be any that keep to these rules, and one draw needn't show every extreme that they name: `segments`: never falls along the tokens; each document has 1 to 128 tokens and one has exactly 128.
All inputs are finite; a program needn't handle non-finite values.
Results may differ from the reference program's by a relative error of at most 0.025.
Values may be sent and summed in bfloat16 or wider, within the bound.
A program may use at most 320 MiB of HBM per device.

```python
import math
from functools import partial
import jax
import jax.numpy as jnp
import numpy as np
from jax import lax

MODEL_WIDTH = 1024
QUERY_HEADS = 8
KEY_VALUE_HEADS = 2
HEAD_SIZE = 64
HM = 24
NS = 128
FF = 2048
KW = 4
SEQ = 128
TOKENS = 16384
LAYER_COUNT = 2


def steps_of(rng, extent, pieces, least, top_value):
    loudness, own = 1.0, jax.random.fold_in(rng, 6)
    for axis_at, blocks in pieces:
        steps = jnp.exp(jax.random.uniform(jax.random.fold_in(own, axis_at), (blocks,), jnp.float32, least / len(pieces), top_value / len(pieces)))
        loudness = loudness * jnp.repeat(steps, extent[axis_at] // blocks).reshape([-1 if axis == axis_at else 1 for axis in range(len(extent))])
    return loudness


def profile(count, total, most, slope):
    portions = [(1 << 20) // math.isqrt(grade ** slope) + 1 for grade in range(2, count + 1)]
    surplus, given = total - most - (count - 1), [1] * (count - 1)
    while surplus > 0:
        candidates = [i for i in range(count - 1) if given[i] < most]
        whole, remaining = sum([portions[i] for i in candidates]), surplus
        for i in candidates:
            addition = min(most - given[i], max(1, remaining * portions[i] // whole), surplus)
            given[i] = given[i] + addition
            surplus = surplus - addition
    return np.array([most] + given)


def uneven(stream_key, amount, total, most, skew):
    if amount == 2:
        one = jax.random.randint(stream_key, (), max(1, total - most), min(most, total - 1) + 1)
        return jnp.stack([one, total - one])
    tallies = jnp.asarray(profile(amount, total, most, skew), jnp.int32)
    pairs = (amount - 1) // 2
    giver, sink = tallies[1:1 + 2 * pairs:2], tallies[2:2 + 2 * pairs:2]
    room = jnp.minimum(giver - 1, most - sink)
    shifted = jax.random.randint(jax.random.fold_in(stream_key, 1), (pairs,), 0, 1 << 20) % (room + 1)
    tallies = tallies.at[1:1 + 2 * pairs:2].set(giver - shifted).at[2:2 + 2 * pairs:2].set(sink + shifted)
    return tallies[jax.random.permutation(jax.random.fold_in(stream_key, 2), amount)]


def centred(own_key, extent, spread, limit, split=(), kind=jnp.bfloat16):
    result = spread * jax.random.normal(own_key, extent, jnp.float32)
    if split:
        result = result * steps_of(own_key, extent, split, -0.22, 0.18)
    return jnp.clip(result, -limit, limit).astype(kind)


def setup_inputs(seed: int = 0) -> dict:
    streams_of = jax.random.split(jax.random.key(seed), 23)
    tokens = centred(streams_of[0], (TOKENS, MODEL_WIDTH), 1.0, 6.0, ((0, 32),))
    segments = jnp.searchsorted(jnp.cumsum(uneven(streams_of[1], TOKENS * 3 // SEQ, TOKENS, SEQ, 0)), jnp.arange(TOKENS), side="right").astype(jnp.int32)
    cotangent = centred(streams_of[2], (TOKENS, MODEL_WIDTH), 1.0, 6.0, ((0, 32),))
    gain_one = jnp.clip(1.0 + 0.1 * jax.random.normal(streams_of[3], (LAYER_COUNT, MODEL_WIDTH), jnp.float32), 0.5, 1.5).astype(jnp.bfloat16)
    gain_two = jnp.clip(1.0 + 0.1 * jax.random.normal(streams_of[4], (LAYER_COUNT, MODEL_WIDTH), jnp.float32), 0.5, 1.5).astype(jnp.bfloat16)
    w_query = centred(streams_of[5], (LAYER_COUNT, MODEL_WIDTH, QUERY_HEADS * HEAD_SIZE), MODEL_WIDTH ** -0.5, 0.1875, ((0, 2), (1, 32), (2, 2)))
    key_weight = centred(streams_of[6], (LAYER_COUNT, MODEL_WIDTH, KEY_VALUE_HEADS * HEAD_SIZE), MODEL_WIDTH ** -0.5, 0.1875, ((0, 2), (1, 32), (2, 2)))
    value_weight = centred(streams_of[7], (LAYER_COUNT, MODEL_WIDTH, KEY_VALUE_HEADS * HEAD_SIZE), MODEL_WIDTH ** -0.5, 0.1875, ((0, 2), (1, 32), (2, 2)))
    w_attn_out = centred(streams_of[8], (LAYER_COUNT, QUERY_HEADS * HEAD_SIZE, MODEL_WIDTH), (QUERY_HEADS * HEAD_SIZE // 4) ** -0.5, 0.5, ((0, 2), (1, 2), (2, 32)))
    w_gate_ssm = centred(streams_of[9], (LAYER_COUNT, MODEL_WIDTH, HM * HEAD_SIZE), MODEL_WIDTH ** -0.5, 0.1875, ((0, 2), (1, 32), (2, 2)))
    w_ssm_in = centred(streams_of[10], (LAYER_COUNT, MODEL_WIDTH, HM * HEAD_SIZE), MODEL_WIDTH ** -0.5, 0.1875, ((0, 2), (1, 32), (2, 2)))
    w_step = centred(streams_of[11], (LAYER_COUNT, MODEL_WIDTH, HM), MODEL_WIDTH ** -0.5, 0.1875, ((0, 2), (1, 32), (2, 2)))
    conv_ssm = centred(streams_of[12], (LAYER_COUNT, KW, HM * HEAD_SIZE), KW ** -0.5, 3.0, ((0, 2), (2, 64)))
    w_state = centred(streams_of[13], (LAYER_COUNT, MODEL_WIDTH, 2 * NS), (4 * MODEL_WIDTH) ** -0.5, 0.09375, ((0, 2), (1, 64)))
    conv_state = centred(streams_of[14], (LAYER_COUNT, KW, 2 * NS), KW ** -0.5, 3.0, ((0, 2), (2, 64)))
    step_bias = jnp.clip(-6.0 + 4.0 * jax.random.uniform(streams_of[15], (LAYER_COUNT, HM), jnp.float32) ** steps_of(streams_of[15], (LAYER_COUNT, HM), ((0, 2), (1, 2)), -0.2, 0.2), -6.0, -2.0)
    decay_log = jnp.clip(2.7 * jax.random.uniform(streams_of[16], (LAYER_COUNT, HM), jnp.float32) ** steps_of(streams_of[16], (LAYER_COUNT, HM), ((0, 2), (1, 2)), -0.2, 0.2), 0.0, 2.7)
    skip_gain = jnp.clip(0.5 + 1.0 * jax.random.uniform(streams_of[17], (LAYER_COUNT, HM), jnp.float32) ** steps_of(streams_of[17], (LAYER_COUNT, HM), ((0, 2), (1, 2)), -0.2, 0.2), 0.5, 1.5)
    w_ssm_out = centred(streams_of[18], (LAYER_COUNT, HM * HEAD_SIZE, MODEL_WIDTH), (HM * HEAD_SIZE) ** -0.5, 0.15625, ((0, 2), (1, 2), (2, 32)))
    w_ffn_gate = centred(streams_of[19], (LAYER_COUNT, MODEL_WIDTH, FF), MODEL_WIDTH ** -0.5, 0.1875, ((0, 2), (1, 32), (2, 2)))
    w_ffn_up = centred(streams_of[20], (LAYER_COUNT, MODEL_WIDTH, FF), MODEL_WIDTH ** -0.5, 0.1875, ((0, 2), (1, 32), (2, 2)))
    w_ffn_down = centred(streams_of[21], (LAYER_COUNT, FF, MODEL_WIDTH), FF ** -0.5, 0.125, ((0, 2), (1, 2), (2, 32)))
    return dict(tokens=tokens, segments=segments, cotangent=cotangent, gain_one=gain_one, gain_two=gain_two, w_query=w_query, key_weight=key_weight, value_weight=value_weight, w_attn_out=w_attn_out, w_gate_ssm=w_gate_ssm, w_ssm_in=w_ssm_in, w_step=w_step, conv_ssm=conv_ssm, w_state=w_state, conv_state=conv_state, step_bias=step_bias, decay_log=decay_log, skip_gain=skip_gain, w_ssm_out=w_ssm_out, w_ffn_gate=w_ffn_gate, w_ffn_up=w_ffn_up, w_ffn_down=w_ffn_down)


EPS = 1e-05
BASE = 10000.0
SCALE = 0.125
NEG = -1e+30
HIGH = lax.Precision.HIGHEST

@jax.custom_vjp
def low(v):
    return lax.optimization_barrier(v.astype(jnp.bfloat16)).astype(jnp.float32)

@jax.custom_vjp
def low_back(v):
    return v

def low_keep(v):
    return (low(v), None)

def low_pass(kept, grad):
    return (grad,)

def back_keep(v):
    return (v, None)

def back_low(kept, grad):
    return (low(grad),)
low.defvjp(low_keep, low_pass)
low_back.defvjp(back_keep, back_low)

def precise_product(left, right):
    return jnp.dot(left, right, precision=HIGH)

def seq_tables(segs):
    sequence_length = segs.shape[0]
    index = jnp.arange(sequence_length, dtype=jnp.int32)
    earlier = lax.optimization_barrier(jnp.sum((segs[None, :] < segs[:, None]).astype(jnp.int32), axis=1))
    position = (index - earlier).astype(jnp.float32)
    mask = (segs[None, :] == segs[:, None]) & (index[None, :] <= index[:, None])
    half = HEAD_SIZE // 2
    frequency = BASE ** (-2.0 * jnp.arange(half, dtype=jnp.float32) / HEAD_SIZE)
    angle = position[:, None] * frequency[None, :]
    return (mask, jnp.cos(angle)[:, None, :], jnp.sin(angle)[:, None, :])

def rms_scale(value_rows, gain):
    return value_rows * lax.rsqrt(lax.optimization_barrier(jnp.mean(value_rows * value_rows, axis=-1, keepdims=True)) + EPS) * gain

def apply_rotary(rotary_cosine, rotary_sine, value_rows):
    half = value_rows.shape[-1] // 2
    first = value_rows[..., :half]
    second = value_rows[..., half:]
    return jnp.concatenate([first * rotary_cosine - second * rotary_sine, second * rotary_cosine + first * rotary_sine], axis=-1)

def attend_weights(mask, scores):
    return jax.nn.softmax(jnp.where(mask, scores, NEG), axis=-1)

def conv_masked(segs, value_rows, kernel):
    sequence_length = value_rows.shape[0]
    width = kernel.shape[0]
    total = jnp.zeros_like(value_rows)
    for offset in range(width):
        moved = jnp.pad(value_rows, ((offset, 0), (0, 0)))[:sequence_length]
        seg_moved = jnp.pad(segs, (offset, 0), constant_values=-1)[:sequence_length]
        keep = seg_moved == segs
        total = total + jnp.where(keep[:, None], moved, 0.0) * kernel[width - 1 - offset]
    return total

def state_prepare(segs, raw, kernel):
    return jax.nn.silu(conv_masked(segs, raw, kernel))

def ssm_prepare(segs, mask, ssm_raw, step_raw, kernel, step_bias, decay_log):
    sequence_length = ssm_raw.shape[0]
    heads = step_raw.shape[1]
    conv_out = jax.nn.silu(conv_masked(segs, ssm_raw, kernel))
    delta = jax.nn.softplus(step_raw + step_bias)
    running = jnp.cumsum(-delta * jnp.exp(decay_log), axis=0)
    gap = running.T[:, :, None] - running.T[:, None, :]
    decay = jnp.where(mask, jnp.exp(jnp.where(mask, gap, 0.0)), 0.0)
    scaled = conv_out.reshape(sequence_length, heads, -1) * delta[:, :, None]
    return (conv_out, scaled, decay)

def gate_out(ssm_y, conv_out, gate_raw, skip_gain):
    sequence_length, heads, width = ssm_y.shape
    total = ssm_y + skip_gain[None, :, None] * conv_out.reshape(sequence_length, heads, width)
    return total.reshape(sequence_length, heads * width) * jax.nn.silu(gate_raw)

def swiglu(gate_up):
    half = gate_up.shape[1] // 2
    return jax.nn.silu(gate_up[:, :half]) * gate_up[:, half:]

def layer(inputs, params, segs):
    gain_one, gain_two, w_query, key_weight, value_weight, w_attn_out, w_gate_ssm, w_ssm_in, w_step, conv_ssm, w_state, conv_state, step_bias, decay_log, skip_gain, w_ssm_out, w_ffn_gate, w_ffn_up, w_ffn_down = params
    sequence_length = inputs.shape[0]
    mask, rotary_cosine, rotary_sine = seq_tables(segs)
    first_norm = low(rms_scale(inputs, gain_one))
    query_rows = low(apply_rotary(rotary_cosine, rotary_sine, low_back(precise_product(first_norm, w_query)).reshape(sequence_length, QUERY_HEADS, HEAD_SIZE)))
    key_rows = low(apply_rotary(rotary_cosine, rotary_sine, low_back(precise_product(first_norm, key_weight)).reshape(sequence_length, KEY_VALUE_HEADS, HEAD_SIZE)))
    value_rows = low(low_back(precise_product(first_norm, value_weight)).reshape(sequence_length, KEY_VALUE_HEADS, HEAD_SIZE))
    query_rows = query_rows.reshape(sequence_length, KEY_VALUE_HEADS, QUERY_HEADS // KEY_VALUE_HEADS, HEAD_SIZE)
    scores = low_back(jnp.einsum('ihgd,jhd->hgij', query_rows, key_rows, precision=HIGH) * SCALE)
    probs = low(attend_weights(mask, scores))
    attended = low(low_back(jnp.einsum('hgij,jhd->ihgd', probs, value_rows, precision=HIGH).reshape(sequence_length, QUERY_HEADS * HEAD_SIZE)))
    gate_raw = low_back(precise_product(first_norm, w_gate_ssm))
    ssm_raw = low_back(precise_product(first_norm, w_ssm_in))
    state_raw = low_back(precise_product(first_norm, w_state))
    step_raw = low_back(precise_product(first_norm, w_step))
    state_act = low(state_prepare(segs, state_raw, conv_state))
    conv_out, scaled, decay = ssm_prepare(segs, mask, ssm_raw, step_raw, conv_ssm, step_bias, decay_log)
    scaled = low(scaled)
    inner = low_back(precise_product(state_act[:, NS:], state_act[:, :NS].T))
    mixed = low(inner[None] * decay)
    ssm_y = low_back(jnp.einsum('hij,jhd->ihd', mixed, scaled, precision=HIGH))
    gated = low(gate_out(ssm_y, conv_out, gate_raw, skip_gain))
    mixer = low_back(precise_product(attended, w_attn_out) + precise_product(gated, w_ssm_out))
    middle = inputs + mixer
    norm_two = low(rms_scale(middle, gain_two))
    gate_up = jnp.concatenate([low_back(precise_product(norm_two, w_ffn_gate)), low_back(precise_product(norm_two, w_ffn_up))], axis=1)
    hidden = low(swiglu(gate_up))
    return middle + low_back(precise_product(hidden, w_ffn_down))

def run_layers(segs, inputs, stacked):
    first = tuple((weight[0] for weight in stacked))
    second = tuple((weight[1] for weight in stacked))

    def both(one_input, one_seg):
        between = low(low_back(layer(one_input, first, one_seg)))
        return layer(between, second, one_seg)
    return jax.vmap(both)(inputs, segs)

def reference(tokens, segments, cotangent, gain_one, gain_two, w_query, key_weight, value_weight, w_attn_out, w_gate_ssm, w_ssm_in, w_step, conv_ssm, w_state, conv_state, step_bias, decay_log, skip_gain, w_ssm_out, w_ffn_gate, w_ffn_up, w_ffn_down):
    weights = (gain_one, gain_two, w_query, key_weight, value_weight, w_attn_out, w_gate_ssm, w_ssm_in, w_step, conv_ssm, w_state, conv_state, step_bias, decay_log, skip_gain, w_ssm_out, w_ffn_gate, w_ffn_up, w_ffn_down)
    floats = tuple((weight.astype(jnp.float32) for weight in weights))
    count = TOKENS // SEQ
    bunch = math.gcd(count, max(1, 4096 // SEQ))
    rounds = count // bunch
    token_rows = tokens.astype(jnp.float32).reshape(rounds, bunch, SEQ, MODEL_WIDTH)
    seg_rows = segments.astype(jnp.int32).reshape(rounds, bunch, SEQ)
    grad_rows = cotangent.astype(jnp.float32).reshape(rounds, bunch, SEQ, MODEL_WIDTH)

    def visit(carry, item):
        inputs, segs, grad_out = item
        output, back = jax.vjp(partial(run_layers, segs), inputs, floats)
        grad_in, grad_weights = back(grad_out)
        carry = jax.tree.map(jnp.add, carry, grad_weights)
        return (carry, (output, grad_in))
    zeros = tuple((jnp.zeros_like(weight) for weight in floats))
    totals, (outputs, grad_ins) = lax.scan(visit, zeros, (token_rows, seg_rows, grad_rows))
    final = outputs.reshape(TOKENS, MODEL_WIDTH).astype(jnp.bfloat16)
    input_grad = grad_ins.reshape(TOKENS, MODEL_WIDTH)
    return (final, input_grad, totals[0], totals[1], totals[2], totals[3], totals[4], totals[5], totals[6], totals[7], totals[8], totals[9], totals[10], totals[11], totals[12], totals[13], totals[14], totals[15], totals[16], totals[17], totals[18])
```

```python
from functools import partial

import jax
import jax.numpy as jnp
from jax import lax
from jax.experimental import pallas as pl
from jax.experimental.pallas import tpu as pltpu
from jax.sharding import PartitionSpec as P

F32 = jnp.float32
BF16 = jnp.bfloat16
EPS = 1e-05
BASE = 10000.0
SCALE = 0.125
NEG = -1e30
SEQ = 128
ROWS = 256
D = 1024
HEAD = 64

W_OUT, W_FFN, W_DN, W_COLS = 2176, 3200, 5248, 6272
KF_X, KF_MID, KF_GATE, KF_SSM, KF_Y, KF_STEP, KF_STATE, KF_GU, KF_COLS = (
    0, 1024, 2048, 3584, 5120, 6656, 6912, 7168, 11264)
KB_N1, KB_N2, KB_Q, KB_KV, KB_AG, KB_HID, KB_COLS = 0, 1024, 2048, 2560, 2816, 4864, 6912
GB_OUT, GB_MID, GB_GU, GB_RAW, GB_ST, GB_COLS = 0, 1024, 2048, 6144, 10240, 10496
SM_G1, SM_G2, SM_CONV, SM_CST, SM_BIAS, SM_DEC, SM_SKIP = 0, 1, 2, 6, 10, 11, 12
SM_ROWS, SM_COLS = 16, 1536
VMEM_LIMIT = 60 * 1024 * 1024


def dot_plain(left, right):
    return jnp.dot(left, right, preferred_element_type=F32)


def dot_left(left, right):
    return lax.dot_general(left, right, (((0,), (0,)), ((), ())), preferred_element_type=F32)


def dot_right(left, right):
    return lax.dot_general(left, right, (((1,), (1,)), ((), ())), preferred_element_type=F32)


def dot_exact(left, right, dims):
    return lax.dot_general(
        left, right, (dims, ((), ())), preferred_element_type=F32, precision=lax.Precision.HIGHEST
    )


def lanes():
    lane = lax.broadcasted_iota(jnp.int32, (SEQ, 128), 1)
    wide = lax.broadcasted_iota(jnp.int32, (ROWS, 128), 1)
    return lane, lane < HEAD, wide < HEAD, (wide & 32) == 0


def swap_halves(v, first_half):
    return jnp.where(first_half, pltpu.roll(v, 96, 1), pltpu.roll(v, 32, 1))


def both_halves(v, low):
    turned = pltpu.roll(v.astype(F32), HEAD, 1).astype(BF16)
    return jnp.where(low, v, turned), jnp.where(low, turned, v)


def head_rows(pairs, low):
    zero = jnp.zeros_like(pairs[0])
    rows = []
    for pair in pairs:
        rows += [jnp.where(low, pair, zero), jnp.where(low, zero, pair)]
    return jnp.concatenate(rows, axis=0)


def conv_of(u, kernel, keeps):
    total = u * kernel[3]
    for o in (1, 2, 3):
        total = total + pltpu.roll(u, o, 0) * keeps[o] * kernel[3 - o]
    return total


def conv_back(u, g, kernel, keeps):
    back = g * kernel[3]
    sums = [None, None, None, jnp.sum(u * g, axis=0, keepdims=True)]
    for o in (1, 2, 3):
        kept = g * keeps[o]
        back = back + pltpu.roll(kept, ROWS - o, 0) * kernel[3 - o]
        sums[3 - o] = jnp.sum(pltpu.roll(u, o, 0) * kept, axis=0, keepdims=True)
    return back, sums


def softplus(v):
    return jnp.maximum(v, 0.0) + jnp.log1p(jnp.exp(-jnp.abs(v)))


def keeps_of(masks):
    pos = jnp.concatenate([jnp.sum(mask, axis=1, keepdims=True) for mask in masks]) - 1.0
    return [None] + [jnp.where(pos >= o, 1.0, 0.0) for o in (1, 2, 3)]


def softmax_rows(scores, mask4):
    scores = jnp.where(mask4, scores, NEG)
    e = jnp.exp(scores - jnp.max(scores, axis=1, keepdims=True))
    return e / jnp.sum(e, axis=1, keepdims=True)


def weight_copies(w_hbm, parts, sem):
    starts = {"mix": 0, "out": W_OUT, "ffn": W_FFN, "down": W_DN}
    copies = {}
    for k, (name, ref) in enumerate(parts):
        for t in range(2):
            copies[name, t] = pltpu.make_async_copy(
                w_hbm.at[t, :, pl.ds(starts[name], ref.shape[2])], ref.at[t], sem.at[2 * k + t])
            copies[name, t].start()
    return copies


def decay_of(running, turned, head, allowed):
    gap = running[:, head:head + 1] - turned[head:head + 1, :]
    return jnp.exp(jnp.where(allowed, gap, NEG))


def geometry(tab):
    cos, sin = tab[:, 0:128], tab[:, 128:256]
    masks = [tab[SEQ * s:SEQ * s + SEQ, 256:384] for s in range(2)]
    return cos, sin, masks, [mask > 0.5 for mask in masks], keeps_of(masks)


def per_sequence(v):
    return v[0:SEQ], v[SEQ:ROWS]


def fwd_body(sc, tok, recv, tab, sm, wst, w_hbm, out_ref, kf_hbm, kb_hbm,
             wmix, wout, wffn, wdn, kf, kb, wsem, osem):
    copies = weight_copies(
        w_hbm, (("mix", wmix), ("out", wout), ("ffn", wffn), ("down", wdn)), wsem)
    slot, first = sc[0], sc[1]
    _, low, low2, first_half = lanes()
    cos, sin, masks, allowed, keeps = geometry(tab)
    square = jnp.zeros((ROWS, 1), F32)
    for j in range(0, D, 256):
        x = jnp.where(first == 1, tok[:, j:j + 256], recv[:, j:j + 256]).astype(F32)
        kf[:, KF_X + j:KF_X + j + 256] = x
        square = square + jnp.sum(x * x, axis=1, keepdims=True)
    r = lax.rsqrt(square * (1.0 / D) + EPS)
    for j in range(0, D, 256):
        kb[:, KB_N1 + j:KB_N1 + j + 256] = (
            kf[:, KF_X + j:KF_X + j + 256] * r * sm[SM_G1:SM_G1 + 1, j:j + 256]).astype(BF16)
    n1 = kb[:, KB_N1:KB_N1 + D]

    state_raw = dot_plain(n1, wst[...])
    kf[:, KF_STATE:KF_STATE + 256] = state_raw
    pre = conv_of(state_raw, [sm[SM_CST + k:SM_CST + k + 1, 0:256] for k in range(4)], keeps)
    act = (pre * jax.nn.sigmoid(pre)).astype(BF16)
    inner = [dot_right(v[:, 128:256], v[:, 0:128]) for v in per_sequence(act)]

    for t in range(2):
        copies["mix", t].wait()
        qs = []
        raw = dot_plain(kb[:, KB_N1:KB_N1 + D], wmix[t, :, 0:256])
        for p in range(2):
            v = raw[:, 128 * p:128 * p + 128]
            qs.append((v * cos + swap_halves(v, first_half) * sin).astype(BF16))
            c = KB_Q + t * 256 + 128 * p
            kb[:, c:c + 128] = qs[p]
        raw = dot_plain(kb[:, KB_N1:KB_N1 + D], wmix[t, :, 256:512])
        v = raw[:, 0:128]
        kv = jnp.where(low2, v * cos + swap_halves(v, first_half) * sin, v).astype(BF16)
        kb[:, KB_KV + t * 128:KB_KV + t * 128 + 128] = kv
        step_raw = raw[:, 128:256]
        kf[:, KF_STEP + t * 128:KF_STEP + t * 128 + 128] = step_raw
        kk, vv = both_halves(kv, low2)
        for s in range(2):
            at = slice(SEQ * s, SEQ * s + SEQ)
            mask4 = jnp.concatenate([masks[s]] * 4, axis=0) > 0.5
            scores = dot_right(head_rows([q[at] for q in qs], low), kk[at]) * SCALE
            heads = dot_plain(softmax_rows(scores, mask4).astype(BF16), vv[at])
            for p in range(2):
                c = KB_AG + t * D + 128 * p
                kb[at, c:c + 128] = jnp.where(
                    low, heads[256 * p:256 * p + 128], heads[256 * p + 128:256 * p + 256]
                ).astype(BF16)

        delta = softplus(step_raw + sm[SM_BIAS:SM_BIAS + 1, t * 128:t * 128 + 128])
        rate = -delta * jnp.exp(sm[SM_DEC:SM_DEC + 1, t * 128:t * 128 + 128])
        running = [dot_exact(mask, v, ((1,), (0,))) for mask, v in zip(masks, per_sequence(rate))]
        turned = [v.T for v in running]
        for b in range(3):
            c0 = t * 768 + 256 * b
            gate2 = dot_plain(kb[:, KB_N1:KB_N1 + D], wmix[t, :, 512 + 256 * b:768 + 256 * b])
            kf[:, KF_GATE + c0:KF_GATE + c0 + 256] = gate2
            ssm2 = dot_plain(kb[:, KB_N1:KB_N1 + D], wmix[t, :, 1280 + 256 * b:1536 + 256 * b])
            kf[:, KF_SSM + c0:KF_SSM + c0 + 256] = ssm2
            for q in range(2):
                c = c0 + 128 * q
                h = 4 * b + 2 * q
                u = ssm2[:, 128 * q:128 * q + 128]
                pre = conv_of(
                    u, [sm[SM_CONV + k:SM_CONV + k + 1, c:c + 128] for k in range(4)], keeps)
                conv = pre * jax.nn.sigmoid(pre)
                scaled = (conv * jnp.where(low2, delta[:, h:h + 1], delta[:, h + 1:h + 2])
                          ).astype(BF16)
                for s in range(2):
                    at = slice(SEQ * s, SEQ * s + SEQ)
                    mixed = jnp.concatenate(
                        [(inner[s] * decay_of(running[s], turned[s], h + e, allowed[s])
                          ).astype(BF16) for e in range(2)], axis=1)
                    ssm_y = dot_plain(mixed, head_rows([scaled[at]], low))
                    kf[at, KF_Y + c:KF_Y + c + 128] = ssm_y
                    total = ssm_y + sm[SM_SKIP:SM_SKIP + 1, c:c + 128] * conv[at]
                    gate = kf[at, KF_GATE + c:KF_GATE + c + 128]
                    g = KB_AG + t * D + 256 + 256 * b + 128 * q
                    kb[at, g:g + 128] = (total * (gate * jax.nn.sigmoid(gate))).astype(BF16)

    copies["out", 0].wait()
    copies["out", 1].wait()
    square = jnp.zeros((ROWS, 1), F32)
    for j in range(0, D, 256):
        part = dot_right(kb[:, KB_AG:KB_AG + D], wout[0, j:j + 256, :]) + dot_right(
            kb[:, KB_AG + D:KB_AG + 2 * D], wout[1, j:j + 256, :])
        mid = kf[:, KF_X + j:KF_X + j + 256] + part
        kf[:, KF_MID + j:KF_MID + j + 256] = mid
        square = square + jnp.sum(mid * mid, axis=1, keepdims=True)
    r = lax.rsqrt(square * (1.0 / D) + EPS)
    for j in range(0, D, 256):
        kb[:, KB_N2 + j:KB_N2 + j + 256] = (
            kf[:, KF_MID + j:KF_MID + j + 256] * r * sm[SM_G2:SM_G2 + 1, j:j + 256]).astype(BF16)
    for t in range(2):
        copies["ffn", t].wait()
        for j in range(0, D, 256):
            gate = dot_plain(kb[:, KB_N2:KB_N2 + D], wffn[t, :, j:j + 256])
            up = dot_plain(kb[:, KB_N2:KB_N2 + D], wffn[t, :, D + j:D + j + 256])
            c = KF_GU + t * 2 * D + j
            kf[:, c:c + 256] = gate
            kf[:, c + D:c + D + 256] = up
            c = KB_HID + t * D + j
            kb[:, c:c + 256] = (gate * jax.nn.sigmoid(gate) * up).astype(BF16)
    save_f = pltpu.make_async_copy(kf, kf_hbm.at[slot], osem.at[0])
    save_b = pltpu.make_async_copy(kb, kb_hbm.at[slot], osem.at[1])
    save_f.start()
    save_b.start()
    copies["down", 0].wait()
    copies["down", 1].wait()
    for j in range(0, D, 256):
        part = dot_right(kb[:, KB_HID:KB_HID + D], wdn[0, j:j + 256, :]) + dot_right(
            kb[:, KB_HID + D:KB_HID + 2 * D], wdn[1, j:j + 256, :])
        out_ref[:, j:j + 256] = (kf[:, KF_MID + j:KF_MID + j + 256] + part).astype(BF16)
    save_f.wait()
    save_b.wait()


def bwd_body(sc, cot, recv, tab, sm, wst, w_hbm, kf_hbm, kb_hbm, gin_ref, ginb_ref, gb_hbm, sg_hbm,
             wmix, wout, wffn, wdn, kf, kb, gb, sg, gn, gmid, colsum, wsem, isem, osem):
    slot, first = sc[0], sc[1]
    loads = []
    for k, (a, b) in enumerate(((KF_GU, KF_COLS), (KF_X, KF_GATE), (KF_GATE, KF_GU))):
        loads.append(pltpu.make_async_copy(
            kf_hbm.at[slot, :, pl.ds(a, b - a)], kf.at[:, pl.ds(a, b - a)], isem.at[k]))
    loads.append(pltpu.make_async_copy(kb_hbm.at[slot], kb, isem.at[3]))
    loads[0].start()
    copies = weight_copies(w_hbm, (("down", wdn),), wsem)
    loads[1].start()
    copies.update(weight_copies(w_hbm, (("ffn", wffn),), wsem.at[pl.ds(2, 2)]))
    copies.update(weight_copies(w_hbm, (("out", wout),), wsem.at[pl.ds(4, 2)]))
    loads[2].start()
    loads[3].start()
    copies.update(weight_copies(w_hbm, (("mix", wmix),), wsem.at[pl.ds(6, 2)]))

    lane, low, low2, first_half = lanes()
    cos, sin, masks, allowed, keeps = geometry(tab)
    sg[...] = jnp.zeros_like(sg)

    for j in range(0, D, 256):
        gout = jnp.where(first == 1, recv[:, j:j + 256], cot[:, j:j + 256])
        gmid[:, j:j + 256] = gout.astype(F32)
        gb[:, GB_OUT + j:GB_OUT + j + 256] = gout
    loads[0].wait()
    for t in range(2):
        copies["down", t].wait()
        for j in range(0, D, 256):
            gh = dot_plain(gb[:, GB_OUT:GB_OUT + D], wdn[t, :, j:j + 256])
            c = KF_GU + t * 2 * D + j
            gate, up = kf[:, c:c + 256], kf[:, c + D:c + D + 256]
            s = jax.nn.sigmoid(gate)
            c = GB_GU + t * 2 * D + j
            gb[:, c:c + 256] = (gh * up * (s * (1.0 + gate * (1.0 - s)))).astype(BF16)
            gb[:, c + D:c + D + 256] = (gh * (gate * s)).astype(BF16)
    loads[1].wait()
    copies["ffn", 0].wait()
    copies["ffn", 1].wait()

    def norm_back(v0, gain_row):
        square = jnp.zeros((ROWS, 1), F32)
        cross = jnp.zeros((ROWS, 1), F32)
        for j in range(0, D, 256):
            v = kf[:, v0 + j:v0 + j + 256]
            square = square + jnp.sum(v * v, axis=1, keepdims=True)
            cross = cross + jnp.sum(
                v * gn[:, j:j + 256] * sm[gain_row:gain_row + 1, j:j + 256], axis=1, keepdims=True)
        r = lax.rsqrt(square * (1.0 / D) + EPS)
        factor = cross * (1.0 / D) * r * r * r
        for j in range(0, D, 256):
            v = kf[:, v0 + j:v0 + j + 256]
            g = gn[:, j:j + 256]
            sg[gain_row:gain_row + 1, j:j + 256] = jnp.sum(g * (v * r), axis=0, keepdims=True)
            gmid[:, j:j + 256] = gmid[:, j:j + 256] + (
                g * sm[gain_row:gain_row + 1, j:j + 256] * r - v * factor)

    for j in range(0, D, 256):
        gn[:, j:j + 256] = dot_right(gb[:, GB_GU:GB_GU + 2 * D], wffn[0, j:j + 256, :]) + dot_right(
            gb[:, GB_GU + 2 * D:GB_GU + 4 * D], wffn[1, j:j + 256, :])
    norm_back(KF_MID, SM_G2)
    for j in range(0, D, 256):
        gb[:, GB_MID + j:GB_MID + j + 256] = gmid[:, j:j + 256].astype(BF16)

    loads[2].wait()
    loads[3].wait()
    state_raw = kf[:, KF_STATE:KF_STATE + 256]
    cst = [sm[SM_CST + k:SM_CST + k + 1, 0:256] for k in range(4)]
    state_pre = conv_of(state_raw, cst, keeps)
    act = (state_pre * jax.nn.sigmoid(state_pre)).astype(BF16)
    acts = per_sequence(act)
    inner = [dot_right(v[:, 128:256], v[:, 0:128]) for v in acts]
    ginner = [jnp.zeros((SEQ, 128), F32), jnp.zeros((SEQ, 128), F32)]

    for t in range(2):
        copies["out", t].wait()
        raw0 = GB_RAW + t * 2 * D
        gatt = dot_plain(gb[:, GB_MID:GB_MID + D], wout[t, :, 0:256]).astype(BF16)
        kk, vv = both_halves(kb[:, KB_KV + t * 128:KB_KV + t * 128 + 128], low2)
        for s in range(2):
            at = slice(SEQ * s, SEQ * s + SEQ)
            mask4 = jnp.concatenate([masks[s]] * 4, axis=0) > 0.5
            gheads = head_rows([gatt[at, 0:128], gatt[at, 128:256]], low)
            c = KB_Q + t * 256
            qheads = head_rows([kb[at, c:c + 128], kb[at, c + 128:c + 256]], low)
            probs = softmax_rows(dot_right(qheads, kk[at]) * SCALE, mask4)
            gprobs = dot_right(gheads, vv[at])
            gscores = (probs * (gprobs - jnp.sum(probs * gprobs, axis=1, keepdims=True))
                       ).astype(BF16)
            gq = dot_plain(gscores, kk[at]) * SCALE
            turn, half = (cos[at], sin[at]), first_half[at]
            for p in range(2):
                v = jnp.where(low, gq[256 * p:256 * p + 128], gq[256 * p + 128:256 * p + 256])
                gb[at, raw0 + 128 * p:raw0 + 128 * p + 128] = (
                    v * turn[0] - swap_halves(v, half) * turn[1]).astype(BF16)
            gk = dot_left(gscores, qheads) * SCALE
            gk = gk + pltpu.roll(gk, HEAD, 1)
            gv = dot_left(probs.astype(BF16), gheads)
            gv = gv + pltpu.roll(gv, HEAD, 1)
            gb[at, raw0 + 256:raw0 + 384] = jnp.where(
                low, gk * turn[0] - swap_halves(gk, half) * turn[1], gv).astype(BF16)

        bias = sm[SM_BIAS:SM_BIAS + 1, t * 128:t * 128 + 128]
        speed = jnp.exp(sm[SM_DEC:SM_DEC + 1, t * 128:t * 128 + 128])
        step = kf[:, KF_STEP + t * 128:KF_STEP + t * 128 + 128] + bias
        delta = softplus(step)
        rate = -delta * speed
        running = [dot_exact(mask, v, ((1,), (0,))) for mask, v in zip(masks, per_sequence(rate))]
        turned = [v.T for v in running]
        grun = [jnp.zeros((SEQ, 128), F32), jnp.zeros((SEQ, 128), F32)]
        gdelta = jnp.zeros((ROWS, 128), F32)
        lane2 = jnp.concatenate([lane, lane], axis=0)
        colsum[...] = jnp.zeros_like(colsum)
        for b in range(3):
            gn[:, 0:256] = dot_plain(
                gb[:, GB_MID:GB_MID + D], wout[t, :, 256 + 256 * b:512 + 256 * b])
            for q in range(2):
                c = t * 768 + 256 * b + 128 * q
                h = 4 * b + 2 * q
                gg = gn[:, 128 * q:128 * q + 128]
                gate = kf[:, KF_GATE + c:KF_GATE + c + 128]
                kernel = [sm[SM_CONV + k:SM_CONV + k + 1, c:c + 128] for k in range(4)]
                skip = sm[SM_SKIP:SM_SKIP + 1, c:c + 128]
                pre = conv_of(kf[:, KF_SSM + c:KF_SSM + c + 128], kernel, keeps)
                sp = jax.nn.sigmoid(pre)
                conv = pre * sp
                wide = jnp.where(low2, delta[:, h:h + 1], delta[:, h + 1:h + 2])
                scaled = (conv * wide).astype(BF16)
                s = jax.nn.sigmoid(gate)
                gtotal = gg * (gate * s)
                total = kf[:, KF_Y + c:KF_Y + c + 128] + skip * conv
                k = raw0 + 512 + 256 * b + 128 * q
                gb[:, k:k + 128] = (gg * total * (s * (1.0 + gate * (1.0 - s)))).astype(BF16)
                sg[SM_SKIP:SM_SKIP + 1, c:c + 128] = jnp.sum(gtotal * conv, axis=0, keepdims=True)
                gtotal_b = gtotal.astype(BF16)
                gscaled = []
                for n in range(2):
                    at = slice(SEQ * n, SEQ * n + SEQ)
                    gy = head_rows([gtotal_b[at]], low)
                    gmixed = dot_right(gy, scaled[at])
                    mixed = []
                    for e in range(2):
                        decay = decay_of(running[n], turned[n], h + e, allowed[n])
                        weight = inner[n] * decay
                        mixed.append(weight.astype(BF16))
                        gm = gmixed[128 * e:128 * e + 128]
                        ginner[n] = ginner[n] + gm * decay
                        ggap = gm * weight
                        grun[n] = jnp.where(
                            lane == h + e, jnp.sum(ggap, axis=1, keepdims=True), grun[n])
                        colsum[n, h + e:h + e + 1, :] = jnp.sum(ggap, axis=0, keepdims=True)
                    gscaled.append(dot_left(jnp.concatenate(mixed, axis=0), gy))
                gscaled = jnp.concatenate(gscaled, axis=0)
                prod = gscaled * conv
                even = jnp.sum(jnp.where(low2, prod, 0.0), axis=1, keepdims=True)
                odd = jnp.sum(jnp.where(low2, 0.0, prod), axis=1, keepdims=True)
                gdelta = jnp.where(lane2 == h, even, jnp.where(lane2 == h + 1, odd, gdelta))
                gconv = gscaled * wide + gtotal * skip
                gpre = gconv * (sp * (1.0 + pre * (1.0 - sp)))
                gu, sums = conv_back(kf[:, KF_SSM + c:KF_SSM + c + 128], gpre, kernel, keeps)
                for k in range(4):
                    sg[SM_CONV + k:SM_CONV + k + 1, c:c + 128] = sums[k]
                k = raw0 + 1280 + 256 * b + 128 * q
                gb[:, k:k + 128] = gu.astype(BF16)
        grate = jnp.concatenate([
            dot_exact(masks[n], grun[n] - colsum[n].T, ((0,), (0,))) for n in range(2)], axis=0)
        gstep = (gdelta - grate * speed) * jax.nn.sigmoid(step)
        gb[:, raw0 + 384:raw0 + 512] = gstep.astype(BF16)
        c = t * 128
        sg[SM_BIAS:SM_BIAS + 1, c:c + 128] = jnp.sum(gstep, axis=0, keepdims=True)
        sg[SM_DEC:SM_DEC + 1, c:c + 128] = jnp.sum(grate * rate, axis=0, keepdims=True)

    gacts = []
    for n in range(2):
        gi = ginner[n].astype(BF16)
        gacts.append(jnp.concatenate(
            [dot_left(gi, acts[n][:, 128:256]), dot_plain(gi, acts[n][:, 0:128])], axis=1))
    gact = jnp.concatenate(gacts, axis=0)
    s = jax.nn.sigmoid(state_pre)
    gpre = gact * (s * (1.0 + state_pre * (1.0 - s)))
    gstate, sums = conv_back(state_raw, gpre, cst, keeps)
    for k in range(4):
        sg[SM_CST + k:SM_CST + k + 1, 0:256] = sums[k]
    gb[:, GB_ST:GB_ST + 256] = gstate.astype(BF16)
    save_g = pltpu.make_async_copy(gb, gb_hbm.at[slot], osem.at[0])
    save_g.start()

    copies["mix", 0].wait()
    copies["mix", 1].wait()
    for j in range(0, D, 256):
        gn[:, j:j + 256] = (
            dot_right(gb[:, GB_RAW:GB_RAW + 2 * D], wmix[0, j:j + 256, :])
            + dot_right(gb[:, GB_RAW + 2 * D:GB_RAW + 4 * D], wmix[1, j:j + 256, :])
            + dot_right(gb[:, GB_ST:GB_ST + 256], wst[j:j + 256, :]))
    norm_back(KF_X, SM_G1)
    for j in range(0, D, 256):
        gin_ref[:, j:j + 256] = gmid[:, j:j + 256]
        ginb_ref[:, j:j + 256] = gmid[:, j:j + 256].astype(BF16)
    save_s = pltpu.make_async_copy(sg, sg_hbm.at[slot], osem.at[1])
    save_s.start()
    save_g.wait()
    save_s.wait()


def any_spec():
    return pl.BlockSpec(memory_space=pl.ANY)


def vmem_spec():
    return pl.BlockSpec(memory_space=pltpu.VMEM)


def smem_spec():
    return pl.BlockSpec(memory_space=pltpu.SMEM)


def weight_scratch():
    return [pltpu.VMEM((2, D, 2 * D), BF16), pltpu.VMEM((2, D, D), BF16),
            pltpu.VMEM((2, D, 2 * D), BF16), pltpu.VMEM((2, D, D), BF16)]


def fwd_call(sc, tok, recv, tab, sm, wst, w, kept):
    def body(*refs):
        ins, rest = refs[:7], refs[7 + len(kept):]
        fwd_body(*ins, *rest)

    return pl.pallas_call(
        body,
        out_shape=(jax.ShapeDtypeStruct((ROWS, D), BF16),
                   jax.ShapeDtypeStruct((2, ROWS, KF_COLS), F32),
                   jax.ShapeDtypeStruct((2, ROWS, KB_COLS), BF16)),
        in_specs=[smem_spec()] + [vmem_spec()] * 5 + [any_spec()] * (1 + len(kept)),
        out_specs=(vmem_spec(), any_spec(), any_spec()),
        scratch_shapes=weight_scratch() + [
            pltpu.VMEM((ROWS, KF_COLS), F32), pltpu.VMEM((ROWS, KB_COLS), BF16),
            pltpu.SemaphoreType.DMA((8,)), pltpu.SemaphoreType.DMA((2,))],
        input_output_aliases={7: 1, 8: 2} if kept else {},
        compiler_params=pltpu.CompilerParams(vmem_limit_bytes=VMEM_LIMIT),
        name="layer_forward",
    )(sc, tok, recv, tab, sm, wst, w, *kept)


def bwd_call(sc, cot, recv, tab, sm, wst, w, kf, kb, grads):
    def body(*refs):
        ins, rest = refs[:9], refs[9 + len(grads):]
        bwd_body(*ins, *rest)

    return pl.pallas_call(
        body,
        out_shape=(jax.ShapeDtypeStruct((ROWS, D), F32),
                   jax.ShapeDtypeStruct((ROWS, D), BF16),
                   jax.ShapeDtypeStruct((2, ROWS, GB_COLS), BF16),
                   jax.ShapeDtypeStruct((2, SM_ROWS, SM_COLS), F32)),
        in_specs=[smem_spec()] + [vmem_spec()] * 5 + [any_spec()] * (3 + len(grads)),
        out_specs=(vmem_spec(), vmem_spec(), any_spec(), any_spec()),
        scratch_shapes=weight_scratch() + [
            pltpu.VMEM((ROWS, KF_COLS), F32), pltpu.VMEM((ROWS, KB_COLS), BF16),
            pltpu.VMEM((ROWS, GB_COLS), BF16), pltpu.VMEM((SM_ROWS, SM_COLS), F32),
            pltpu.VMEM((ROWS, D), F32), pltpu.VMEM((ROWS, D), F32), pltpu.VMEM((2, SEQ, 128), F32),
            pltpu.SemaphoreType.DMA((8,)), pltpu.SemaphoreType.DMA((4,)),
            pltpu.SemaphoreType.DMA((2,))],
        input_output_aliases={9: 2, 10: 3} if grads else {},
        compiler_params=pltpu.CompilerParams(vmem_limit_bytes=VMEM_LIMIT),
        name="layer_backward",
    )(sc, cot, recv, tab, sm, wst, w, kf, kb, *grads)


def tables_of(segs):
    index = jnp.arange(SEQ, dtype=jnp.int32)
    same = segs[:, None, :] == segs[:, :, None]
    mask = same & (index[None, None, :] <= index[None, :, None])
    pos = jnp.sum(mask, axis=2).astype(F32) - 1.0
    lane = jnp.arange(128, dtype=jnp.int32)
    frequency = BASE ** (-2.0 * (lane % 32).astype(F32) / HEAD)
    angle = pos[:, :, None] * frequency[None, None, :]
    sign = jnp.where((lane & 32) == 0, -1.0, 1.0)
    return jnp.concatenate(
        [jnp.cos(angle), jnp.sin(angle) * sign, mask.astype(F32)], axis=2).reshape(ROWS, 384)


A_COLS, B_COLS = W_FFN, W_COLS - W_FFN
MESH = pl.DeviceIdType.MESH


def where_am_i():
    core, d = lax.axis_index("tensor"), lax.axis_index("dp")
    return core, d // 8, (d // 2) % 4, d % 2


def place_on_dp(y, z, h):
    return {"dp": y * 8 + z * 2 + h}


class Copies:
    def __init__(self, send_sem, recv_sem):
        self.send_sem, self.recv_sem, self.all = send_sem, recv_sem, []

    def send(self, src, dst, device):
        k = len(self.all)
        copy = pltpu.make_async_remote_copy(
            src_ref=src, dst_ref=dst, send_sem=self.send_sem.at[k], recv_sem=self.recv_sem.at[k],
            device_id=device, device_id_type=MESH)
        copy.start()
        self.all.append(copy)
        return copy

    def drain(self):
        for copy in self.all:
            copy.wait_send()


def greet(core, y, z, h, more=()):
    barrier = pltpu.get_barrier_semaphore()
    others = [place_on_dp((y + 1) % 4, z, h), place_on_dp((y + 3) % 4, z, h),
              place_on_dp(y, (z + 1) % 4, h), place_on_dp(y, (z + 3) % 4, h),
              place_on_dp(y, z, 1 - h), {"tensor": 1 - core}]
    for other in (*others, *more):
        pl.semaphore_signal(barrier, inc=1, device_id=other, device_id_type=MESH)
    pl.semaphore_wait(barrier, len(others) + len(more))
    return others


GATHER_COPIES = 36


def gather_body(p, heads, w, all_heads, send_sem, recv_sem, own_sem):
    core, y, z, h = where_am_i()
    yp, ym, zp, zm, across, sibling = greet(core, y, z, h)
    own = pltpu.make_async_copy(p, w.at[core, y, z, h], own_sem.at[0])
    own.start()
    own_heads = pltpu.make_async_copy(heads, all_heads.at[core], own_sem.at[1])
    own_heads.start()
    net = Copies(send_sem, recv_sem)
    beside = [net.send(heads, all_heads.at[core], sibling)]
    partner = net.send(p, w.at[core, y, z, h], across)
    a, b = pl.ds(0, A_COLS), pl.ds(A_COLS, B_COLS)
    halves = ((a, pl.ds(0, 1664), pl.ds(1664, 1536), yp, ym, zp, zm),
              (b, pl.ds(A_COLS, 1536), pl.ds(A_COLS + 1536, 1536), zp, zm, yp, ym))

    def ring_block(k, step, hh, cols):
        if k == 0:
            return w.at[core, (y + step) % 4, z, hh, :, cols]
        return w.at[core, y, (z + step) % 4, hh, :, cols]

    def plane(k, step, cols):
        if k == 0:
            return w.at[core, :, (z + step) % 4, :, :, cols]
        return w.at[core, (y + step) % 4, :, :, :, cols]

    first = []
    for k, (cols, _, _, up, down, _, _) in enumerate(halves):
        mine = ring_block(k, 0, h, cols)
        first.append((k, h, net.send(p.at[:, cols], mine, up), net.send(p.at[:, cols], mine, down)))
    partner.wait_recv()
    for k, (cols, _, _, up, down, _, _) in enumerate(halves):
        theirs = ring_block(k, 0, 1 - h, cols)
        first.append((k, 1 - h, net.send(theirs, theirs, up), net.send(theirs, theirs, down)))
    second = []
    for k, hh, going_up, going_down in first:
        _, one, two, up, down, _, _ = halves[k]
        going_up.wait_recv()
        block = ring_block(k, 3, hh, one)
        second.append(net.send(block, block, up))
        going_down.wait_recv()
        block = ring_block(k, 1, hh, two)
        second.append(net.send(block, block, down))
    own.wait()
    own_heads.wait()
    third = []
    for k in range(2):
        cols, _, _, _, _, up, down = halves[k]
        for copy in (second[2 * k], second[2 * k + 1], second[4 + 2 * k], second[5 + 2 * k]):
            copy.wait_recv()
        mine = plane(k, 0, cols)
        third.append((net.send(mine, mine, up), net.send(mine, mine, down)))
        beside.append(net.send(mine, mine, sibling))
    fourth = []
    for k in range(2):
        cols, one, two, _, _, up, down = halves[k]
        third[k][0].wait_recv()
        block = plane(k, 3, one)
        fourth.append(net.send(block, block, up))
        block = plane(k, 3, cols)
        beside.append(net.send(block, block, sibling))
        third[k][1].wait_recv()
        block = plane(k, 1, two)
        fourth.append(net.send(block, block, down))
        block = plane(k, 1, cols)
        beside.append(net.send(block, block, sibling))
    for k in range(2):
        for e in range(2):
            fourth[2 * k + e].wait_recv()
            block = plane(k, 2, halves[k][1 + e])
            beside.append(net.send(block, block, sibling))
    for copy in beside:
        copy.wait_recv()
    net.drain()


def gather_weights(packed, heads):
    w, all_heads = pl.pallas_call(
        gather_body,
        out_shape=(jax.ShapeDtypeStruct((2, 4, 4, 2, 32, W_COLS), BF16),
                   jax.ShapeDtypeStruct((2, 8, 128), F32)),
        in_specs=[any_spec(), any_spec()],
        out_specs=(any_spec(), any_spec()),
        scratch_shapes=[pltpu.SemaphoreType.DMA((GATHER_COPIES,)),
                        pltpu.SemaphoreType.DMA((GATHER_COPIES,)), pltpu.SemaphoreType.DMA((2,))],
        compiler_params=pltpu.CompilerParams(collective_id=0, has_side_effects=True),
        name="gather_weights",
    )(packed, heads)
    return w, all_heads


REDUCE_COPIES = 45
ORDER = (2, 1, 3, 0)


def reduce_body(kb_hbm, gb_hbm, sg_hbm, leaving, staying, out, small, coming, stayed, kb, gb, sg, by_y,
                by_z, by_h, by_core, n1t, midt, n2t, outt, st, sent_a, sent_b, held_a,
                held_b, x1_a, x1_b, x2_a, x2_b, y1_a, y1_b, y2_a, y2_b, last, send_sem, recv_sem,
                load_sem):
    core, y, z, h = where_am_i()
    load_k = pltpu.make_async_copy(kb_hbm.at[0], kb, load_sem.at[0])
    load_g = pltpu.make_async_copy(gb_hbm.at[0], gb, load_sem.at[1])
    load_k.start()
    load_g.start()
    load_s = pltpu.make_async_copy(sg_hbm.at[0], sg, load_sem.at[2])
    load_s.start()
    section = lax.axis_index("section")
    yp, ym, zp, zm, across, sibling = greet(
        core, y, z, h, (place_on_dp((y + 2) % 4, z, h), place_on_dp(y, (z + 2) % 4, h),
                        {"section": 1 - section}, {"section": 1 - section, "tensor": 1 - core}))
    net = Copies(send_sem, recv_sem)

    def both(ref, c, n):
        return ref[:, pl.ds(c, n)]

    def turn(ref, c, to):
        for j in range(0, D, 256):
            v = both(ref, c + j, 256).T
            to[j // 256] = v.reshape(4, 64, 256)

    small_groups = (
        (by_y, y, [place_on_dp((y + k) % 4, z, h) for k in (1, 2, 3)]),
        (by_z, z, [place_on_dp(y, (z + k) % 4, h) for k in (1, 2, 3)]),
        (by_h, h, [across]), (by_core, core, [sibling]))

    def small_send(n, total):
        ref, at, others = small_groups[n]
        ref[at] = total
        return [net.send(ref.at[at], ref.at[at], other) for other in others]

    def small_sum(n, copies):
        for copy in copies:
            copy.wait_recv()
        ref = small_groups[n][0]
        total = ref[0] + ref[1]
        for k in range(2, ref.shape[0]):
            total = total + ref[k]
        return total

    load_s.wait()
    small_copies = small_send(0, sg[...])
    rows = pl.ds(pl.multiple_of(core * 256, 256), 256)
    kept_here = pltpu.make_async_copy(staying, stayed.at[rows], load_sem.at[3])
    kept_here.start()
    moved = [net.send(staying, stayed.at[rows], sibling),
             net.send(leaving, coming.at[rows], {"section": 1 - section}),
             net.send(leaving, coming.at[rows], {"section": 1 - section, "tensor": 1 - core})]

    load_k.wait()
    turn(kb, KB_N1, n1t)
    turn(kb, KB_N2, n2t)
    load_g.wait()
    turn(gb, GB_MID, midt)
    turn(gb, GB_OUT, outt)
    for j in range(4):
        v = dot_plain(n1t[j].reshape(256, 256), both(gb, GB_ST, 256)).astype(BF16)
        t, y0 = j // 2, 2 * (j % 2)
        v = v.reshape(2, 4, 2, 16, 256)
        st[t, y0] = v[0]
        st[t, y0 + 1] = v[1]

    def wide(base, t, count, j, size):
        return pl.multiple_of(base + t * count + j * size, 128)

    def tiles(n, step):
        pl.loop(0, n)(step)

    def chunk_a(i, t, ref, add):
        at = (z + ORDER[i]) % 4
        n1 = n1t[:, at].reshape(256, 256)
        mid = midt[:, at].reshape(256, 256)

        def put(v, c, n):
            where = (i, slice(None), pl.ds(c, n))
            ref[where] = (v + ref[where].astype(F32) if add else v).astype(BF16)

        def mix(j):
            put(dot_plain(n1, both(gb, wide(GB_RAW, t, 2 * D, j, 512), 512)),
                pl.multiple_of(j * 512, 128), 512)

        def outer(j):
            put(dot_plain(mid, both(kb, wide(KB_AG, t, D, j, 512), 512)),
                pl.multiple_of(W_OUT + j * 512, 128), 512)

        tiles(4, mix)
        v = st[t, :, at].astype(F32)
        v = jnp.concatenate([v[..., 0:128], v[..., 128:256]], axis=2).reshape(256, 128)
        put(v, 2 * D, 128)
        tiles(2, outer)

    def chunk_b(i, t, ref, add):
        at = (y + ORDER[i]) % 4
        n2 = n2t[at].reshape(256, 256)
        go = outt[at].reshape(256, 256)

        def put(v, c, n):
            where = (i, slice(None), pl.ds(c, n))
            ref[where] = (v + ref[where].astype(F32) if add else v).astype(BF16)

        def ffn(j):
            put(dot_plain(n2, both(gb, wide(GB_GU, t, 2 * D, j, 512), 512)),
                pl.multiple_of(j * 512, 128), 512)

        def down(j):
            put(dot_plain(go, both(kb, wide(KB_HID, t, D, j, 512), 512)),
                pl.multiple_of(2 * D + j * 512, 128), 512)

        tiles(4, ffn)
        tiles(2, down)

    def add_rows(ref, other, rows, cols):
        def step(j):
            at = pl.ds(pl.multiple_of(j * 32, 32), 32)
            ref[at, :] = (ref[at, :].astype(F32) + other[at, :].astype(F32)).astype(BF16)
        pl.loop(0, rows // 32)(step)

    def add_two(ref, one, two, rows):
        def step(j):
            at = pl.ds(pl.multiple_of(j * 32, 32), 32)
            ref[at, :] = (ref[at, :].astype(F32) + one[at, :].astype(F32)
                          + two[at, :].astype(F32)).astype(BF16)
        pl.loop(0, rows // 32)(step)

    halves = ((chunk_a, sent_a, held_a, x1_a, x2_a, zp, zm),
              (chunk_b, sent_b, held_b, x1_b, x2_b, yp, ym))
    beside = {}

    def for_sibling(i, k):
        chunk, sent, held = halves[k][:3]
        chunk(i, 1 - core, sent, False)
        beside[i, k] = net.send(sent.at[i], held.at[i], sibling)

    def for_self(i, k):
        chunk, sent, held = halves[k][:3]
        beside[i, k].wait_recv()
        chunk(i, core, held, True)

    low, high = pl.ds(0, 128), pl.ds(128, 128)
    far, near = {}, {}
    steps = [(i, k) for i in range(4) for k in range(2)]
    for_sibling(*steps[0])
    for n, (i, k) in enumerate(steps):
        if n + 1 < len(steps):
            for_sibling(*steps[n + 1])
        for_self(i, k)
        if n < 3:
            small_copies = small_send(n + 1, small_sum(n, small_copies))
        if n == 3:
            small[...] = small_sum(n, small_copies)
        held, x1, x2, up, down = halves[k][2:]
        if i == 0:
            far[k] = (net.send(held.at[0, low], x1.at[0], up),
                      net.send(held.at[0, high], x1.at[1], down))
        if i == 1:
            near[k] = [net.send(held.at[1, high], x2.at[0, high], up)]
        if i == 2:
            near[k].append(net.send(held.at[2, low], x2.at[1, low], down))
    for k in range(2):
        held, x1, x2, up, down = halves[k][2:]
        far[k][0].wait_recv()
        add_rows(held.at[1, low], x1.at[0], 128, None)
        near[k].append(net.send(held.at[1, low], x2.at[0, low], up))
        far[k][1].wait_recv()
        add_rows(held.at[2, high], x1.at[1], 128, None)
        near[k].append(net.send(held.at[2, high], x2.at[1, high], down))

    rings = ((held_a, y1_a, y2_a, yp, ym, y), (held_b, y1_b, y2_b, zp, zm, z))

    def rows_of(held, at, step, part):
        return held.at[3, pl.ds(pl.multiple_of(((at + step) % 4) * 64 + part * 32, 32), 32)]

    far, close = {}, {}
    for k in range(2):
        held, x1, x2, _, _ = halves[k][2:]
        for copy in near[k]:
            copy.wait_recv()
        add_two(held.at[3], x2.at[0], x2.at[1], 256)
        _, y1, y2, up, down, at = rings[k]
        far[k] = (net.send(rows_of(held, at, 2, 0), y1.at[0], up),
                  net.send(rows_of(held, at, 2, 1), y1.at[1], down))
        close[k] = [net.send(rows_of(held, at, 1, 1), y2.at[0, 1], up),
                    net.send(rows_of(held, at, 3, 0), y2.at[1, 0], down)]
    for k in range(2):
        held, y1, y2, up, down, at = rings[k]
        far[k][0].wait_recv()
        add_rows(rows_of(held, at, 1, 0), y1.at[0], 32, None)
        close[k].append(net.send(rows_of(held, at, 1, 0), y2.at[0, 0], up))
        far[k][1].wait_recv()
        add_rows(rows_of(held, at, 3, 1), y1.at[1], 32, None)
        close[k].append(net.send(rows_of(held, at, 3, 1), y2.at[1, 1], down))
    final = []
    for k in range(2):
        held, y1, y2, up, down, at = rings[k]
        for copy in close[k]:
            copy.wait_recv()
        for part in range(2):
            add_two(rows_of(held, at, 0, part), y2.at[0, part], y2.at[1, part], 32)
        cols = pl.ds(0, A_COLS) if k == 0 else pl.ds(A_COLS, B_COLS)
        final.append((cols, held, at, net.send(
            rows_of(held, at, 0, 1 - h), last.at[:, cols], across)))
    for cols, held, at, copy in final:
        copy.wait_recv()
        out[:, cols] = rows_of(held, at, 0, h)[...].astype(F32) + last[:, cols].astype(F32)
    kept_here.wait()
    for copy in moved:
        copy.wait_recv()
    net.drain()


def reduce_grads(kb, gb, sg, leaving, staying):
    def pair(cols, rows, count=2):
        return pltpu.VMEM((count, rows, cols), BF16)

    return pl.pallas_call(
        reduce_body,
        out_shape=(jax.ShapeDtypeStruct((32, W_COLS), F32),
                   jax.ShapeDtypeStruct((SM_ROWS, SM_COLS), F32),
                   jax.ShapeDtypeStruct((512, 512), BF16),
                   jax.ShapeDtypeStruct((512, 512), F32)),
        in_specs=[any_spec()] * 5,
        out_specs=(vmem_spec(), vmem_spec(), any_spec(), any_spec()),
        scratch_shapes=[
            pltpu.VMEM((ROWS, KB_COLS), BF16), pltpu.VMEM((ROWS, GB_COLS), BF16),
            pltpu.VMEM((SM_ROWS, SM_COLS), F32),
            *[pltpu.VMEM((n, SM_ROWS, SM_COLS), F32) for n in (4, 4, 2, 2)],
            *[pltpu.VMEM((4, 4, 64, 256), BF16)] * 4, pltpu.VMEM((2, 4, 4, 2, 16, 256), BF16),
            pair(A_COLS, 256, 4), pair(B_COLS, 256, 4), pair(A_COLS, 256, 4), pair(B_COLS, 256, 4),
            pair(A_COLS, 128), pair(B_COLS, 128), pair(A_COLS, 256), pair(B_COLS, 256),
            pair(A_COLS, 32), pair(B_COLS, 32),
            pltpu.VMEM((2, 2, 32, A_COLS), BF16), pltpu.VMEM((2, 2, 32, B_COLS), BF16),
            pltpu.VMEM((32, W_COLS), BF16),
            pltpu.SemaphoreType.DMA((REDUCE_COPIES,)), pltpu.SemaphoreType.DMA((REDUCE_COPIES,)),
            pltpu.SemaphoreType.DMA((4,))],
        compiler_params=pltpu.CompilerParams(
            collective_id=1, has_side_effects=True, vmem_limit_bytes=VMEM_LIMIT),
        name="reduce_grads",
    )(kb, gb, sg, leaving, staying)


def spread(values, each, whole):
    turn = lax.broadcasted_iota(jnp.int32, (128, whole), 0)
    lane = lax.broadcasted_iota(jnp.int32, (128, whole), 1)
    line = lax.broadcasted_iota(jnp.int32, (64, whole), 0)
    where = lax.broadcasted_iota(jnp.int32, (64, whole), 1)
    pick = jnp.where((lane % each == turn) & (turn < each), 1.0, 0.0).astype(BF16)
    return jnp.sum(
        jnp.where(where // each == line, dot_plain(values, pick), 0.0), axis=0, keepdims=True)


def prepare_body(w, heads, sm, wst, tile, sem):
    copies = [pltpu.make_async_copy(
        w.at[:, :, :, :, pl.ds(0, 16), pl.ds(384, 128)], tile, sem.at[0])]
    for t in range(2):
        for half in range(2):
            copies.append(pltpu.make_async_copy(
                w.at[t, :, :, :, pl.ds(16 * half, 16), pl.ds(2 * D, 128)],
                wst.at[t, :, :, :, :, pl.ds(128 * half, 128)], sem.at[1 + 2 * t + half]))
    for copy in copies:
        copy.start()
    sm[...] = jnp.zeros_like(sm)
    for t in range(2):
        sm[SM_BIAS:SM_BIAS + 1, 128 * t:128 * t + 128] = heads[t, 0:1, :]
        sm[SM_DEC:SM_DEC + 1, 128 * t:128 * t + 128] = heads[t, 1:2, :]
        for p in range(6):
            c = 768 * t + 128 * p
            lane = lax.broadcasted_iota(jnp.int32, (1, 128), 1)
            sm[SM_SKIP:SM_SKIP + 1, c:c + 128] = jnp.where(
                lane < HEAD, heads[t, 2:3, 2 * p:2 * p + 1], heads[t, 2:3, 2 * p + 1:2 * p + 2])
    copies[0].wait()
    lines = tile[...].reshape(64, 16, 128).astype(F32)

    def line(row, first):
        return pltpu.roll(lines[:, row, :], 128 - first, 1).astype(BF16)

    sm[SM_G1:SM_G1 + 1, 0:D] = spread(line(0, 12), 16, D)
    sm[SM_G2:SM_G2 + 1, 0:D] = spread(line(0, 28), 16, D)
    for k in range(4):
        sm[SM_CONV + k:SM_CONV + k + 1, :] = spread(line(1, 12 + 24 * k), 24, SM_COLS)
        sm[SM_CST + k:SM_CST + k + 1, 0:256] = spread(line(0, 44 + 4 * k), 4, 256)
    for copy in copies[1:]:
        copy.wait()


def prepare(w, all_heads):
    sm, wst = pl.pallas_call(
        prepare_body,
        out_shape=(jax.ShapeDtypeStruct((SM_ROWS, SM_COLS), F32),
                   jax.ShapeDtypeStruct((2, 4, 4, 2, 16, 256), BF16)),
        in_specs=[any_spec(), vmem_spec()],
        out_specs=(vmem_spec(), vmem_spec()),
        scratch_shapes=[pltpu.VMEM((2, 4, 4, 2, 16, 128), BF16), pltpu.SemaphoreType.DMA((5,))],
        compiler_params=pltpu.CompilerParams(vmem_limit_bytes=VMEM_LIMIT),
        name="prepare_small",
    )(w, all_heads)
    return sm, wst.reshape(D, 256)


def finish_body(at, red, small, coming, stayed, final, igrad, g1, g2, query, key, value, attn,
                gate, ssm, step, conv, state, cst, bias, dec, skip, ssm_out, ffn_gate, ffn_up,
                ffn_down):
    first, core, place = at[0], at[1], at[2]
    final[...] = jnp.where(first == 1, coming[...], stayed[...].astype(BF16))
    igrad[...] = jnp.where(first == 1, stayed[...], coming[...].astype(F32))
    query[0] = red[:, 0:256]
    kv = red[:, 256:384]
    key[0] = kv[:, 0:64]
    value[0] = pltpu.roll(kv, 64, 1)[:, 0:64]
    step[0] = red[:, 384:512][:, 0:12]
    gate[0] = red[:, 512:1280]
    ssm[0] = red[:, 1280:2048]
    state[0, :, 0:128] = red[0:16, 2 * D:W_OUT]
    state[0, :, 128:256] = red[16:32, 2 * D:W_OUT]
    attn[0] = red[:, W_OUT:W_OUT + 256].T
    ssm_out[0] = red[:, W_OUT + 256:W_FFN].T
    ffn_gate[0] = red[:, W_FFN:W_FFN + D]
    ffn_up[0] = red[:, W_FFN + D:W_DN]
    ffn_down[0] = red[:, W_DN:W_COLS].T

    def mine(rows, cols, size):
        v = small[rows, pl.ds(pl.multiple_of(place * size // 128 * 128, 128), cols)]
        return pltpu.roll(v, (cols - place * size % 128) % cols, 1)

    for k, (ref, size) in enumerate(((g1, 16), (g2, 16))):
        ref[...] = mine(pl.ds(0, 8), 128, size)[k:k + 1, 0:size]
    pair = jnp.concatenate([small[0:8, :], jnp.zeros((8, 128), F32)], axis=1)
    turned = pltpu.roll(pair, (SM_COLS + 128 - place * 24) % (SM_COLS + 128), 1)
    conv[0] = turned[SM_CONV:SM_CONV + 4, 0:24]
    tail = small[:, 0:256]
    turned = pltpu.roll(tail, (256 - place * 4) % 256, 1)
    cst[0] = turned[SM_CST:SM_CST + 4, 0:4]
    for row, ref in ((SM_BIAS, bias), (SM_DEC, dec)):
        v = small[8:16, pl.ds(pl.multiple_of(core * 128, 128), 128)]
        ref[...] = v[row - 8:row - 7, 0:12]
    lane = lax.broadcasted_iota(jnp.int32, (8, 128), 1)
    sums = jnp.zeros((8, 128), F32)
    for p in range(6):
        v = small[8:16, pl.ds(pl.multiple_of(core * 768 + 128 * p, 128), 128)]
        even = jnp.sum(jnp.where(lane < HEAD, v, 0.0), axis=1, keepdims=True)
        odd = jnp.sum(jnp.where(lane < HEAD, 0.0, v), axis=1, keepdims=True)
        sums = jnp.where(lane == 2 * p, even, jnp.where(lane == 2 * p + 1, odd, sums))
    skip[...] = sums[SM_SKIP - 8:SM_SKIP - 7, 0:12]


def finish(at, red, small, coming, stayed):
    shapes = [((512, 512), BF16)] + [(shape, F32) for shape in (
        (512, 512), (1, 16), (1, 16), (1, 32, 256), (1, 32, 64), (1, 32, 64), (1, 256, 32),
        (1, 32, 768), (1, 32, 768), (1, 32, 12), (1, 4, 24), (1, 16, 256), (1, 4, 4), (1, 12),
        (1, 12), (1, 12), (1, 768, 32), (1, 32, 1024), (1, 32, 1024), (1, 1024, 32))]
    return pl.pallas_call(
        finish_body,
        out_shape=tuple(jax.ShapeDtypeStruct(*shape) for shape in shapes),
        in_specs=[smem_spec()] + [vmem_spec()] * 4,
        out_specs=tuple(vmem_spec() for _ in shapes),
        compiler_params=pltpu.CompilerParams(vmem_limit_bytes=VMEM_LIMIT),
        name="finish_outputs",
    )(at, red, small, coming, stayed)


def local(tokens, segments, cotangent, gain_one, gain_two, w_query, key_weight, value_weight,
          w_attn_out, w_gate_ssm, w_ssm_in, w_step, conv_ssm, w_state, conv_state, step_bias,
          decay_log, skip_gain, w_ssm_out, w_ffn_gate, w_ffn_up, w_ffn_down):
    core = lax.axis_index("tensor")
    place = core * lax.axis_size("dp") + lax.axis_index("dp")
    first = lax.axis_index("section") == 0
    first_i = first.astype(jnp.int32)

    state = w_state[0]
    spare = 116
    one = jnp.concatenate([gain_one[0], gain_two[0], conv_state[0].ravel()])
    two = conv_ssm[0].ravel()
    smalls = jnp.concatenate([
        jnp.pad(v, (0, spare - v.shape[0]))[None] for v in (one, two)], axis=0)
    smalls = jnp.pad(smalls, ((0, 30), (0, 0)))
    heads = jnp.pad(jnp.concatenate([step_bias, decay_log, skip_gain]), ((0, 5), (0, 116)))
    packed = jnp.concatenate([
        w_query[0], key_weight[0], value_weight[0], w_step[0], smalls,
        w_gate_ssm[0], w_ssm_in[0], jnp.concatenate([state[:, 0:128], state[:, 128:256]], axis=0),
        w_attn_out[0].T, w_ssm_out[0].T, w_ffn_gate[0], w_ffn_up[0], w_ffn_down[0].T], axis=1)
    gathered, all_heads = gather_weights(packed, heads)
    sm, wst = prepare(gathered, all_heads)
    weights = gathered.reshape(2, D, W_COLS)

    tok = lax.dynamic_slice_in_dim(tokens, core * ROWS, ROWS)
    cot = lax.dynamic_slice_in_dim(cotangent, core * ROWS, ROWS)
    tab = tables_of(lax.dynamic_slice_in_dim(segments, core * ROWS, ROWS).reshape(2, SEQ))

    real_first = jnp.stack([jnp.where(first, 0, 1), first_i])
    real_second = jnp.stack([jnp.where(first, 1, 0), first_i])
    nothing = jnp.zeros((ROWS, D), BF16)
    out, *kept = fwd_call(real_first, tok, nothing, tab, sm, wst, weights, ())
    received = lax.ppermute(out, "section", [(0, 1)])
    out, *kept = fwd_call(real_second, tok, received, tab, sm, wst, weights, kept)
    _, gin_b, *grads = bwd_call(real_second, cot, nothing, tab, sm, wst, weights, *kept, ())
    received = lax.ppermute(gin_b, "section", [(1, 0)])
    gin, _, *grads = bwd_call(real_first, cot, received, tab, sm, wst, weights, *kept, grads)

    leaving = jnp.where(first, gin[:, 512:].astype(BF16), out[:, :512])
    staying = jnp.where(first, gin[:, :512], out[:, 512:].astype(F32))
    red, small, coming, stayed = reduce_grads(kept[1], grads[0], grads[1], leaving, staying)
    at = jnp.stack([first_i, core, place])
    return finish(at, red, small, coming, stayed)


def solution(mesh):
    rows = P("dp", None)
    flat = P("section", ("tensor", "dp"))
    split_in = P("section", "dp", "tensor")
    split_out = P("section", "tensor", "dp")
    kernel = P("section", None, ("tensor", "dp"))
    head = P("section", "tensor")
    state = P("section", ("tensor", "dp"), None)
    params = (flat, flat, split_in, split_in, split_in, split_out, split_in, split_in, split_in,
              kernel, state, kernel, head, head, head, split_out, split_in, split_in, split_out)
    halves = P("dp", "section")
    return jax.shard_map(
        local, mesh=mesh, in_specs=(rows, P("dp"), rows, *params),
        out_specs=(halves, halves, *params), check_vma=False)
```

```python
from functools import partial

import jax
import jax.numpy as jnp
from jax import lax
from jax.experimental import pallas as pl
from jax.experimental.pallas import tpu as pltpu
from jax.sharding import PartitionSpec as P

F32 = jnp.float32
BF16 = jnp.bfloat16
EPS = 1e-05
BASE = 10000.0
SCALE = 0.125
NEG = -1e30
SEQ = 128
ROWS = 256
D = 1024
HEAD = 64

W_OUT, W_FFN, W_DN, W_COLS = 2176, 3200, 5248, 6272
KF_X, KF_MID, KF_GATE, KF_SSM, KF_Y, KF_STEP, KF_STATE, KF_GU, KF_COLS = (
    0, 1024, 2048, 3584, 5120, 6656, 6912, 7168, 11264)
KB_N1, KB_N2, KB_Q, KB_KV, KB_AG, KB_HID, KB_COLS = 0, 1024, 2048, 2560, 2816, 4864, 6912
GB_OUT, GB_MID, GB_GU, GB_RAW, GB_ST, GB_COLS = 0, 1024, 2048, 6144, 10240, 10496
SM_G1, SM_G2, SM_CONV, SM_CST, SM_BIAS, SM_DEC, SM_SKIP = 0, 1, 2, 6, 10, 11, 12
SM_ROWS, SM_COLS = 16, 1536
VMEM_LIMIT = 60 * 1024 * 1024
AHEAD = 6


def dot_plain(left, right):
    return jnp.dot(left, right, preferred_element_type=F32)


def dot_left(left, right):
    return lax.dot_general(left, right, (((0,), (0,)), ((), ())), preferred_element_type=F32)


def dot_right(left, right):
    return lax.dot_general(left, right, (((1,), (1,)), ((), ())), preferred_element_type=F32)


def dot_exact(left, right, dims):
    return lax.dot_general(
        left, right, (dims, ((), ())), preferred_element_type=F32, precision=lax.Precision.HIGHEST
    )


def lanes():
    lane = lax.broadcasted_iota(jnp.int32, (SEQ, 128), 1)
    wide = lax.broadcasted_iota(jnp.int32, (ROWS, 128), 1)
    return lane, lane < HEAD, wide < HEAD, (wide & 32) == 0


def swap_halves(v, first_half):
    return jnp.where(first_half, pltpu.roll(v, 96, 1), pltpu.roll(v, 32, 1))


def both_halves(v, low):
    turned = pltpu.roll(v.astype(F32), HEAD, 1).astype(BF16)
    return jnp.where(low, v, turned), jnp.where(low, turned, v)


def head_rows(pairs, low):
    zero = jnp.zeros_like(pairs[0])
    rows = []
    for pair in pairs:
        rows += [jnp.where(low, pair, zero), jnp.where(low, zero, pair)]
    return jnp.concatenate(rows, axis=0)


def conv_of(u, kernel, keeps):
    total = u * kernel[3]
    for o in (1, 2, 3):
        total = total + pltpu.roll(u, o, 0) * keeps[o] * kernel[3 - o]
    return total


def conv_back(u, g, kernel, keeps):
    back = g * kernel[3]
    sums = [None, None, None, jnp.sum(u * g, axis=0, keepdims=True)]
    for o in (1, 2, 3):
        kept = g * keeps[o]
        back = back + pltpu.roll(kept, ROWS - o, 0) * kernel[3 - o]
        sums[3 - o] = jnp.sum(pltpu.roll(u, o, 0) * kept, axis=0, keepdims=True)
    return back, sums


def softplus(v):
    return jnp.maximum(v, 0.0) + jnp.log1p(jnp.exp(-jnp.abs(v)))


def keeps_of(masks):
    pos = jnp.concatenate([jnp.sum(mask, axis=1, keepdims=True) for mask in masks]) - 1.0
    return [None] + [jnp.where(pos >= o, 1.0, 0.0) for o in (1, 2, 3)]


def softmax_rows(scores, mask4):
    scores = jnp.where(mask4, scores, NEG)
    e = jnp.exp(scores - jnp.max(scores, axis=1, keepdims=True))
    return e / jnp.sum(e, axis=1, keepdims=True)


class Loads:
    def __init__(self, copies, ahead):
        self.copies, self.next, self.ahead = copies, 0, ahead
        self.start(ahead)

    def start(self, count):
        for copy in self.copies[self.next:self.next + count]:
            copy.start()
        self.next += count

    def wait(self, count=1):
        for _ in range(count):
            self.copies[self.next - self.ahead].wait()
            self.start(1)


def weight_loads(w_hbm, column, ref, sem):
    return [pltpu.make_async_copy(
        w_hbm.at[t, :, pl.ds(column, ref.shape[2])], ref.at[t], sem.at[t]) for t in range(2)]


def decay_of(running, turned, head, allowed):
    gap = running[:, head:head + 1] - turned[head:head + 1, :]
    return jnp.exp(jnp.where(allowed, gap, NEG))


def geometry(tab):
    cos, sin = tab[:, 0:128], tab[:, 128:256]
    masks = [tab[SEQ * s:SEQ * s + SEQ, 256:384] for s in range(2)]
    return cos, sin, masks, [mask > 0.5 for mask in masks], keeps_of(masks)


def per_sequence(v):
    return v[0:SEQ], v[SEQ:ROWS]


def fwd_body(sc, tok, recv, tab, sm, wst, w_hbm, out_ref, kf_hbm, kb_hbm,
             wmix, wout, wffn, wdn, kf, kb, wsem, osem):
    loads = Loads(
        weight_loads(w_hbm, 0, wmix, wsem) + weight_loads(w_hbm, W_OUT, wout, wsem.at[pl.ds(2, 2)])
        + weight_loads(w_hbm, W_FFN, wffn, wsem.at[pl.ds(4, 2)])
        + weight_loads(w_hbm, W_DN, wdn, wsem.at[pl.ds(6, 2)]), AHEAD)
    slot, first = sc[0], sc[1]
    _, low, low2, first_half = lanes()
    cos, sin, masks, allowed, keeps = geometry(tab)
    square = jnp.zeros((ROWS, 1), F32)
    for j in range(0, D, 256):
        x = jnp.where(first == 1, tok[:, j:j + 256], recv[:, j:j + 256]).astype(F32)
        kf[:, KF_X + j:KF_X + j + 256] = x
        square = square + jnp.sum(x * x, axis=1, keepdims=True)
    r = lax.rsqrt(square * (1.0 / D) + EPS)
    for j in range(0, D, 256):
        kb[:, KB_N1 + j:KB_N1 + j + 256] = (
            kf[:, KF_X + j:KF_X + j + 256] * r * sm[SM_G1:SM_G1 + 1, j:j + 256]).astype(BF16)
    n1 = kb[:, KB_N1:KB_N1 + D]

    state_raw = dot_plain(n1, wst[...])
    kf[:, KF_STATE:KF_STATE + 256] = state_raw
    pre = conv_of(state_raw, [sm[SM_CST + k:SM_CST + k + 1, 0:256] for k in range(4)], keeps)
    act = (pre * jax.nn.sigmoid(pre)).astype(BF16)
    inner = [dot_right(v[:, 128:256], v[:, 0:128]) for v in per_sequence(act)]

    for t in range(2):
        loads.wait()
        qs = []
        raw = dot_plain(kb[:, KB_N1:KB_N1 + D], wmix[t, :, 0:256])
        for p in range(2):
            v = raw[:, 128 * p:128 * p + 128]
            qs.append((v * cos + swap_halves(v, first_half) * sin).astype(BF16))
            c = KB_Q + t * 256 + 128 * p
            kb[:, c:c + 128] = qs[p]
        raw = dot_plain(kb[:, KB_N1:KB_N1 + D], wmix[t, :, 256:512])
        v = raw[:, 0:128]
        kv = jnp.where(low2, v * cos + swap_halves(v, first_half) * sin, v).astype(BF16)
        kb[:, KB_KV + t * 128:KB_KV + t * 128 + 128] = kv
        step_raw = raw[:, 128:256]
        kf[:, KF_STEP + t * 128:KF_STEP + t * 128 + 128] = step_raw
        kk, vv = both_halves(kv, low2)
        for s in range(2):
            at = slice(SEQ * s, SEQ * s + SEQ)
            mask4 = jnp.concatenate([masks[s]] * 4, axis=0) > 0.5
            scores = dot_right(head_rows([q[at] for q in qs], low), kk[at]) * SCALE
            heads = dot_plain(softmax_rows(scores, mask4).astype(BF16), vv[at])
            for p in range(2):
                c = KB_AG + t * D + 128 * p
                kb[at, c:c + 128] = jnp.where(
                    low, heads[256 * p:256 * p + 128], heads[256 * p + 128:256 * p + 256]
                ).astype(BF16)

        delta = softplus(step_raw + sm[SM_BIAS:SM_BIAS + 1, t * 128:t * 128 + 128])
        rate = -delta * jnp.exp(sm[SM_DEC:SM_DEC + 1, t * 128:t * 128 + 128])
        running = [dot_exact(mask, v, ((1,), (0,))) for mask, v in zip(masks, per_sequence(rate))]
        turned = [v.T for v in running]
        for b in range(3):
            c0 = t * 768 + 256 * b
            gate2 = dot_plain(kb[:, KB_N1:KB_N1 + D], wmix[t, :, 512 + 256 * b:768 + 256 * b])
            kf[:, KF_GATE + c0:KF_GATE + c0 + 256] = gate2
            ssm2 = dot_plain(kb[:, KB_N1:KB_N1 + D], wmix[t, :, 1280 + 256 * b:1536 + 256 * b])
            kf[:, KF_SSM + c0:KF_SSM + c0 + 256] = ssm2
            for q in range(2):
                c = c0 + 128 * q
                h = 4 * b + 2 * q
                u = ssm2[:, 128 * q:128 * q + 128]
                pre = conv_of(
                    u, [sm[SM_CONV + k:SM_CONV + k + 1, c:c + 128] for k in range(4)], keeps)
                conv = pre * jax.nn.sigmoid(pre)
                scaled = (conv * jnp.where(low2, delta[:, h:h + 1], delta[:, h + 1:h + 2])
                          ).astype(BF16)
                for s in range(2):
                    at = slice(SEQ * s, SEQ * s + SEQ)
                    mixed = jnp.concatenate(
                        [(inner[s] * decay_of(running[s], turned[s], h + e, allowed[s])
                          ).astype(BF16) for e in range(2)], axis=1)
                    ssm_y = dot_plain(mixed, head_rows([scaled[at]], low))
                    kf[at, KF_Y + c:KF_Y + c + 128] = ssm_y
                    total = ssm_y + sm[SM_SKIP:SM_SKIP + 1, c:c + 128] * conv[at]
                    gate = kf[at, KF_GATE + c:KF_GATE + c + 128]
                    g = KB_AG + t * D + 256 + 256 * b + 128 * q
                    kb[at, g:g + 128] = (total * (gate * jax.nn.sigmoid(gate))).astype(BF16)

    loads.wait(2)
    square = jnp.zeros((ROWS, 1), F32)
    for j in range(0, D, 256):
        part = dot_right(kb[:, KB_AG:KB_AG + D], wout[0, j:j + 256, :]) + dot_right(
            kb[:, KB_AG + D:KB_AG + 2 * D], wout[1, j:j + 256, :])
        mid = kf[:, KF_X + j:KF_X + j + 256] + part
        kf[:, KF_MID + j:KF_MID + j + 256] = mid
        square = square + jnp.sum(mid * mid, axis=1, keepdims=True)
    r = lax.rsqrt(square * (1.0 / D) + EPS)
    for j in range(0, D, 256):
        kb[:, KB_N2 + j:KB_N2 + j + 256] = (
            kf[:, KF_MID + j:KF_MID + j + 256] * r * sm[SM_G2:SM_G2 + 1, j:j + 256]).astype(BF16)
    for t in range(2):
        loads.wait()
        for j in range(0, D, 256):
            gate = dot_plain(kb[:, KB_N2:KB_N2 + D], wffn[t, :, j:j + 256])
            up = dot_plain(kb[:, KB_N2:KB_N2 + D], wffn[t, :, D + j:D + j + 256])
            c = KF_GU + t * 2 * D + j
            kf[:, c:c + 256] = gate
            kf[:, c + D:c + D + 256] = up
            c = KB_HID + t * D + j
            kb[:, c:c + 256] = (gate * jax.nn.sigmoid(gate) * up).astype(BF16)
    save_f = pltpu.make_async_copy(kf, kf_hbm.at[slot], osem.at[0])
    save_b = pltpu.make_async_copy(kb, kb_hbm.at[slot], osem.at[1])
    save_f.start()
    save_b.start()
    loads.wait(2)
    for j in range(0, D, 256):
        part = dot_right(kb[:, KB_HID:KB_HID + D], wdn[0, j:j + 256, :]) + dot_right(
            kb[:, KB_HID + D:KB_HID + 2 * D], wdn[1, j:j + 256, :])
        out_ref[:, j:j + 256] = (kf[:, KF_MID + j:KF_MID + j + 256] + part).astype(BF16)
    save_f.wait()
    save_b.wait()


def bwd_body(sc, cot, recv, tab, sm, wst, w_hbm, kf_hbm, kb_hbm, gin_ref, ginb_ref, gb_hbm, sg_hbm,
             wmix, wout, wffn, wdn, kf, kb, gb, sg, gn, gmid, colsum, wsem, isem, osem):
    slot, first = sc[0], sc[1]
    kept = [pltpu.make_async_copy(
        kf_hbm.at[slot, :, pl.ds(a, b - a)], kf.at[:, pl.ds(a, b - a)], isem.at[n])
        for n, (a, b) in enumerate(((KF_GU, KF_GU + 2 * D), (KF_GU + 2 * D, KF_COLS),
                                    (KF_X, KF_GATE), (KF_GATE, KF_GU)))]
    kept.append(pltpu.make_async_copy(kb_hbm.at[slot], kb, isem.at[4]))
    down = weight_loads(w_hbm, W_DN, wdn, wsem)
    ffn = weight_loads(w_hbm, W_FFN, wffn, wsem.at[pl.ds(2, 2)])
    outer = weight_loads(w_hbm, W_OUT, wout, wsem.at[pl.ds(4, 2)])
    mix = weight_loads(w_hbm, 0, wmix, wsem.at[pl.ds(6, 2)])
    loads = Loads([down[0], kept[0], down[1], kept[1], ffn[0], ffn[1], kept[2], outer[0], kept[4],
                   kept[3], outer[1], mix[0], mix[1]], AHEAD)

    lane, low, low2, first_half = lanes()
    cos, sin, masks, allowed, keeps = geometry(tab)
    sg[...] = jnp.zeros_like(sg)

    for j in range(0, D, 256):
        gout = jnp.where(first == 1, recv[:, j:j + 256], cot[:, j:j + 256])
        gmid[:, j:j + 256] = gout.astype(F32)
        gb[:, GB_OUT + j:GB_OUT + j + 256] = gout
    for t in range(2):
        loads.wait(2)
        for j in range(0, D, 256):
            gh = dot_plain(gb[:, GB_OUT:GB_OUT + D], wdn[t, :, j:j + 256])
            c = KF_GU + t * 2 * D + j
            gate, up = kf[:, c:c + 256], kf[:, c + D:c + D + 256]
            s = jax.nn.sigmoid(gate)
            c = GB_GU + t * 2 * D + j
            gb[:, c:c + 256] = (gh * up * (s * (1.0 + gate * (1.0 - s)))).astype(BF16)
            gb[:, c + D:c + D + 256] = (gh * (gate * s)).astype(BF16)
    loads.wait(2)

    def norm_back(v0, gain_row):
        square = jnp.zeros((ROWS, 1), F32)
        cross = jnp.zeros((ROWS, 1), F32)
        for j in range(0, D, 256):
            v = kf[:, v0 + j:v0 + j + 256]
            square = square + jnp.sum(v * v, axis=1, keepdims=True)
            cross = cross + jnp.sum(
                v * gn[:, j:j + 256] * sm[gain_row:gain_row + 1, j:j + 256], axis=1, keepdims=True)
        r = lax.rsqrt(square * (1.0 / D) + EPS)
        factor = cross * (1.0 / D) * r * r * r
        for j in range(0, D, 256):
            v = kf[:, v0 + j:v0 + j + 256]
            g = gn[:, j:j + 256]
            sg[gain_row:gain_row + 1, j:j + 256] = jnp.sum(g * (v * r), axis=0, keepdims=True)
            gmid[:, j:j + 256] = gmid[:, j:j + 256] + (
                g * sm[gain_row:gain_row + 1, j:j + 256] * r - v * factor)

    for j in range(0, D, 256):
        gn[:, j:j + 256] = dot_right(gb[:, GB_GU:GB_GU + 2 * D], wffn[0, j:j + 256, :]) + dot_right(
            gb[:, GB_GU + 2 * D:GB_GU + 4 * D], wffn[1, j:j + 256, :])
    loads.wait()
    norm_back(KF_MID, SM_G2)
    for j in range(0, D, 256):
        gb[:, GB_MID + j:GB_MID + j + 256] = gmid[:, j:j + 256].astype(BF16)

    loads.wait(3)
    state_raw = kf[:, KF_STATE:KF_STATE + 256]
    cst = [sm[SM_CST + k:SM_CST + k + 1, 0:256] for k in range(4)]
    state_pre = conv_of(state_raw, cst, keeps)
    act = (state_pre * jax.nn.sigmoid(state_pre)).astype(BF16)
    acts = per_sequence(act)
    inner = [dot_right(v[:, 128:256], v[:, 0:128]) for v in acts]
    ginner = [jnp.zeros((SEQ, 128), F32), jnp.zeros((SEQ, 128), F32)]

    for t in range(2):
        if t == 1:
            loads.wait()
        raw0 = GB_RAW + t * 2 * D
        gatt = dot_plain(gb[:, GB_MID:GB_MID + D], wout[t, :, 0:256]).astype(BF16)
        kk, vv = both_halves(kb[:, KB_KV + t * 128:KB_KV + t * 128 + 128], low2)
        for s in range(2):
            at = slice(SEQ * s, SEQ * s + SEQ)
            mask4 = jnp.concatenate([masks[s]] * 4, axis=0) > 0.5
            gheads = head_rows([gatt[at, 0:128], gatt[at, 128:256]], low)
            c = KB_Q + t * 256
            qheads = head_rows([kb[at, c:c + 128], kb[at, c + 128:c + 256]], low)
            probs = softmax_rows(dot_right(qheads, kk[at]) * SCALE, mask4)
            gprobs = dot_right(gheads, vv[at])
            gscores = (probs * (gprobs - jnp.sum(probs * gprobs, axis=1, keepdims=True))
                       ).astype(BF16)
            gq = dot_plain(gscores, kk[at]) * SCALE
            turn, half = (cos[at], sin[at]), first_half[at]
            for p in range(2):
                v = jnp.where(low, gq[256 * p:256 * p + 128], gq[256 * p + 128:256 * p + 256])
                gb[at, raw0 + 128 * p:raw0 + 128 * p + 128] = (
                    v * turn[0] - swap_halves(v, half) * turn[1]).astype(BF16)
            gk = dot_left(gscores, qheads) * SCALE
            gk = gk + pltpu.roll(gk, HEAD, 1)
            gv = dot_left(probs.astype(BF16), gheads)
            gv = gv + pltpu.roll(gv, HEAD, 1)
            gb[at, raw0 + 256:raw0 + 384] = jnp.where(
                low, gk * turn[0] - swap_halves(gk, half) * turn[1], gv).astype(BF16)

        bias = sm[SM_BIAS:SM_BIAS + 1, t * 128:t * 128 + 128]
        speed = jnp.exp(sm[SM_DEC:SM_DEC + 1, t * 128:t * 128 + 128])
        step = kf[:, KF_STEP + t * 128:KF_STEP + t * 128 + 128] + bias
        delta = softplus(step)
        rate = -delta * speed
        running = [dot_exact(mask, v, ((1,), (0,))) for mask, v in zip(masks, per_sequence(rate))]
        turned = [v.T for v in running]
        grun = [jnp.zeros((SEQ, 128), F32), jnp.zeros((SEQ, 128), F32)]
        gdelta = jnp.zeros((ROWS, 128), F32)
        lane2 = jnp.concatenate([lane, lane], axis=0)
        colsum[...] = jnp.zeros_like(colsum)
        for b in range(3):
            gn[:, 0:256] = dot_plain(
                gb[:, GB_MID:GB_MID + D], wout[t, :, 256 + 256 * b:512 + 256 * b])
            for q in range(2):
                c = t * 768 + 256 * b + 128 * q
                h = 4 * b + 2 * q
                gg = gn[:, 128 * q:128 * q + 128]
                gate = kf[:, KF_GATE + c:KF_GATE + c + 128]
                kernel = [sm[SM_CONV + k:SM_CONV + k + 1, c:c + 128] for k in range(4)]
                skip = sm[SM_SKIP:SM_SKIP + 1, c:c + 128]
                pre = conv_of(kf[:, KF_SSM + c:KF_SSM + c + 128], kernel, keeps)
                sp = jax.nn.sigmoid(pre)
                conv = pre * sp
                wide = jnp.where(low2, delta[:, h:h + 1], delta[:, h + 1:h + 2])
                scaled = (conv * wide).astype(BF16)
                s = jax.nn.sigmoid(gate)
                gtotal = gg * (gate * s)
                total = kf[:, KF_Y + c:KF_Y + c + 128] + skip * conv
                k = raw0 + 512 + 256 * b + 128 * q
                gb[:, k:k + 128] = (gg * total * (s * (1.0 + gate * (1.0 - s)))).astype(BF16)
                sg[SM_SKIP:SM_SKIP + 1, c:c + 128] = jnp.sum(gtotal * conv, axis=0, keepdims=True)
                gtotal_b = gtotal.astype(BF16)
                gscaled = []
                for n in range(2):
                    at = slice(SEQ * n, SEQ * n + SEQ)
                    gy = head_rows([gtotal_b[at]], low)
                    gmixed = dot_right(gy, scaled[at])
                    mixed = []
                    for e in range(2):
                        decay = decay_of(running[n], turned[n], h + e, allowed[n])
                        weight = inner[n] * decay
                        mixed.append(weight.astype(BF16))
                        gm = gmixed[128 * e:128 * e + 128]
                        ginner[n] = ginner[n] + gm * decay
                        ggap = gm * weight
                        grun[n] = jnp.where(
                            lane == h + e, jnp.sum(ggap, axis=1, keepdims=True), grun[n])
                        colsum[n, h + e:h + e + 1, :] = jnp.sum(ggap, axis=0, keepdims=True)
                    gscaled.append(dot_left(jnp.concatenate(mixed, axis=0), gy))
                gscaled = jnp.concatenate(gscaled, axis=0)
                prod = gscaled * conv
                even = jnp.sum(jnp.where(low2, prod, 0.0), axis=1, keepdims=True)
                odd = jnp.sum(jnp.where(low2, 0.0, prod), axis=1, keepdims=True)
                gdelta = jnp.where(lane2 == h, even, jnp.where(lane2 == h + 1, odd, gdelta))
                gconv = gscaled * wide + gtotal * skip
                gpre = gconv * (sp * (1.0 + pre * (1.0 - sp)))
                gu, sums = conv_back(kf[:, KF_SSM + c:KF_SSM + c + 128], gpre, kernel, keeps)
                for k in range(4):
                    sg[SM_CONV + k:SM_CONV + k + 1, c:c + 128] = sums[k]
                k = raw0 + 1280 + 256 * b + 128 * q
                gb[:, k:k + 128] = gu.astype(BF16)
        grate = jnp.concatenate([
            dot_exact(masks[n], grun[n] - colsum[n].T, ((0,), (0,))) for n in range(2)], axis=0)
        gstep = (gdelta - grate * speed) * jax.nn.sigmoid(step)
        gb[:, raw0 + 384:raw0 + 512] = gstep.astype(BF16)
        c = t * 128
        sg[SM_BIAS:SM_BIAS + 1, c:c + 128] = jnp.sum(gstep, axis=0, keepdims=True)
        sg[SM_DEC:SM_DEC + 1, c:c + 128] = jnp.sum(grate * rate, axis=0, keepdims=True)

    gacts = []
    for n in range(2):
        gi = ginner[n].astype(BF16)
        gacts.append(jnp.concatenate(
            [dot_left(gi, acts[n][:, 128:256]), dot_plain(gi, acts[n][:, 0:128])], axis=1))
    gact = jnp.concatenate(gacts, axis=0)
    s = jax.nn.sigmoid(state_pre)
    gpre = gact * (s * (1.0 + state_pre * (1.0 - s)))
    gstate, sums = conv_back(state_raw, gpre, cst, keeps)
    for k in range(4):
        sg[SM_CST + k:SM_CST + k + 1, 0:256] = sums[k]
    gb[:, GB_ST:GB_ST + 256] = gstate.astype(BF16)
    save_g = pltpu.make_async_copy(gb, gb_hbm.at[slot], osem.at[0])
    save_g.start()

    loads.wait(2)
    for j in range(0, D, 256):
        gn[:, j:j + 256] = (
            dot_right(gb[:, GB_RAW:GB_RAW + 2 * D], wmix[0, j:j + 256, :])
            + dot_right(gb[:, GB_RAW + 2 * D:GB_RAW + 4 * D], wmix[1, j:j + 256, :])
            + dot_right(gb[:, GB_ST:GB_ST + 256], wst[j:j + 256, :]))
    norm_back(KF_X, SM_G1)
    for j in range(0, D, 256):
        gin_ref[:, j:j + 256] = gmid[:, j:j + 256]
        ginb_ref[:, j:j + 256] = gmid[:, j:j + 256].astype(BF16)
    save_s = pltpu.make_async_copy(sg, sg_hbm.at[slot], osem.at[1])
    save_s.start()
    save_g.wait()
    save_s.wait()


def any_spec():
    return pl.BlockSpec(memory_space=pl.ANY)


def vmem_spec():
    return pl.BlockSpec(memory_space=pltpu.VMEM)


def smem_spec():
    return pl.BlockSpec(memory_space=pltpu.SMEM)


def weight_scratch():
    return [pltpu.VMEM((2, D, 2 * D), BF16), pltpu.VMEM((2, D, D), BF16),
            pltpu.VMEM((2, D, 2 * D), BF16), pltpu.VMEM((2, D, D), BF16)]


def fwd_call(sc, tok, recv, tab, sm, wst, w, kept):
    def body(*refs):
        ins, rest = refs[:7], refs[7 + len(kept):]
        fwd_body(*ins, *rest)

    return pl.pallas_call(
        body,
        out_shape=(jax.ShapeDtypeStruct((ROWS, D), BF16),
                   jax.ShapeDtypeStruct((2, ROWS, KF_COLS), F32),
                   jax.ShapeDtypeStruct((2, ROWS, KB_COLS), BF16)),
        in_specs=[smem_spec()] + [vmem_spec()] * 5 + [any_spec()] * (1 + len(kept)),
        out_specs=(vmem_spec(), any_spec(), any_spec()),
        scratch_shapes=weight_scratch() + [
            pltpu.VMEM((ROWS, KF_COLS), F32), pltpu.VMEM((ROWS, KB_COLS), BF16),
            pltpu.SemaphoreType.DMA((8,)), pltpu.SemaphoreType.DMA((2,))],
        input_output_aliases={7: 1, 8: 2} if kept else {},
        compiler_params=pltpu.CompilerParams(vmem_limit_bytes=VMEM_LIMIT),
        name="layer_forward",
    )(sc, tok, recv, tab, sm, wst, w, *kept)


def bwd_call(sc, cot, recv, tab, sm, wst, w, kf, kb, grads):
    def body(*refs):
        ins, rest = refs[:9], refs[9 + len(grads):]
        bwd_body(*ins, *rest)

    return pl.pallas_call(
        body,
        out_shape=(jax.ShapeDtypeStruct((ROWS, D), F32),
                   jax.ShapeDtypeStruct((ROWS, D), BF16),
                   jax.ShapeDtypeStruct((2, ROWS, GB_COLS), BF16),
                   jax.ShapeDtypeStruct((2, SM_ROWS, SM_COLS), F32)),
        in_specs=[smem_spec()] + [vmem_spec()] * 5 + [any_spec()] * (3 + len(grads)),
        out_specs=(vmem_spec(), vmem_spec(), any_spec(), any_spec()),
        scratch_shapes=weight_scratch() + [
            pltpu.VMEM((ROWS, KF_COLS), F32), pltpu.VMEM((ROWS, KB_COLS), BF16),
            pltpu.VMEM((ROWS, GB_COLS), BF16), pltpu.VMEM((SM_ROWS, SM_COLS), F32),
            pltpu.VMEM((ROWS, D), F32), pltpu.VMEM((ROWS, D), F32), pltpu.VMEM((2, SEQ, 128), F32),
            pltpu.SemaphoreType.DMA((8,)), pltpu.SemaphoreType.DMA((5,)),
            pltpu.SemaphoreType.DMA((2,))],
        input_output_aliases={9: 2, 10: 3} if grads else {},
        compiler_params=pltpu.CompilerParams(vmem_limit_bytes=VMEM_LIMIT),
        name="layer_backward",
    )(sc, cot, recv, tab, sm, wst, w, kf, kb, *grads)


def tables_of(segs):
    index = jnp.arange(SEQ, dtype=jnp.int32)
    same = segs[:, None, :] == segs[:, :, None]
    mask = same & (index[None, None, :] <= index[None, :, None])
    pos = jnp.sum(mask, axis=2).astype(F32) - 1.0
    lane = jnp.arange(128, dtype=jnp.int32)
    frequency = BASE ** (-2.0 * (lane % 32).astype(F32) / HEAD)
    angle = pos[:, :, None] * frequency[None, None, :]
    sign = jnp.where((lane & 32) == 0, -1.0, 1.0)
    return jnp.concatenate(
        [jnp.cos(angle), jnp.sin(angle) * sign, mask.astype(F32)], axis=2).reshape(ROWS, 384)


A_COLS, B_COLS = W_FFN, W_COLS - W_FFN
MESH = pl.DeviceIdType.MESH


def where_am_i():
    core, d = lax.axis_index("tensor"), lax.axis_index("dp")
    return core, d // 8, (d // 2) % 4, d % 2


def place_on_dp(y, z, h):
    return {"dp": y * 8 + z * 2 + h}


class Copies:
    def __init__(self, send_sem, recv_sem):
        self.send_sem, self.recv_sem, self.all = send_sem, recv_sem, []

    def send(self, src, dst, device):
        k = len(self.all)
        copy = pltpu.make_async_remote_copy(
            src_ref=src, dst_ref=dst, send_sem=self.send_sem.at[k], recv_sem=self.recv_sem.at[k],
            device_id=device, device_id_type=MESH)
        copy.start()
        self.all.append(copy)
        return copy

    def drain(self):
        for copy in self.all:
            copy.wait_send()


def greet(core, y, z, h, more=()):
    barrier = pltpu.get_barrier_semaphore()
    others = [place_on_dp((y + 1) % 4, z, h), place_on_dp((y + 3) % 4, z, h),
              place_on_dp(y, (z + 1) % 4, h), place_on_dp(y, (z + 3) % 4, h),
              place_on_dp(y, z, 1 - h), {"tensor": 1 - core}]
    for other in (*others, *more):
        pl.semaphore_signal(barrier, inc=1, device_id=other, device_id_type=MESH)
    pl.semaphore_wait(barrier, len(others) + len(more))
    return others


GATHER_COPIES = 54


def gather_body(p, heads, w, all_heads, send_sem, recv_sem, own_sem):
    core, y, z, h = where_am_i()
    yp, ym, zp, zm, across, sibling = greet(core, y, z, h)
    own = pltpu.make_async_copy(p, w.at[core, y, z, h], own_sem.at[0])
    own.start()
    own_heads = pltpu.make_async_copy(heads, all_heads.at[core], own_sem.at[1])
    own_heads.start()
    net = Copies(send_sem, recv_sem)
    beside = [net.send(heads, all_heads.at[core], sibling)]
    partner = net.send(p, w.at[core, y, z, h], across)
    a, b = pl.ds(0, A_COLS), pl.ds(A_COLS, B_COLS)
    halves = ((a, pl.ds(0, 1664), pl.ds(1664, 1536), yp, ym, zp, zm),
              (b, pl.ds(A_COLS, 1536), pl.ds(A_COLS + 1536, 1536), zp, zm, yp, ym))

    def ring_block(k, step, hh, cols):
        if k == 0:
            return w.at[core, (y + step) % 4, z, hh, :, cols]
        return w.at[core, y, (z + step) % 4, hh, :, cols]

    def plane(k, step, hh, cols):
        if k == 0:
            return w.at[core, :, (z + step) % 4, hh, :, cols]
        return w.at[core, (y + step) % 4, :, hh, :, cols]

    def ring_one(hh, mine):
        copies = []
        for k, (cols, _, _, up, down, _, _) in enumerate(halves):
            block = ring_block(k, 0, hh, cols)
            src = p.at[:, cols] if mine else block
            copies.append((net.send(src, block, up), net.send(src, block, down)))
        return copies

    def ring_one_on(hh, copies):
        onward = []
        for k, (_, one, two, up, down, _, _) in enumerate(halves):
            copies[k][0].wait_recv()
            block = ring_block(k, 3, hh, one)
            going_up = net.send(block, block, up)
            copies[k][1].wait_recv()
            block = ring_block(k, 1, hh, two)
            onward.append((going_up, net.send(block, block, down)))
        return onward

    def ring_two(hh, onward):
        copies = []
        for k, (cols, _, _, _, _, up, down) in enumerate(halves):
            onward[k][0].wait_recv()
            onward[k][1].wait_recv()
            block = plane(k, 0, hh, cols)
            copies.append((net.send(block, block, up), net.send(block, block, down)))
            beside.append(net.send(block, block, sibling))
        return copies

    def ring_two_on(hh, copies):
        onward = []
        for k, (cols, one, two, _, _, up, down) in enumerate(halves):
            copies[k][0].wait_recv()
            block = plane(k, 3, hh, one)
            going_up = net.send(block, block, up)
            copies[k][1].wait_recv()
            block = plane(k, 1, hh, two)
            onward.append((going_up, net.send(block, block, down)))
            for step in (3, 1):
                block = plane(k, step, hh, cols)
                beside.append(net.send(block, block, sibling))
        return onward

    def ring_two_end(hh, onward):
        for k, (_, one, two, _, _, _, _) in enumerate(halves):
            for copy, cols in zip(onward[k], (one, two)):
                copy.wait_recv()
                block = plane(k, 2, hh, cols)
                beside.append(net.send(block, block, sibling))

    mine = ring_one_on(h, ring_one(h, True))
    own.wait()
    own_heads.wait()
    mine = ring_two(h, mine)
    partner.wait_recv()
    theirs = ring_one_on(1 - h, ring_one(1 - h, False))
    mine = ring_two_on(h, mine)
    theirs = ring_two(1 - h, theirs)
    ring_two_end(h, mine)
    theirs = ring_two_on(1 - h, theirs)
    ring_two_end(1 - h, theirs)
    for copy in beside:
        copy.wait_recv()
    net.drain()


def gather_weights(packed, heads):
    w, all_heads = pl.pallas_call(
        gather_body,
        out_shape=(jax.ShapeDtypeStruct((2, 4, 4, 2, 32, W_COLS), BF16),
                   jax.ShapeDtypeStruct((2, 8, 128), F32)),
        in_specs=[any_spec(), any_spec()],
        out_specs=(any_spec(), any_spec()),
        scratch_shapes=[pltpu.SemaphoreType.DMA((GATHER_COPIES,)),
                        pltpu.SemaphoreType.DMA((GATHER_COPIES,)), pltpu.SemaphoreType.DMA((2,))],
        compiler_params=pltpu.CompilerParams(collective_id=0, has_side_effects=True),
        name="gather_weights",
    )(packed, heads)
    return w, all_heads


REDUCE_COPIES = 11 + 2 * 34
ORDER = (2, 1, 3, 0)
GROUPS = (((0, W_OUT), (W_OUT, D)), ((0, 2 * D), (2 * D, D)))


def reduce_body(kb_hbm, gb_hbm, sg_hbm, out_hbm, gin_hbm, ginb_hbm, red, small, coming, stayed,
                kb, gb, sg, by_y, by_z, by_h, by_core, leaving, leaving_too, staying, staying_too,
                n1t, midt, n2t, outt, st, sent_a, sent_b, held_a, held_b, x1_a, x1_b, x2_a, x2_b,
                y1_a, y1_b, y2_a, y2_b, last, send_sem, recv_sem, load_sem):
    core, y, z, h = where_am_i()
    section = lax.axis_index("section")

    def load(k, src, dst):
        copy = pltpu.make_async_copy(src, dst, load_sem.at[k])
        copy.start()
        return copy

    def columns(k, src, dst, start, stop):
        at = pl.ds(start, stop - start)
        return load(k, src.at[0, :, at], dst.at[:, at])

    load_norms = columns(0, kb_hbm, kb, KB_N1, KB_Q)
    load_raw = columns(1, gb_hbm, gb, GB_GU, GB_COLS)
    load_s = load(2, sg_hbm.at[0], sg)
    load_rest = [columns(3, kb_hbm, kb, KB_Q, KB_COLS), columns(4, gb_hbm, gb, GB_OUT, GB_GU)]
    near, far_half = pl.ds(0, 512), pl.ds(512, 512)
    load_moved = [load(5, out_hbm.at[:, near], leaving), load(6, ginb_hbm.at[:, far_half], leaving_too),
                  load(7, gin_hbm.at[:, near], staying), load(8, out_hbm.at[:, far_half], staying_too)]
    yp, ym, zp, zm, across, sibling = greet(
        core, y, z, h, (place_on_dp((y + 2) % 4, z, h), place_on_dp(y, (z + 2) % 4, h),
                        {"section": 1 - section}, {"section": 1 - section, "tensor": 1 - core}))
    net = Copies(send_sem, recv_sem)

    def both(ref, c, n):
        return ref[:, pl.ds(c, n)]

    def turn(ref, c, to):
        for j in range(0, D, 256):
            v = both(ref, c + j, 256).T
            to[j // 256] = v.reshape(4, 64, 256)

    small_groups = (
        (by_y, y, [place_on_dp((y + k) % 4, z, h) for k in (1, 2, 3)]),
        (by_z, z, [place_on_dp(y, (z + k) % 4, h) for k in (1, 2, 3)]),
        (by_h, h, [across]), (by_core, core, [sibling]))

    def small_send(n, total):
        ref, at, others = small_groups[n]
        ref[at] = total
        return [net.send(ref.at[at], ref.at[at], other) for other in others]

    def small_sum(n, copies):
        for copy in copies:
            copy.wait_recv()
        ref = small_groups[n][0]
        total = ref[0] + ref[1]
        for k in range(2, ref.shape[0]):
            total = total + ref[k]
        return total

    load_s.wait()
    small_copies = small_send(0, sg[...])
    load_norms.wait()
    turn(kb, KB_N1, n1t)
    turn(kb, KB_N2, n2t)
    load_raw.wait()
    for j in range(4):
        v = dot_plain(n1t[j].reshape(256, 256), both(gb, GB_ST, 256)).astype(BF16)
        t, y0 = j // 2, 2 * (j % 2)
        v = v.reshape(2, 4, 2, 16, 256)
        st[t, y0] = v[0]
        st[t, y0 + 1] = v[1]

    def move_outputs():
        for copy in load_moved:
            copy.wait()
        first = section == 0
        leaving[...] = jnp.where(first, leaving_too[...], leaving[...])
        staying[...] = jnp.where(first, staying[...], staying_too[...].astype(F32))
        rows = pl.ds(pl.multiple_of(core * 256, 256), 256)
        return load(9, staying, stayed.at[rows]), [
            net.send(staying, stayed.at[rows], sibling),
            net.send(leaving, coming.at[rows], {"section": 1 - section}),
            net.send(leaving, coming.at[rows], {"section": 1 - section, "tensor": 1 - core})]

    def wide(base, t, count, j, size):
        return pl.multiple_of(base + t * count + j * size, 128)

    def tiles(n, step):
        pl.loop(0, n)(step)

    def chunk(g, i, k, t, ref, add):
        def put(v, c, n):
            where = (i, slice(None), pl.ds(c, n))
            ref[where] = (v + ref[where].astype(F32) if add else v).astype(BF16)

        if k == 0:
            at = (z + ORDER[i]) % 4
            left = (n1t, midt)[g][:, at].reshape(256, 256)
        else:
            at = (y + ORDER[i]) % 4
            left = (n2t, outt)[g][at].reshape(256, 256)
        right, base = ((gb, GB_RAW), (kb, KB_AG), (gb, GB_GU), (kb, KB_HID))[2 * k + g]
        start, count = GROUPS[k][g][0], 2 * D if g == 0 else D

        def step(j):
            put(dot_plain(left, both(right, wide(base, t, count, j, 512), 512)),
                pl.multiple_of(start + j * 512, 128), 512)

        tiles(count // 512, step)
        if k == 0 and g == 0:
            v = st[t, :, at].astype(F32)
            v = jnp.concatenate([v[..., 0:128], v[..., 128:256]], axis=2).reshape(256, 128)
            put(v, 2 * D, 128)

    def add_rows(ref, other, rows):
        def step(j):
            at = pl.ds(pl.multiple_of(j * 32, 32), 32)
            ref[at, :] = (ref[at, :].astype(F32) + other[at, :].astype(F32)).astype(BF16)
        pl.loop(0, rows // 32)(step)

    def add_two(ref, one, two, rows):
        def step(j):
            at = pl.ds(pl.multiple_of(j * 32, 32), 32)
            ref[at, :] = (ref[at, :].astype(F32) + one[at, :].astype(F32)
                          + two[at, :].astype(F32)).astype(BF16)
        pl.loop(0, rows // 32)(step)

    halves = ((sent_a, held_a, x1_a, x2_a, zp, zm), (sent_b, held_b, x1_b, x2_b, yp, ym))
    low, high = pl.ds(0, 128), pl.ds(128, 128)
    cols = [[pl.ds(*span) for span in spans] for spans in GROUPS]
    beside, far, near = {}, {}, {}

    def for_sibling(g, i, k):
        sent, held = halves[k][:2]
        chunk(g, i, k, 1 - core, sent, False)
        at = cols[k][g]
        beside[g, i, k] = net.send(sent.at[i, :, at], held.at[i, :, at], sibling)

    steps = [(g, i, k) for g in range(2) for i in range(4) for k in range(2)]
    for_sibling(*steps[0])
    for n, (g, i, k) in enumerate(steps):
        if n == 6:
            for copy in load_rest:
                copy.wait()
            turn(gb, GB_MID, midt)
            turn(gb, GB_OUT, outt)
        if n + 1 < len(steps):
            for_sibling(*steps[n + 1])
        _, held, x1, x2, up, down = halves[k]
        at = cols[k][g]
        beside[g, i, k].wait_recv()
        chunk(g, i, k, core, held, True)
        if i == 0:
            far[g, k] = (net.send(held.at[0, low, at], x1.at[0, :, at], up),
                         net.send(held.at[0, high, at], x1.at[1, :, at], down))
        if i == 1:
            near[g, k] = [net.send(held.at[1, high, at], x2.at[0, high, at], up)]
        if i == 2:
            near[g, k].append(net.send(held.at[2, low, at], x2.at[1, low, at], down))
        if n == 1:
            kept_here, moved = move_outputs()
        if n in (2, 4, 6):
            small_copies = small_send(n // 2, small_sum(n // 2 - 1, small_copies))
        if n == 8:
            small[...] = small_sum(3, small_copies)
    for g in range(2):
        for k in range(2):
            _, held, x1, x2, up, down = halves[k]
            at = cols[k][g]
            far[g, k][0].wait_recv()
            add_rows(held.at[1, low, at], x1.at[0, :, at], 128)
            near[g, k].append(net.send(held.at[1, low, at], x2.at[0, low, at], up))
            far[g, k][1].wait_recv()
            add_rows(held.at[2, high, at], x1.at[1, :, at], 128)
            near[g, k].append(net.send(held.at[2, high, at], x2.at[1, high, at], down))

    rings = ((held_a, y1_a, y2_a, yp, ym, y), (held_b, y1_b, y2_b, zp, zm, z))
    far, close, final = {}, {}, {}

    def rows_of(g, k, step, part):
        held, place = rings[k][0], rings[k][5]
        start = pl.multiple_of(((place + step) % 4) * 64 + part * 32, 32)
        return held.at[3, pl.ds(start, 32), cols[k][g]]

    for g in range(2):
        for k in range(2):
            _, held, x1, x2, _, _ = halves[k]
            _, y1, y2, up, down, _ = rings[k]
            at = cols[k][g]
            for copy in near[g, k]:
                copy.wait_recv()
            add_two(held.at[3, :, at], x2.at[0, :, at], x2.at[1, :, at], 256)
            far[g, k] = (net.send(rows_of(g, k, 2, 0), y1.at[0, :, at], up),
                         net.send(rows_of(g, k, 2, 1), y1.at[1, :, at], down))
            close[g, k] = [net.send(rows_of(g, k, 1, 1), y2.at[0, 1, :, at], up),
                           net.send(rows_of(g, k, 3, 0), y2.at[1, 0, :, at], down)]
    for g in range(2):
        for k in range(2):
            _, y1, y2, up, down, _ = rings[k]
            at = cols[k][g]
            far[g, k][0].wait_recv()
            add_rows(rows_of(g, k, 1, 0), y1.at[0, :, at], 32)
            close[g, k].append(net.send(rows_of(g, k, 1, 0), y2.at[0, 0, :, at], up))
            far[g, k][1].wait_recv()
            add_rows(rows_of(g, k, 3, 1), y1.at[1, :, at], 32)
            close[g, k].append(net.send(rows_of(g, k, 3, 1), y2.at[1, 1, :, at], down))
    for g in range(2):
        for k in range(2):
            y2 = rings[k][2]
            at = cols[k][g]
            for copy in close[g, k]:
                copy.wait_recv()
            for part in range(2):
                add_two(rows_of(g, k, 0, part), y2.at[0, part, :, at], y2.at[1, part, :, at], 32)
            start, size = GROUPS[k][g]
            whole = pl.ds(start + k * A_COLS, size)
            final[g, k] = whole, net.send(rows_of(g, k, 0, 1 - h), last.at[:, whole], across)
    for g in range(2):
        for k in range(2):
            whole, copy = final[g, k]
            copy.wait_recv()
            red[:, whole] = rows_of(g, k, 0, h)[...].astype(F32) + last[:, whole].astype(F32)
    kept_here.wait()
    for copy in moved:
        copy.wait_recv()
    net.drain()


def reduce_grads(kb, gb, sg, out, gin, gin_b):
    def pair(cols, rows, count=2):
        return pltpu.VMEM((count, rows, cols), BF16)

    return pl.pallas_call(
        reduce_body,
        out_shape=(jax.ShapeDtypeStruct((32, W_COLS), F32),
                   jax.ShapeDtypeStruct((SM_ROWS, SM_COLS), F32),
                   jax.ShapeDtypeStruct((512, 512), BF16),
                   jax.ShapeDtypeStruct((512, 512), F32)),
        in_specs=[any_spec()] * 6,
        out_specs=(vmem_spec(), vmem_spec(), any_spec(), any_spec()),
        scratch_shapes=[
            pltpu.VMEM((ROWS, KB_COLS), BF16), pltpu.VMEM((ROWS, GB_COLS), BF16),
            pltpu.VMEM((SM_ROWS, SM_COLS), F32),
            *[pltpu.VMEM((n, SM_ROWS, SM_COLS), F32) for n in (4, 4, 2, 2)],
            *[pltpu.VMEM((256, 512), kind) for kind in (BF16, BF16, F32, BF16)],
            *[pltpu.VMEM((4, 4, 64, 256), BF16)] * 4, pltpu.VMEM((2, 4, 4, 2, 16, 256), BF16),
            pair(A_COLS, 256, 4), pair(B_COLS, 256, 4), pair(A_COLS, 256, 4), pair(B_COLS, 256, 4),
            pair(A_COLS, 128), pair(B_COLS, 128), pair(A_COLS, 256), pair(B_COLS, 256),
            pair(A_COLS, 32), pair(B_COLS, 32),
            pltpu.VMEM((2, 2, 32, A_COLS), BF16), pltpu.VMEM((2, 2, 32, B_COLS), BF16),
            pltpu.VMEM((32, W_COLS), BF16),
            pltpu.SemaphoreType.DMA((REDUCE_COPIES,)), pltpu.SemaphoreType.DMA((REDUCE_COPIES,)),
            pltpu.SemaphoreType.DMA((10,))],
        compiler_params=pltpu.CompilerParams(
            collective_id=1, has_side_effects=True, vmem_limit_bytes=VMEM_LIMIT),
        name="reduce_grads",
    )(kb, gb, sg, out, gin, gin_b)


def spread(values, each, whole):
    turn = lax.broadcasted_iota(jnp.int32, (128, whole), 0)
    lane = lax.broadcasted_iota(jnp.int32, (128, whole), 1)
    line = lax.broadcasted_iota(jnp.int32, (64, whole), 0)
    where = lax.broadcasted_iota(jnp.int32, (64, whole), 1)
    pick = jnp.where((lane % each == turn) & (turn < each), 1.0, 0.0).astype(BF16)
    return jnp.sum(
        jnp.where(where // each == line, dot_plain(values, pick), 0.0), axis=0, keepdims=True)


def prepare_body(w, heads, sm, wst, tile, sem):
    copies = [pltpu.make_async_copy(
        w.at[:, :, :, :, pl.ds(0, 16), pl.ds(384, 128)], tile, sem.at[0])]
    for t in range(2):
        for half in range(2):
            copies.append(pltpu.make_async_copy(
                w.at[t, :, :, :, pl.ds(16 * half, 16), pl.ds(2 * D, 128)],
                wst.at[t, :, :, :, :, pl.ds(128 * half, 128)], sem.at[1 + 2 * t + half]))
    for copy in copies:
        copy.start()
    sm[...] = jnp.zeros_like(sm)
    for t in range(2):
        sm[SM_BIAS:SM_BIAS + 1, 128 * t:128 * t + 128] = heads[t, 0:1, :]
        sm[SM_DEC:SM_DEC + 1, 128 * t:128 * t + 128] = heads[t, 1:2, :]
        for p in range(6):
            c = 768 * t + 128 * p
            lane = lax.broadcasted_iota(jnp.int32, (1, 128), 1)
            sm[SM_SKIP:SM_SKIP + 1, c:c + 128] = jnp.where(
                lane < HEAD, heads[t, 2:3, 2 * p:2 * p + 1], heads[t, 2:3, 2 * p + 1:2 * p + 2])
    copies[0].wait()
    lines = tile[...].reshape(64, 16, 128).astype(F32)

    def line(row, first):
        return pltpu.roll(lines[:, row, :], 128 - first, 1).astype(BF16)

    sm[SM_G1:SM_G1 + 1, 0:D] = spread(line(0, 12), 16, D)
    sm[SM_G2:SM_G2 + 1, 0:D] = spread(line(0, 28), 16, D)
    for k in range(4):
        sm[SM_CONV + k:SM_CONV + k + 1, :] = spread(line(1, 12 + 24 * k), 24, SM_COLS)
        sm[SM_CST + k:SM_CST + k + 1, 0:256] = spread(line(0, 44 + 4 * k), 4, 256)
    for copy in copies[1:]:
        copy.wait()


def prepare(w, all_heads):
    sm, wst = pl.pallas_call(
        prepare_body,
        out_shape=(jax.ShapeDtypeStruct((SM_ROWS, SM_COLS), F32),
                   jax.ShapeDtypeStruct((2, 4, 4, 2, 16, 256), BF16)),
        in_specs=[any_spec(), vmem_spec()],
        out_specs=(vmem_spec(), vmem_spec()),
        scratch_shapes=[pltpu.VMEM((2, 4, 4, 2, 16, 128), BF16), pltpu.SemaphoreType.DMA((5,))],
        compiler_params=pltpu.CompilerParams(vmem_limit_bytes=VMEM_LIMIT),
        name="prepare_small",
    )(w, all_heads)
    return sm, wst.reshape(D, 256)


def finish_body(at, red, small, coming, stayed, final, igrad, g1, g2, query, key, value, attn,
                gate, ssm, step, conv, state, cst, bias, dec, skip, ssm_out, ffn_gate, ffn_up,
                ffn_down):
    first, core, place = at[0], at[1], at[2]
    final[...] = jnp.where(first == 1, coming[...], stayed[...].astype(BF16))
    igrad[...] = jnp.where(first == 1, stayed[...], coming[...].astype(F32))
    query[0] = red[:, 0:256]
    kv = red[:, 256:384]
    key[0] = kv[:, 0:64]
    value[0] = pltpu.roll(kv, 64, 1)[:, 0:64]
    step[0] = red[:, 384:512][:, 0:12]
    gate[0] = red[:, 512:1280]
    ssm[0] = red[:, 1280:2048]
    state[0, :, 0:128] = red[0:16, 2 * D:W_OUT]
    state[0, :, 128:256] = red[16:32, 2 * D:W_OUT]
    attn[0] = red[:, W_OUT:W_OUT + 256]
    ssm_out[0] = red[:, W_OUT + 256:W_FFN]
    ffn_gate[0] = red[:, W_FFN:W_FFN + D]
    ffn_up[0] = red[:, W_FFN + D:W_DN]
    ffn_down[0] = red[:, W_DN:W_COLS]

    def mine(rows, cols, size):
        v = small[rows, pl.ds(pl.multiple_of(place * size // 128 * 128, 128), cols)]
        return pltpu.roll(v, (cols - place * size % 128) % cols, 1)

    for k, (ref, size) in enumerate(((g1, 16), (g2, 16))):
        ref[...] = mine(pl.ds(0, 8), 128, size)[k:k + 1, 0:size]
    pair = jnp.concatenate([small[0:8, :], jnp.zeros((8, 128), F32)], axis=1)
    turned = pltpu.roll(pair, (SM_COLS + 128 - place * 24) % (SM_COLS + 128), 1)
    conv[0] = turned[SM_CONV:SM_CONV + 4, 0:24]
    tail = small[:, 0:256]
    turned = pltpu.roll(tail, (256 - place * 4) % 256, 1)
    cst[0] = turned[SM_CST:SM_CST + 4, 0:4]
    for row, ref in ((SM_BIAS, bias), (SM_DEC, dec)):
        v = small[8:16, pl.ds(pl.multiple_of(core * 128, 128), 128)]
        ref[...] = v[row - 8:row - 7, 0:12]
    lane = lax.broadcasted_iota(jnp.int32, (8, 128), 1)
    sums = jnp.zeros((8, 128), F32)
    for p in range(6):
        v = small[8:16, pl.ds(pl.multiple_of(core * 768 + 128 * p, 128), 128)]
        even = jnp.sum(jnp.where(lane < HEAD, v, 0.0), axis=1, keepdims=True)
        odd = jnp.sum(jnp.where(lane < HEAD, 0.0, v), axis=1, keepdims=True)
        sums = jnp.where(lane == 2 * p, even, jnp.where(lane == 2 * p + 1, odd, sums))
    skip[...] = sums[SM_SKIP - 8:SM_SKIP - 7, 0:12]


def finish(at, red, small, coming, stayed):
    shapes = [((512, 512), BF16)] + [(shape, F32) for shape in (
        (512, 512), (1, 16), (1, 16), (1, 32, 256), (1, 32, 64), (1, 32, 64), (1, 32, 256),
        (1, 32, 768), (1, 32, 768), (1, 32, 12), (1, 4, 24), (1, 16, 256), (1, 4, 4), (1, 12),
        (1, 12), (1, 12), (1, 32, 768), (1, 32, 1024), (1, 32, 1024), (1, 32, 1024))]
    outs = pl.pallas_call(
        finish_body,
        out_shape=tuple(jax.ShapeDtypeStruct(*shape) for shape in shapes),
        in_specs=[smem_spec()] + [vmem_spec()] * 4,
        out_specs=tuple(vmem_spec() for _ in shapes),
        compiler_params=pltpu.CompilerParams(vmem_limit_bytes=VMEM_LIMIT),
        name="finish_outputs",
    )(at, red, small, coming, stayed)
    turned = (7, 17, 20)
    return tuple(v.swapaxes(1, 2) if k in turned else v for k, v in enumerate(outs))


def local(tokens, segments, cotangent, gain_one, gain_two, w_query, key_weight, value_weight,
          w_attn_out, w_gate_ssm, w_ssm_in, w_step, conv_ssm, w_state, conv_state, step_bias,
          decay_log, skip_gain, w_ssm_out, w_ffn_gate, w_ffn_up, w_ffn_down):
    core = lax.axis_index("tensor")
    place = core * lax.axis_size("dp") + lax.axis_index("dp")
    first = lax.axis_index("section") == 0
    first_i = first.astype(jnp.int32)

    state = w_state[0]
    spare = 116
    one = jnp.concatenate([gain_one[0], gain_two[0], conv_state[0].ravel()])
    two = conv_ssm[0].ravel()
    smalls = jnp.concatenate([
        jnp.pad(v, (0, spare - v.shape[0]))[None] for v in (one, two)], axis=0)
    smalls = jnp.pad(smalls, ((0, 30), (0, 0)))
    heads = jnp.pad(jnp.concatenate([step_bias, decay_log, skip_gain]), ((0, 5), (0, 116)))
    packed = jnp.concatenate([
        w_query[0], key_weight[0], value_weight[0], w_step[0], smalls,
        w_gate_ssm[0], w_ssm_in[0], jnp.concatenate([state[:, 0:128], state[:, 128:256]], axis=0),
        w_attn_out[0].T, w_ssm_out[0].T, w_ffn_gate[0], w_ffn_up[0], w_ffn_down[0].T], axis=1)
    gathered, all_heads = gather_weights(packed, heads)
    sm, wst = prepare(gathered, all_heads)
    weights = gathered.reshape(2, D, W_COLS)

    tok = lax.dynamic_slice_in_dim(tokens, core * ROWS, ROWS)
    cot = lax.dynamic_slice_in_dim(cotangent, core * ROWS, ROWS)
    tab = tables_of(lax.dynamic_slice_in_dim(segments, core * ROWS, ROWS).reshape(2, SEQ))

    real_first = jnp.stack([jnp.where(first, 0, 1), first_i])
    real_second = jnp.stack([jnp.where(first, 1, 0), first_i])
    nothing = jnp.zeros((ROWS, D), BF16)
    out, *kept = fwd_call(real_first, tok, nothing, tab, sm, wst, weights, ())
    received = lax.ppermute(out, "section", [(0, 1)])
    out, *kept = fwd_call(real_second, tok, received, tab, sm, wst, weights, kept)
    _, gin_b, *grads = bwd_call(real_second, cot, nothing, tab, sm, wst, weights, *kept, ())
    received = lax.ppermute(gin_b, "section", [(1, 0)])
    gin, gin_b, *grads = bwd_call(real_first, cot, received, tab, sm, wst, weights, *kept, grads)

    red, small, coming, stayed = reduce_grads(kept[1], grads[0], grads[1], out, gin, gin_b)
    at = jnp.stack([first_i, core, place])
    return finish(at, red, small, coming, stayed)


def solution(mesh):
    rows = P("dp", None)
    flat = P("section", ("tensor", "dp"))
    split_in = P("section", "dp", "tensor")
    split_out = P("section", "tensor", "dp")
    kernel = P("section", None, ("tensor", "dp"))
    head = P("section", "tensor")
    state = P("section", ("tensor", "dp"), None)
    params = (flat, flat, split_in, split_in, split_in, split_out, split_in, split_in, split_in,
              kernel, state, kernel, head, head, head, split_out, split_in, split_in, split_out)
    halves = P("dp", "section")
    return jax.shard_map(
        local, mesh=mesh, in_specs=(rows, P("dp"), rows, *params),
        out_specs=(halves, halves, *params), check_vma=False)
```

```python
from functools import partial

import jax
import jax.numpy as jnp
from jax import lax
from jax.experimental import pallas as pl
from jax.experimental.pallas import tpu as pltpu
from jax.sharding import PartitionSpec as P

F32 = jnp.float32
BF16 = jnp.bfloat16
EPS = 1e-05
BASE = 10000.0
SCALE = 0.125
NEG = -1e30
SEQ = 128
ROWS = 256
D = 1024
HEAD = 64

W_OUT, W_FFN, W_DN, W_COLS = 2176, 3200, 5248, 6272
KF_X, KF_MID, KF_GATE, KF_SSM, KF_Y, KF_STEP, KF_STATE, KF_GU, KF_COLS = (
    0, 1024, 2048, 3584, 5120, 6656, 6912, 7168, 11264)
KB_N1, KB_N2, KB_Q, KB_KV, KB_AG, KB_HID, KB_COLS = 0, 1024, 2048, 2560, 2816, 4864, 6912
GB_OUT, GB_MID, GB_GU, GB_RAW, GB_ST, GB_COLS = 0, 1024, 2048, 6144, 10240, 10496
SM_G1, SM_G2, SM_CONV, SM_CST, SM_BIAS, SM_DEC, SM_SKIP = 0, 1, 2, 6, 10, 11, 12
SM_ROWS, SM_COLS = 16, 1536
VMEM_LIMIT = 60 * 1024 * 1024
AHEAD = 6


def dot_plain(left, right):
    return jnp.dot(left, right, preferred_element_type=F32)


def dot_left(left, right):
    return lax.dot_general(left, right, (((0,), (0,)), ((), ())), preferred_element_type=F32)


def dot_right(left, right):
    return lax.dot_general(left, right, (((1,), (1,)), ((), ())), preferred_element_type=F32)


def dot_exact(left, right, dims):
    return lax.dot_general(
        left, right, (dims, ((), ())), preferred_element_type=F32, precision=lax.Precision.HIGHEST
    )


def lanes():
    lane = lax.broadcasted_iota(jnp.int32, (SEQ, 128), 1)
    wide = lax.broadcasted_iota(jnp.int32, (ROWS, 128), 1)
    return lane, lane < HEAD, wide < HEAD, (wide & 32) == 0


def swap_halves(v, first_half):
    return jnp.where(first_half, pltpu.roll(v, 96, 1), pltpu.roll(v, 32, 1))


def both_halves(v, low):
    turned = pltpu.roll(v.astype(F32), HEAD, 1).astype(BF16)
    return jnp.where(low, v, turned), jnp.where(low, turned, v)


def head_rows(pairs, low):
    zero = jnp.zeros_like(pairs[0])
    rows = []
    for pair in pairs:
        rows += [jnp.where(low, pair, zero), jnp.where(low, zero, pair)]
    return jnp.concatenate(rows, axis=0)


def conv_of(u, kernel, keeps):
    total = u * kernel[3]
    for o in (1, 2, 3):
        total = total + pltpu.roll(u, o, 0) * keeps[o] * kernel[3 - o]
    return total


def conv_back(u, g, kernel, keeps):
    back = g * kernel[3]
    sums = [None, None, None, jnp.sum(u * g, axis=0, keepdims=True)]
    for o in (1, 2, 3):
        kept = g * keeps[o]
        back = back + pltpu.roll(kept, ROWS - o, 0) * kernel[3 - o]
        sums[3 - o] = jnp.sum(pltpu.roll(u, o, 0) * kept, axis=0, keepdims=True)
    return back, sums


def softplus(v):
    return jnp.maximum(v, 0.0) + jnp.log1p(jnp.exp(-jnp.abs(v)))


def keeps_of(masks):
    pos = jnp.concatenate([jnp.sum(mask, axis=1, keepdims=True) for mask in masks]) - 1.0
    return [None] + [jnp.where(pos >= o, 1.0, 0.0) for o in (1, 2, 3)]


def softmax_rows(scores, mask4):
    scores = jnp.where(mask4, scores, NEG)
    e = jnp.exp(scores - jnp.max(scores, axis=1, keepdims=True))
    return e / jnp.sum(e, axis=1, keepdims=True)


class Loads:
    def __init__(self, copies, ahead):
        self.copies, self.next, self.ahead = copies, 0, ahead
        self.start(ahead)

    def start(self, count):
        for copy in self.copies[self.next:self.next + count]:
            copy.start()
        self.next += count

    def wait(self, count=1):
        for _ in range(count):
            self.copies[self.next - self.ahead].wait()
            self.start(1)


def weight_loads(w_hbm, column, ref, sem):
    return [pltpu.make_async_copy(
        w_hbm.at[t, :, pl.ds(column, ref.shape[2])], ref.at[t], sem.at[t]) for t in range(2)]


def decay_of(running, turned, head, allowed):
    gap = running[:, head:head + 1] - turned[head:head + 1, :]
    return jnp.exp(jnp.where(allowed, gap, NEG))


def geometry(tab):
    cos, sin = tab[:, 0:128], tab[:, 128:256]
    masks = [tab[SEQ * s:SEQ * s + SEQ, 256:384] for s in range(2)]
    return cos, sin, masks, [mask > 0.5 for mask in masks], keeps_of(masks)


def per_sequence(v):
    return v[0:SEQ], v[SEQ:ROWS]


def fwd_body(sc, tok, recv, tab, sm, wst, w_hbm, out_ref, kf_hbm, kb_hbm,
             wmix, wout, wffn, wdn, kf, kb, wsem, osem):
    loads = Loads(
        weight_loads(w_hbm, 0, wmix, wsem) + weight_loads(w_hbm, W_OUT, wout, wsem.at[pl.ds(2, 2)])
        + weight_loads(w_hbm, W_FFN, wffn, wsem.at[pl.ds(4, 2)])
        + weight_loads(w_hbm, W_DN, wdn, wsem.at[pl.ds(6, 2)]), AHEAD)
    slot, first = sc[0], sc[1]
    _, low, low2, first_half = lanes()
    cos, sin, masks, allowed, keeps = geometry(tab)
    square = jnp.zeros((ROWS, 1), F32)
    for j in range(0, D, 256):
        x = jnp.where(first == 1, tok[:, j:j + 256], recv[:, j:j + 256]).astype(F32)
        kf[:, KF_X + j:KF_X + j + 256] = x
        square = square + jnp.sum(x * x, axis=1, keepdims=True)
    r = lax.rsqrt(square * (1.0 / D) + EPS)
    for j in range(0, D, 256):
        kb[:, KB_N1 + j:KB_N1 + j + 256] = (
            kf[:, KF_X + j:KF_X + j + 256] * r * sm[SM_G1:SM_G1 + 1, j:j + 256]).astype(BF16)
    n1 = kb[:, KB_N1:KB_N1 + D]

    state_raw = dot_plain(n1, wst[...])
    kf[:, KF_STATE:KF_STATE + 256] = state_raw
    pre = conv_of(state_raw, [sm[SM_CST + k:SM_CST + k + 1, 0:256] for k in range(4)], keeps)
    act = (pre * jax.nn.sigmoid(pre)).astype(BF16)
    inner = [dot_right(v[:, 128:256], v[:, 0:128]) for v in per_sequence(act)]

    for t in range(2):
        loads.wait()
        qs = []
        raw = dot_plain(kb[:, KB_N1:KB_N1 + D], wmix[t, :, 0:256])
        for p in range(2):
            v = raw[:, 128 * p:128 * p + 128]
            qs.append((v * cos + swap_halves(v, first_half) * sin).astype(BF16))
            c = KB_Q + t * 256 + 128 * p
            kb[:, c:c + 128] = qs[p]
        raw = dot_plain(kb[:, KB_N1:KB_N1 + D], wmix[t, :, 256:512])
        v = raw[:, 0:128]
        kv = jnp.where(low2, v * cos + swap_halves(v, first_half) * sin, v).astype(BF16)
        kb[:, KB_KV + t * 128:KB_KV + t * 128 + 128] = kv
        step_raw = raw[:, 128:256]
        kf[:, KF_STEP + t * 128:KF_STEP + t * 128 + 128] = step_raw
        kk, vv = both_halves(kv, low2)
        for s in range(2):
            at = slice(SEQ * s, SEQ * s + SEQ)
            mask4 = jnp.concatenate([masks[s]] * 4, axis=0) > 0.5
            scores = dot_right(head_rows([q[at] for q in qs], low), kk[at]) * SCALE
            heads = dot_plain(softmax_rows(scores, mask4).astype(BF16), vv[at])
            for p in range(2):
                c = KB_AG + t * D + 128 * p
                kb[at, c:c + 128] = jnp.where(
                    low, heads[256 * p:256 * p + 128], heads[256 * p + 128:256 * p + 256]
                ).astype(BF16)

        delta = softplus(step_raw + sm[SM_BIAS:SM_BIAS + 1, t * 128:t * 128 + 128])
        rate = -delta * jnp.exp(sm[SM_DEC:SM_DEC + 1, t * 128:t * 128 + 128])
        running = [dot_exact(mask, v, ((1,), (0,))) for mask, v in zip(masks, per_sequence(rate))]
        turned = [v.T for v in running]
        for b in range(3):
            c0 = t * 768 + 256 * b
            gate2 = dot_plain(kb[:, KB_N1:KB_N1 + D], wmix[t, :, 512 + 256 * b:768 + 256 * b])
            kf[:, KF_GATE + c0:KF_GATE + c0 + 256] = gate2
            ssm2 = dot_plain(kb[:, KB_N1:KB_N1 + D], wmix[t, :, 1280 + 256 * b:1536 + 256 * b])
            kf[:, KF_SSM + c0:KF_SSM + c0 + 256] = ssm2
            for q in range(2):
                c = c0 + 128 * q
                h = 4 * b + 2 * q
                u = ssm2[:, 128 * q:128 * q + 128]
                pre = conv_of(
                    u, [sm[SM_CONV + k:SM_CONV + k + 1, c:c + 128] for k in range(4)], keeps)
                conv = pre * jax.nn.sigmoid(pre)
                scaled = (conv * jnp.where(low2, delta[:, h:h + 1], delta[:, h + 1:h + 2])
                          ).astype(BF16)
                for s in range(2):
                    at = slice(SEQ * s, SEQ * s + SEQ)
                    mixed = jnp.concatenate(
                        [(inner[s] * decay_of(running[s], turned[s], h + e, allowed[s])
                          ).astype(BF16) for e in range(2)], axis=1)
                    ssm_y = dot_plain(mixed, head_rows([scaled[at]], low))
                    kf[at, KF_Y + c:KF_Y + c + 128] = ssm_y
                    total = ssm_y + sm[SM_SKIP:SM_SKIP + 1, c:c + 128] * conv[at]
                    gate = kf[at, KF_GATE + c:KF_GATE + c + 128]
                    g = KB_AG + t * D + 256 + 256 * b + 128 * q
                    kb[at, g:g + 128] = (total * (gate * jax.nn.sigmoid(gate))).astype(BF16)

    loads.wait(2)
    square = jnp.zeros((ROWS, 1), F32)
    for j in range(0, D, 256):
        part = dot_right(kb[:, KB_AG:KB_AG + D], wout[0, j:j + 256, :]) + dot_right(
            kb[:, KB_AG + D:KB_AG + 2 * D], wout[1, j:j + 256, :])
        mid = kf[:, KF_X + j:KF_X + j + 256] + part
        kf[:, KF_MID + j:KF_MID + j + 256] = mid
        square = square + jnp.sum(mid * mid, axis=1, keepdims=True)
    r = lax.rsqrt(square * (1.0 / D) + EPS)
    for j in range(0, D, 256):
        kb[:, KB_N2 + j:KB_N2 + j + 256] = (
            kf[:, KF_MID + j:KF_MID + j + 256] * r * sm[SM_G2:SM_G2 + 1, j:j + 256]).astype(BF16)
    for t in range(2):
        loads.wait()
        for j in range(0, D, 256):
            gate = dot_plain(kb[:, KB_N2:KB_N2 + D], wffn[t, :, j:j + 256])
            up = dot_plain(kb[:, KB_N2:KB_N2 + D], wffn[t, :, D + j:D + j + 256])
            c = KF_GU + t * 2 * D + j
            kf[:, c:c + 256] = gate
            kf[:, c + D:c + D + 256] = up
            c = KB_HID + t * D + j
            kb[:, c:c + 256] = (gate * jax.nn.sigmoid(gate) * up).astype(BF16)
    save_f = pltpu.make_async_copy(kf, kf_hbm.at[slot], osem.at[0])
    save_b = pltpu.make_async_copy(kb, kb_hbm.at[slot], osem.at[1])
    save_f.start()
    save_b.start()
    loads.wait(2)
    for j in range(0, D, 256):
        part = dot_right(kb[:, KB_HID:KB_HID + D], wdn[0, j:j + 256, :]) + dot_right(
            kb[:, KB_HID + D:KB_HID + 2 * D], wdn[1, j:j + 256, :])
        out_ref[:, j:j + 256] = (kf[:, KF_MID + j:KF_MID + j + 256] + part).astype(BF16)
    save_f.wait()
    save_b.wait()


def bwd_body(sc, cot, recv, tab, sm, wst, w_hbm, kf_hbm, kb_hbm, gin_ref, ginb_ref, gb_hbm, sg_hbm,
             wmix, wout, wffn, wdn, kf, kb, gb, sg, gn, gmid, colsum, wsem, isem, osem):
    slot, first = sc[0], sc[1]
    kept = [pltpu.make_async_copy(
        kf_hbm.at[slot, :, pl.ds(a, b - a)], kf.at[:, pl.ds(a, b - a)], isem.at[n])
        for n, (a, b) in enumerate(((KF_GU, KF_GU + 2 * D), (KF_GU + 2 * D, KF_COLS),
                                    (KF_X, KF_GATE), (KF_GATE, KF_GU)))]
    kept.append(pltpu.make_async_copy(kb_hbm.at[slot], kb, isem.at[4]))
    down = weight_loads(w_hbm, W_DN, wdn, wsem)
    ffn = weight_loads(w_hbm, W_FFN, wffn, wsem.at[pl.ds(2, 2)])
    outer = weight_loads(w_hbm, W_OUT, wout, wsem.at[pl.ds(4, 2)])
    mix = weight_loads(w_hbm, 0, wmix, wsem.at[pl.ds(6, 2)])
    loads = Loads([down[0], kept[0], down[1], kept[1], ffn[0], ffn[1], kept[2], outer[0], kept[4],
                   kept[3], outer[1], mix[0], mix[1]], AHEAD)

    lane, low, low2, first_half = lanes()
    cos, sin, masks, allowed, keeps = geometry(tab)
    sg[...] = jnp.zeros_like(sg)

    for j in range(0, D, 256):
        gout = jnp.where(first == 1, recv[:, j:j + 256], cot[:, j:j + 256])
        gmid[:, j:j + 256] = gout.astype(F32)
        gb[:, GB_OUT + j:GB_OUT + j + 256] = gout
    for t in range(2):
        loads.wait(2)
        for j in range(0, D, 256):
            gh = dot_plain(gb[:, GB_OUT:GB_OUT + D], wdn[t, :, j:j + 256])
            c = KF_GU + t * 2 * D + j
            gate, up = kf[:, c:c + 256], kf[:, c + D:c + D + 256]
            s = jax.nn.sigmoid(gate)
            c = GB_GU + t * 2 * D + j
            gb[:, c:c + 256] = (gh * up * (s * (1.0 + gate * (1.0 - s)))).astype(BF16)
            gb[:, c + D:c + D + 256] = (gh * (gate * s)).astype(BF16)
    loads.wait(2)

    def norm_back(v0, gain_row):
        square = jnp.zeros((ROWS, 1), F32)
        cross = jnp.zeros((ROWS, 1), F32)
        for j in range(0, D, 256):
            v = kf[:, v0 + j:v0 + j + 256]
            square = square + jnp.sum(v * v, axis=1, keepdims=True)
            cross = cross + jnp.sum(
                v * gn[:, j:j + 256] * sm[gain_row:gain_row + 1, j:j + 256], axis=1, keepdims=True)
        r = lax.rsqrt(square * (1.0 / D) + EPS)
        factor = cross * (1.0 / D) * r * r * r
        for j in range(0, D, 256):
            v = kf[:, v0 + j:v0 + j + 256]
            g = gn[:, j:j + 256]
            sg[gain_row:gain_row + 1, j:j + 256] = jnp.sum(g * (v * r), axis=0, keepdims=True)
            gmid[:, j:j + 256] = gmid[:, j:j + 256] + (
                g * sm[gain_row:gain_row + 1, j:j + 256] * r - v * factor)

    for j in range(0, D, 256):
        gn[:, j:j + 256] = dot_right(gb[:, GB_GU:GB_GU + 2 * D], wffn[0, j:j + 256, :]) + dot_right(
            gb[:, GB_GU + 2 * D:GB_GU + 4 * D], wffn[1, j:j + 256, :])
    loads.wait()
    norm_back(KF_MID, SM_G2)
    for j in range(0, D, 256):
        gb[:, GB_MID + j:GB_MID + j + 256] = gmid[:, j:j + 256].astype(BF16)

    loads.wait(3)
    state_raw = kf[:, KF_STATE:KF_STATE + 256]
    cst = [sm[SM_CST + k:SM_CST + k + 1, 0:256] for k in range(4)]
    state_pre = conv_of(state_raw, cst, keeps)
    act = (state_pre * jax.nn.sigmoid(state_pre)).astype(BF16)
    acts = per_sequence(act)
    inner = [dot_right(v[:, 128:256], v[:, 0:128]) for v in acts]
    ginner = [jnp.zeros((SEQ, 128), F32), jnp.zeros((SEQ, 128), F32)]

    for t in range(2):
        if t == 1:
            loads.wait()
        raw0 = GB_RAW + t * 2 * D
        gatt = dot_plain(gb[:, GB_MID:GB_MID + D], wout[t, :, 0:256]).astype(BF16)
        kk, vv = both_halves(kb[:, KB_KV + t * 128:KB_KV + t * 128 + 128], low2)
        for s in range(2):
            at = slice(SEQ * s, SEQ * s + SEQ)
            mask4 = jnp.concatenate([masks[s]] * 4, axis=0) > 0.5
            gheads = head_rows([gatt[at, 0:128], gatt[at, 128:256]], low)
            c = KB_Q + t * 256
            qheads = head_rows([kb[at, c:c + 128], kb[at, c + 128:c + 256]], low)
            probs = softmax_rows(dot_right(qheads, kk[at]) * SCALE, mask4)
            gprobs = dot_right(gheads, vv[at])
            gscores = (probs * (gprobs - jnp.sum(probs * gprobs, axis=1, keepdims=True))
                       ).astype(BF16)
            gq = dot_plain(gscores, kk[at]) * SCALE
            turn, half = (cos[at], sin[at]), first_half[at]
            for p in range(2):
                v = jnp.where(low, gq[256 * p:256 * p + 128], gq[256 * p + 128:256 * p + 256])
                gb[at, raw0 + 128 * p:raw0 + 128 * p + 128] = (
                    v * turn[0] - swap_halves(v, half) * turn[1]).astype(BF16)
            gk = dot_left(gscores, qheads) * SCALE
            gk = gk + pltpu.roll(gk, HEAD, 1)
            gv = dot_left(probs.astype(BF16), gheads)
            gv = gv + pltpu.roll(gv, HEAD, 1)
            gb[at, raw0 + 256:raw0 + 384] = jnp.where(
                low, gk * turn[0] - swap_halves(gk, half) * turn[1], gv).astype(BF16)

        bias = sm[SM_BIAS:SM_BIAS + 1, t * 128:t * 128 + 128]
        speed = jnp.exp(sm[SM_DEC:SM_DEC + 1, t * 128:t * 128 + 128])
        step = kf[:, KF_STEP + t * 128:KF_STEP + t * 128 + 128] + bias
        delta = softplus(step)
        rate = -delta * speed
        running = [dot_exact(mask, v, ((1,), (0,))) for mask, v in zip(masks, per_sequence(rate))]
        turned = [v.T for v in running]
        grun = [jnp.zeros((SEQ, 128), F32), jnp.zeros((SEQ, 128), F32)]
        gdelta = jnp.zeros((ROWS, 128), F32)
        lane2 = jnp.concatenate([lane, lane], axis=0)
        colsum[...] = jnp.zeros_like(colsum)
        for b in range(3):
            gn[:, 0:256] = dot_plain(
                gb[:, GB_MID:GB_MID + D], wout[t, :, 256 + 256 * b:512 + 256 * b])
            for q in range(2):
                c = t * 768 + 256 * b + 128 * q
                h = 4 * b + 2 * q
                gg = gn[:, 128 * q:128 * q + 128]
                gate = kf[:, KF_GATE + c:KF_GATE + c + 128]
                kernel = [sm[SM_CONV + k:SM_CONV + k + 1, c:c + 128] for k in range(4)]
                skip = sm[SM_SKIP:SM_SKIP + 1, c:c + 128]
                pre = conv_of(kf[:, KF_SSM + c:KF_SSM + c + 128], kernel, keeps)
                sp = jax.nn.sigmoid(pre)
                conv = pre * sp
                wide = jnp.where(low2, delta[:, h:h + 1], delta[:, h + 1:h + 2])
                scaled = (conv * wide).astype(BF16)
                s = jax.nn.sigmoid(gate)
                gtotal = gg * (gate * s)
                total = kf[:, KF_Y + c:KF_Y + c + 128] + skip * conv
                k = raw0 + 512 + 256 * b + 128 * q
                gb[:, k:k + 128] = (gg * total * (s * (1.0 + gate * (1.0 - s)))).astype(BF16)
                sg[SM_SKIP:SM_SKIP + 1, c:c + 128] = jnp.sum(gtotal * conv, axis=0, keepdims=True)
                gtotal_b = gtotal.astype(BF16)
                gscaled = []
                for n in range(2):
                    at = slice(SEQ * n, SEQ * n + SEQ)
                    gy = head_rows([gtotal_b[at]], low)
                    gmixed = dot_right(gy, scaled[at])
                    mixed = []
                    for e in range(2):
                        decay = decay_of(running[n], turned[n], h + e, allowed[n])
                        weight = inner[n] * decay
                        mixed.append(weight.astype(BF16))
                        gm = gmixed[128 * e:128 * e + 128]
                        ginner[n] = ginner[n] + gm * decay
                        ggap = gm * weight
                        grun[n] = jnp.where(
                            lane == h + e, jnp.sum(ggap, axis=1, keepdims=True), grun[n])
                        colsum[n, h + e:h + e + 1, :] = jnp.sum(ggap, axis=0, keepdims=True)
                    gscaled.append(dot_left(jnp.concatenate(mixed, axis=0), gy))
                gscaled = jnp.concatenate(gscaled, axis=0)
                prod = gscaled * conv
                even = jnp.sum(jnp.where(low2, prod, 0.0), axis=1, keepdims=True)
                odd = jnp.sum(jnp.where(low2, 0.0, prod), axis=1, keepdims=True)
                gdelta = jnp.where(lane2 == h, even, jnp.where(lane2 == h + 1, odd, gdelta))
                gconv = gscaled * wide + gtotal * skip
                gpre = gconv * (sp * (1.0 + pre * (1.0 - sp)))
                gu, sums = conv_back(kf[:, KF_SSM + c:KF_SSM + c + 128], gpre, kernel, keeps)
                for k in range(4):
                    sg[SM_CONV + k:SM_CONV + k + 1, c:c + 128] = sums[k]
                k = raw0 + 1280 + 256 * b + 128 * q
                gb[:, k:k + 128] = gu.astype(BF16)
        grate = jnp.concatenate([
            dot_exact(masks[n], grun[n] - colsum[n].T, ((0,), (0,))) for n in range(2)], axis=0)
        gstep = (gdelta - grate * speed) * jax.nn.sigmoid(step)
        gb[:, raw0 + 384:raw0 + 512] = gstep.astype(BF16)
        c = t * 128
        sg[SM_BIAS:SM_BIAS + 1, c:c + 128] = jnp.sum(gstep, axis=0, keepdims=True)
        sg[SM_DEC:SM_DEC + 1, c:c + 128] = jnp.sum(grate * rate, axis=0, keepdims=True)

    gacts = []
    for n in range(2):
        gi = ginner[n].astype(BF16)
        gacts.append(jnp.concatenate(
            [dot_left(gi, acts[n][:, 128:256]), dot_plain(gi, acts[n][:, 0:128])], axis=1))
    gact = jnp.concatenate(gacts, axis=0)
    s = jax.nn.sigmoid(state_pre)
    gpre = gact * (s * (1.0 + state_pre * (1.0 - s)))
    gstate, sums = conv_back(state_raw, gpre, cst, keeps)
    for k in range(4):
        sg[SM_CST + k:SM_CST + k + 1, 0:256] = sums[k]
    gb[:, GB_ST:GB_ST + 256] = gstate.astype(BF16)
    save_g = pltpu.make_async_copy(gb, gb_hbm.at[slot], osem.at[0])
    save_g.start()

    loads.wait(2)
    for j in range(0, D, 256):
        gn[:, j:j + 256] = (
            dot_right(gb[:, GB_RAW:GB_RAW + 2 * D], wmix[0, j:j + 256, :])
            + dot_right(gb[:, GB_RAW + 2 * D:GB_RAW + 4 * D], wmix[1, j:j + 256, :])
            + dot_right(gb[:, GB_ST:GB_ST + 256], wst[j:j + 256, :]))
    norm_back(KF_X, SM_G1)
    for j in range(0, D, 256):
        gin_ref[:, j:j + 256] = gmid[:, j:j + 256]
        ginb_ref[:, j:j + 256] = gmid[:, j:j + 256].astype(BF16)
    save_s = pltpu.make_async_copy(sg, sg_hbm.at[slot], osem.at[1])
    save_s.start()
    save_g.wait()
    save_s.wait()


def any_spec():
    return pl.BlockSpec(memory_space=pl.ANY)


def vmem_spec():
    return pl.BlockSpec(memory_space=pltpu.VMEM)


def smem_spec():
    return pl.BlockSpec(memory_space=pltpu.SMEM)


def weight_scratch():
    return [pltpu.VMEM((2, D, 2 * D), BF16), pltpu.VMEM((2, D, D), BF16),
            pltpu.VMEM((2, D, 2 * D), BF16), pltpu.VMEM((2, D, D), BF16)]


def fwd_call(sc, tok, recv, tab, sm, wst, w, kept):
    def body(*refs):
        ins, rest = refs[:7], refs[7 + len(kept):]
        fwd_body(*ins, *rest)

    return pl.pallas_call(
        body,
        out_shape=(jax.ShapeDtypeStruct((ROWS, D), BF16),
                   jax.ShapeDtypeStruct((2, ROWS, KF_COLS), F32),
                   jax.ShapeDtypeStruct((2, ROWS, KB_COLS), BF16)),
        in_specs=[smem_spec()] + [vmem_spec()] * 5 + [any_spec()] * (1 + len(kept)),
        out_specs=(vmem_spec(), any_spec(), any_spec()),
        scratch_shapes=weight_scratch() + [
            pltpu.VMEM((ROWS, KF_COLS), F32), pltpu.VMEM((ROWS, KB_COLS), BF16),
            pltpu.SemaphoreType.DMA((8,)), pltpu.SemaphoreType.DMA((2,))],
        input_output_aliases={7: 1, 8: 2} if kept else {},
        compiler_params=pltpu.CompilerParams(vmem_limit_bytes=VMEM_LIMIT),
        name="layer_forward",
    )(sc, tok, recv, tab, sm, wst, w, *kept)


def bwd_call(sc, cot, recv, tab, sm, wst, w, kf, kb, grads):
    def body(*refs):
        ins, rest = refs[:9], refs[9 + len(grads):]
        bwd_body(*ins, *rest)

    return pl.pallas_call(
        body,
        out_shape=(jax.ShapeDtypeStruct((ROWS, D), F32),
                   jax.ShapeDtypeStruct((ROWS, D), BF16),
                   jax.ShapeDtypeStruct((2, ROWS, GB_COLS), BF16),
                   jax.ShapeDtypeStruct((2, SM_ROWS, SM_COLS), F32)),
        in_specs=[smem_spec()] + [vmem_spec()] * 5 + [any_spec()] * (3 + len(grads)),
        out_specs=(vmem_spec(), vmem_spec(), any_spec(), any_spec()),
        scratch_shapes=weight_scratch() + [
            pltpu.VMEM((ROWS, KF_COLS), F32), pltpu.VMEM((ROWS, KB_COLS), BF16),
            pltpu.VMEM((ROWS, GB_COLS), BF16), pltpu.VMEM((SM_ROWS, SM_COLS), F32),
            pltpu.VMEM((ROWS, D), F32), pltpu.VMEM((ROWS, D), F32), pltpu.VMEM((2, SEQ, 128), F32),
            pltpu.SemaphoreType.DMA((8,)), pltpu.SemaphoreType.DMA((5,)),
            pltpu.SemaphoreType.DMA((2,))],
        input_output_aliases={9: 2, 10: 3} if grads else {},
        compiler_params=pltpu.CompilerParams(vmem_limit_bytes=VMEM_LIMIT),
        name="layer_backward",
    )(sc, cot, recv, tab, sm, wst, w, kf, kb, *grads)


def tables_of(segs):
    index = jnp.arange(SEQ, dtype=jnp.int32)
    same = segs[:, None, :] == segs[:, :, None]
    mask = same & (index[None, None, :] <= index[None, :, None])
    pos = jnp.sum(mask, axis=2).astype(F32) - 1.0
    lane = jnp.arange(128, dtype=jnp.int32)
    frequency = BASE ** (-2.0 * (lane % 32).astype(F32) / HEAD)
    angle = pos[:, :, None] * frequency[None, None, :]
    sign = jnp.where((lane & 32) == 0, -1.0, 1.0)
    return jnp.concatenate(
        [jnp.cos(angle), jnp.sin(angle) * sign, mask.astype(F32)], axis=2).reshape(ROWS, 384)


A_COLS, B_COLS = W_FFN, W_COLS - W_FFN
MESH = pl.DeviceIdType.MESH


def where_am_i():
    core, d = lax.axis_index("tensor"), lax.axis_index("dp")
    return core, d // 8, (d // 2) % 4, d % 2


def place_on_dp(y, z, h):
    return {"dp": y * 8 + z * 2 + h}


class Copies:
    def __init__(self, send_sem, recv_sem):
        self.send_sem, self.recv_sem, self.all = send_sem, recv_sem, []

    def send(self, src, dst, device):
        k = len(self.all)
        copy = pltpu.make_async_remote_copy(
            src_ref=src, dst_ref=dst, send_sem=self.send_sem.at[k], recv_sem=self.recv_sem.at[k],
            device_id=device, device_id_type=MESH)
        copy.start()
        self.all.append(copy)
        return copy

    def drain(self, done=()):
        assert len(self.all) == self.send_sem.shape[0]
        for copy in self.all:
            if not any(copy is other for other in done):
                copy.wait_send()


def greet(core, y, z, h, more=()):
    barrier = pltpu.get_barrier_semaphore()
    others = [place_on_dp((y + 1) % 4, z, h), place_on_dp((y + 3) % 4, z, h),
              place_on_dp(y, (z + 1) % 4, h), place_on_dp(y, (z + 3) % 4, h),
              place_on_dp(y, z, 1 - h), {"tensor": 1 - core}]
    for other in (*others, *more):
        pl.semaphore_signal(barrier, inc=1, device_id=other, device_id_type=MESH)
    pl.semaphore_wait(barrier, len(others) + len(more))
    return others


GATHER_COPIES = 73


def gather_body(p, heads, cot, tab, w, all_heads, cot_late, tab_late, send_sem, recv_sem, own_sem):
    core, y, z, h = where_am_i()
    yp, ym, zp, zm, across, sibling = greet(core, y, z, h)
    own = pltpu.make_async_copy(p, w.at[core, y, z, h], own_sem.at[0])
    own.start()
    own_heads = pltpu.make_async_copy(heads, all_heads.at[core], own_sem.at[1])
    own_heads.start()
    net = Copies(send_sem, recv_sem)
    beside = [net.send(heads, all_heads.at[core], sibling)]
    partner = [net.send(p.at[:, cols], w.at[core, y, z, h, :, cols], across)
               for cols in (pl.ds(0, W_OUT), pl.ds(A_COLS, 2 * D))]
    top, bottom = pl.ds(0, SEQ), pl.ds(SEQ, SEQ)
    tops = [pltpu.make_async_copy(src.at[top], dst.at[top], own_sem.at[2 + k])
            for k, (src, dst) in enumerate(((cot, cot_late), (tab, tab_late)))]
    for copy in tops:
        copy.start()
    bottoms = [net.send(src.at[bottom], dst.at[bottom], across)
               for src, dst in ((cot, cot_late), (tab, tab_late))]
    a, b = pl.ds(0, A_COLS), pl.ds(A_COLS, B_COLS)
    all_halves = ((a, pl.ds(0, 1664), pl.ds(1664, 1536), yp, ym, zp, zm),
                  (b, pl.ds(A_COLS, 1536), pl.ds(A_COLS + 1536, 1536), zp, zm, yp, ym))
    most = ((pl.ds(0, W_OUT), pl.ds(0, 1152), pl.ds(1152, 1024), yp, ym, zp, zm),
            (pl.ds(A_COLS, 2 * D), pl.ds(A_COLS, D), pl.ds(A_COLS + D, D), zp, zm, yp, ym))
    rest = (pl.ds(W_OUT, D), pl.ds(W_DN, D))
    crossing = []

    def cross(k, step):
        block = plane(k, step, h, rest[k])
        crossing.append((net.send(block, block, across), plane(k, step, 1 - h, rest[k])))

    def crossed(count):
        for copy, block in crossing[:count]:
            copy.wait_recv()
            beside.append(net.send(block, block, sibling))
        del crossing[:count]

    def ring_block(k, step, hh, cols):
        if k == 0:
            return w.at[core, (y + step) % 4, z, hh, :, cols]
        return w.at[core, y, (z + step) % 4, hh, :, cols]

    def plane(k, step, hh, cols):
        if k == 0:
            return w.at[core, :, (z + step) % 4, hh, :, cols]
        return w.at[core, (y + step) % 4, :, hh, :, cols]

    def ring_one(hh, mine):
        copies = []
        for k, (cols, _, _, up, down, _, _) in enumerate(all_halves if mine else most):
            block = ring_block(k, 0, hh, cols)
            src = p.at[:, cols] if mine else block
            copies.append((net.send(src, block, up), net.send(src, block, down)))
        return copies

    def ring_one_on(hh, copies, halves):
        onward = []
        for k, (_, one, two, up, down, _, _) in enumerate(halves):
            copies[k][0].wait_recv()
            block = ring_block(k, 3, hh, one)
            going_up = net.send(block, block, up)
            copies[k][1].wait_recv()
            block = ring_block(k, 1, hh, two)
            onward.append((going_up, net.send(block, block, down)))
        return onward

    def ring_two(hh, onward, halves):
        copies = []
        for k, (cols, _, _, _, _, up, down) in enumerate(halves):
            onward[k][0].wait_recv()
            onward[k][1].wait_recv()
            block = plane(k, 0, hh, cols)
            copies.append((net.send(block, block, up), net.send(block, block, down)))
            beside.append(net.send(block, block, sibling))
            if halves is all_halves:
                cross(k, 0)
        return copies

    def ring_two_on(hh, copies, halves):
        onward = []
        for k, (cols, one, two, _, _, up, down) in enumerate(halves):
            copies[k][0].wait_recv()
            block = plane(k, 3, hh, one)
            going_up = net.send(block, block, up)
            copies[k][1].wait_recv()
            block = plane(k, 1, hh, two)
            onward.append((going_up, net.send(block, block, down)))
            for step in (3, 1):
                block = plane(k, step, hh, cols)
                beside.append(net.send(block, block, sibling))
                if halves is all_halves:
                    cross(k, step)
        return onward

    def ring_two_end(hh, onward, halves):
        for k, (_, one, two, _, _, _, _) in enumerate(halves):
            for copy, cols in zip(onward[k], (one, two)):
                copy.wait_recv()
                block = plane(k, 2, hh, cols)
                beside.append(net.send(block, block, sibling))
            if halves is all_halves:
                cross(k, 2)

    mine = ring_one_on(h, ring_one(h, True), all_halves)
    own.wait()
    own_heads.wait()
    mine = ring_two(h, mine, all_halves)
    for copy in partner:
        copy.wait_recv()
    theirs = ring_one_on(1 - h, ring_one(1 - h, False), most)
    mine = ring_two_on(h, mine, all_halves)
    theirs = ring_two(1 - h, theirs, most)
    ring_two_end(h, mine, all_halves)
    crossed(2)
    theirs = ring_two_on(1 - h, theirs, most)
    crossed(4)
    ring_two_end(1 - h, theirs, most)
    crossed(2)
    for copy in beside + bottoms:
        copy.wait_recv()
    for copy in tops:
        copy.wait()
    net.drain()


def gather_weights(packed, heads, cot, tab):
    return pl.pallas_call(
        gather_body,
        out_shape=(jax.ShapeDtypeStruct((2, 4, 4, 2, 32, W_COLS), BF16),
                   jax.ShapeDtypeStruct((2, 8, 128), F32),
                   jax.ShapeDtypeStruct((ROWS, D), BF16),
                   jax.ShapeDtypeStruct((ROWS, 384), F32)),
        in_specs=[any_spec()] * 4,
        out_specs=(any_spec(),) * 4,
        scratch_shapes=[pltpu.SemaphoreType.DMA((GATHER_COPIES,)),
                        pltpu.SemaphoreType.DMA((GATHER_COPIES,)), pltpu.SemaphoreType.DMA((4,))],
        compiler_params=pltpu.CompilerParams(collective_id=0, has_side_effects=True),
        name="gather_weights",
    )(packed, heads, cot, tab)


def relay_body(src, dst, send_sem, recv_sem):
    core, y, z, h = where_am_i()
    other = 1 - lax.axis_index("section")
    here = {"section": other}
    there = {"section": other, **place_on_dp(y, z, 1 - h)}
    barrier = pltpu.get_barrier_semaphore()
    for device in (here, there):
        pl.semaphore_signal(barrier, inc=1, device_id=device, device_id_type=MESH)
    pl.semaphore_wait(barrier, 2)
    net = Copies(send_sem, recv_sem)
    for start, device in ((0, here), (SEQ, there)):
        rows = pl.ds(start, SEQ)
        net.send(src.at[rows], dst.at[rows], device)
    for copy in net.all:
        copy.wait_recv()
    net.drain()


def relay(rows, collective_id):
    return pl.pallas_call(
        relay_body,
        out_shape=jax.ShapeDtypeStruct((ROWS, D), BF16),
        in_specs=[any_spec()],
        out_specs=any_spec(),
        scratch_shapes=[pltpu.SemaphoreType.DMA((2,)), pltpu.SemaphoreType.DMA((2,))],
        compiler_params=pltpu.CompilerParams(collective_id=collective_id, has_side_effects=True),
        name="relay_sections",
    )(rows)


REDUCE_COPIES = 15 + 34
ORDER = (2, 1, 3, 0)
GROUPS = (((0, A_COLS),), ((0, B_COLS),))
PARTS = ((0, W_OUT), (0, 2 * D))


def reduce_body(kb_hbm, gb_hbm, sg_hbm, out_hbm, gin_hbm, ginb_hbm, red, small, coming, stayed,
                kb, gb, sg, by_y, by_z, by_h, by_core, leaving, leaving_too, staying, staying_too,
                swapped, n1t, midt, n2t, outt, st, sent_a, sent_b, held_a, held_b, x1_a, x1_b, x2_a, x2_b,
                y1_a, y1_b, y2_a, y2_b, last, send_sem, recv_sem, load_sem):
    core, y, z, h = where_am_i()
    section = lax.axis_index("section")

    def load(k, src, dst):
        copy = pltpu.make_async_copy(src, dst, load_sem.at[k])
        copy.start()
        return copy

    def columns(k, src, dst, start, stop):
        at = pl.ds(start, stop - start)
        return load(k, src.at[0, :, at], dst.at[:, at])

    load_norms = columns(0, kb_hbm, kb, KB_N1, KB_Q)
    load_raw = columns(1, gb_hbm, gb, GB_GU, GB_COLS)
    load_s = load(2, sg_hbm.at[0], sg)
    load_rest = [columns(3, kb_hbm, kb, KB_Q, KB_COLS), columns(4, gb_hbm, gb, GB_OUT, GB_GU)]
    near, far_half = pl.ds(0, 512), pl.ds(512, 512)
    load_moved = [load(5, out_hbm.at[:, near], leaving), load(6, ginb_hbm.at[:, far_half], leaving_too),
                  load(7, gin_hbm.at[:, near], staying), load(8, out_hbm.at[:, far_half], staying_too)]
    yp, ym, zp, zm, across, sibling = greet(
        core, y, z, h, (place_on_dp((y + 2) % 4, z, h), place_on_dp(y, (z + 2) % 4, h),
                        *[{"section": 1 - section, "tensor": c, **place_on_dp(y, z, hh)}
                          for c in (core, 1 - core) for hh in (h, 1 - h)]))
    net = Copies(send_sem, recv_sem)

    def both(ref, c, n):
        return ref[:, pl.ds(c, n)]

    def turn(ref, c, to):
        for j in range(0, D, 256):
            v = both(ref, c + j, 256).T
            to[j // 256] = v.reshape(4, 64, 256)

    small_groups = (
        (by_y, y, [place_on_dp((y + k) % 4, z, h) for k in (1, 2, 3)]),
        (by_z, z, [place_on_dp(y, (z + k) % 4, h) for k in (1, 2, 3)]),
        (by_h, h, [across]), (by_core, core, [sibling]))

    def small_send(n, total):
        ref, at, others = small_groups[n]
        ref[at] = total
        return [net.send(ref.at[at], ref.at[at], other) for other in others]

    def small_sum(n, copies):
        for copy in copies:
            copy.wait_recv()
        ref = small_groups[n][0]
        total = ref[0] + ref[1]
        for k in range(2, ref.shape[0]):
            total = total + ref[k]
        return total

    load_s.wait()
    small_copies = small_send(0, sg[...])
    load_norms.wait()
    turn(kb, KB_N1, n1t)
    turn(kb, KB_N2, n2t)
    load_raw.wait()
    for j in range(4):
        v = dot_plain(n1t[j].reshape(256, 256), both(gb, GB_ST, 256)).astype(BF16)
        t, y0 = j // 2, 2 * (j % 2)
        v = v.reshape(2, 4, 2, 16, 256)
        st[t, y0] = v[0]
        st[t, y0 + 1] = v[1]
    for copy in load_rest:
        copy.wait()
    turn(gb, GB_MID, midt)
    turn(gb, GB_OUT, outt)

    def move_outputs():
        for copy in load_moved:
            copy.wait()
        first = section == 0
        leaving[...] = jnp.where(first, leaving_too[...], leaving[...])
        staying[...] = jnp.where(first, staying[...], staying_too[...].astype(F32))
        back = place_on_dp(y, z, h + section * (1 - 2 * h))
        copies = [net.send(staying.at[bottom], swapped, across)]
        for half, rows, place in ((top, rows_top, place_on_dp(y, z, h)),
                                  (bottom, rows_bottom, back)):
            for c in (core, 1 - core):
                copies.append(net.send(leaving.at[half], coming.at[rows],
                                       {"section": 1 - section, "tensor": c, **place}))
        copies.append(net.send(staying.at[top], stayed.at[rows_top], sibling))
        return copies

    def settle_outputs(copies):
        copies[0].wait_recv()
        copies[0].wait_send()
        staying[bottom, :] = jnp.where(section == 0, staying[bottom, :], swapped[...])
        copies.append(net.send(staying.at[bottom], stayed.at[rows_bottom], sibling))
        return load(9, staying, stayed.at[pl.ds(pl.multiple_of(core * 256, 256), 256)])

    top, bottom = pl.ds(0, SEQ), pl.ds(SEQ, SEQ)
    rows_top = pl.ds(pl.multiple_of(core * 256, 128), SEQ)
    rows_bottom = pl.ds(pl.multiple_of(core * 256 + SEQ, 128), SEQ)

    def wide(base, t, count, j, size):
        return pl.multiple_of(base + t * count + j * size, 128)

    def tiles(n, step):
        pl.loop(0, n)(step)

    def chunk(g, i, k, t, ref, add):
        def put(v, c, n):
            where = (i, slice(None), pl.ds(c, n))
            ref[where] = (v + ref[where].astype(F32) if add else v).astype(BF16)

        if k == 0:
            at = (z + ORDER[i]) % 4
            left = (n1t, midt)[g][:, at].reshape(256, 256)
        else:
            at = (y + ORDER[i]) % 4
            left = (n2t, outt)[g][at].reshape(256, 256)
        right, base = ((gb, GB_RAW), (kb, KB_AG), (gb, GB_GU), (kb, KB_HID))[2 * k + g]
        start, count = PARTS[k][g], 2 * D if g == 0 else D

        def step(j):
            put(dot_plain(left, both(right, wide(base, t, count, j, 512), 512)),
                pl.multiple_of(start + j * 512, 128), 512)

        tiles(count // 512, step)
        if k == 0 and g == 0:
            v = st[t, :, at].astype(F32)
            v = jnp.concatenate([v[..., 0:128], v[..., 128:256]], axis=2).reshape(256, 128)
            put(v, 2 * D, 128)

    def add_rows(ref, other, rows):
        def step(j):
            at = pl.ds(pl.multiple_of(j * 32, 32), 32)
            ref[at, :] = (ref[at, :].astype(F32) + other[at, :].astype(F32)).astype(BF16)
        pl.loop(0, rows // 32)(step)

    def add_two(ref, one, two, rows):
        def step(j):
            at = pl.ds(pl.multiple_of(j * 32, 32), 32)
            ref[at, :] = (ref[at, :].astype(F32) + one[at, :].astype(F32)
                          + two[at, :].astype(F32)).astype(BF16)
        pl.loop(0, rows // 32)(step)

    halves = ((sent_a, held_a, x1_a, x2_a, zp, zm), (sent_b, held_b, x1_b, x2_b, yp, ym))
    low, high = pl.ds(0, 128), pl.ds(128, 128)
    cols = [[pl.ds(*span) for span in spans] for spans in GROUPS]
    beside, far, near = {}, {}, {}

    def for_sibling(g, i, k):
        sent, held = halves[k][:2]
        chunk(0, i, k, 1 - core, sent, False)
        chunk(1, i, k, 1 - core, sent, False)
        at = cols[k][g]
        beside[g, i, k] = net.send(sent.at[i, :, at], held.at[i, :, at], sibling)

    steps = [(0, i, k) for i in range(4) for k in range(2)]
    for_sibling(*steps[0])
    for n, (g, i, k) in enumerate(steps):
        if n + 1 < len(steps):
            for_sibling(*steps[n + 1])
        _, held, x1, x2, up, down = halves[k]
        at = cols[k][g]
        beside[g, i, k].wait_recv()
        chunk(0, i, k, core, held, True)
        chunk(1, i, k, core, held, True)
        if i == 0:
            far[g, k] = (net.send(held.at[0, low, at], x1.at[0, :, at], up),
                         net.send(held.at[0, high, at], x1.at[1, :, at], down))
        if i == 1:
            near[g, k] = [net.send(held.at[1, high, at], x2.at[0, high, at], up)]
        if i == 2:
            near[g, k].append(net.send(held.at[2, low, at], x2.at[1, low, at], down))
        if n == 1:
            moved = move_outputs()
        if n == 7:
            kept_here = settle_outputs(moved)
        if n in (2, 3, 4):
            small_copies = small_send(n - 1, small_sum(n - 2, small_copies))
        if n == 5:
            small[...] = small_sum(3, small_copies)
    for g in range(len(GROUPS[0])):
        for k in range(2):
            _, held, x1, x2, up, down = halves[k]
            at = cols[k][g]
            far[g, k][0].wait_recv()
            add_rows(held.at[1, low, at], x1.at[0, :, at], 128)
            near[g, k].append(net.send(held.at[1, low, at], x2.at[0, low, at], up))
            far[g, k][1].wait_recv()
            add_rows(held.at[2, high, at], x1.at[1, :, at], 128)
            near[g, k].append(net.send(held.at[2, high, at], x2.at[1, high, at], down))

    rings = ((held_a, y1_a, y2_a, yp, ym, y), (held_b, y1_b, y2_b, zp, zm, z))
    far, close, final = {}, {}, {}

    def rows_of(g, k, step, part):
        held, place = rings[k][0], rings[k][5]
        start = pl.multiple_of(((place + step) % 4) * 64 + part * 32, 32)
        return held.at[3, pl.ds(start, 32), cols[k][g]]

    for g in range(len(GROUPS[0])):
        for k in range(2):
            _, held, x1, x2, _, _ = halves[k]
            _, y1, y2, up, down, _ = rings[k]
            at = cols[k][g]
            for copy in near[g, k]:
                copy.wait_recv()
            add_two(held.at[3, :, at], x2.at[0, :, at], x2.at[1, :, at], 256)
            far[g, k] = (net.send(rows_of(g, k, 2, 0), y1.at[0, :, at], up),
                         net.send(rows_of(g, k, 2, 1), y1.at[1, :, at], down))
            close[g, k] = [net.send(rows_of(g, k, 1, 1), y2.at[0, 1, :, at], up),
                           net.send(rows_of(g, k, 3, 0), y2.at[1, 0, :, at], down)]
    for g in range(len(GROUPS[0])):
        for k in range(2):
            _, y1, y2, up, down, _ = rings[k]
            at = cols[k][g]
            far[g, k][0].wait_recv()
            add_rows(rows_of(g, k, 1, 0), y1.at[0, :, at], 32)
            close[g, k].append(net.send(rows_of(g, k, 1, 0), y2.at[0, 0, :, at], up))
            far[g, k][1].wait_recv()
            add_rows(rows_of(g, k, 3, 1), y1.at[1, :, at], 32)
            close[g, k].append(net.send(rows_of(g, k, 3, 1), y2.at[1, 1, :, at], down))
    for g in range(len(GROUPS[0])):
        for k in range(2):
            y2 = rings[k][2]
            at = cols[k][g]
            for copy in close[g, k]:
                copy.wait_recv()
            for part in range(2):
                add_two(rows_of(g, k, 0, part), y2.at[0, part, :, at], y2.at[1, part, :, at], 32)
            start, size = GROUPS[k][g]
            whole = pl.ds(start + k * A_COLS, size)
            final[g, k] = whole, net.send(rows_of(g, k, 0, 1 - h), last.at[:, whole], across)
    for g in range(len(GROUPS[0])):
        for k in range(2):
            whole, copy = final[g, k]
            copy.wait_recv()
            red[:, whole] = rows_of(g, k, 0, h)[...].astype(F32) + last[:, whole].astype(F32)
    kept_here.wait()
    for copy in moved[1:]:
        copy.wait_recv()
    net.drain(moved[:1])


def reduce_grads(kb, gb, sg, out, gin, gin_b):
    def pair(cols, rows, count=2):
        return pltpu.VMEM((count, rows, cols), BF16)

    return pl.pallas_call(
        reduce_body,
        out_shape=(jax.ShapeDtypeStruct((32, W_COLS), F32),
                   jax.ShapeDtypeStruct((SM_ROWS, SM_COLS), F32),
                   jax.ShapeDtypeStruct((512, 512), BF16),
                   jax.ShapeDtypeStruct((512, 512), F32)),
        in_specs=[any_spec()] * 6,
        out_specs=(vmem_spec(), vmem_spec(), any_spec(), any_spec()),
        scratch_shapes=[
            pltpu.VMEM((ROWS, KB_COLS), BF16), pltpu.VMEM((ROWS, GB_COLS), BF16),
            pltpu.VMEM((SM_ROWS, SM_COLS), F32),
            *[pltpu.VMEM((n, SM_ROWS, SM_COLS), F32) for n in (4, 4, 2, 2)],
            *[pltpu.VMEM((256, 512), kind) for kind in (BF16, BF16, F32, BF16)],
            pltpu.VMEM((SEQ, 512), F32),
            *[pltpu.VMEM((4, 4, 64, 256), BF16)] * 4, pltpu.VMEM((2, 4, 4, 2, 16, 256), BF16),
            pair(A_COLS, 256, 4), pair(B_COLS, 256, 4), pair(A_COLS, 256, 4), pair(B_COLS, 256, 4),
            pair(A_COLS, 128), pair(B_COLS, 128), pair(A_COLS, 256), pair(B_COLS, 256),
            pair(A_COLS, 32), pair(B_COLS, 32),
            pltpu.VMEM((2, 2, 32, A_COLS), BF16), pltpu.VMEM((2, 2, 32, B_COLS), BF16),
            pltpu.VMEM((32, W_COLS), BF16),
            pltpu.SemaphoreType.DMA((REDUCE_COPIES,)), pltpu.SemaphoreType.DMA((REDUCE_COPIES,)),
            pltpu.SemaphoreType.DMA((10,))],
        compiler_params=pltpu.CompilerParams(
            collective_id=1, has_side_effects=True, vmem_limit_bytes=VMEM_LIMIT),
        name="reduce_grads",
    )(kb, gb, sg, out, gin, gin_b)


def spread(values, each, whole):
    turn = lax.broadcasted_iota(jnp.int32, (128, whole), 0)
    lane = lax.broadcasted_iota(jnp.int32, (128, whole), 1)
    line = lax.broadcasted_iota(jnp.int32, (64, whole), 0)
    where = lax.broadcasted_iota(jnp.int32, (64, whole), 1)
    pick = jnp.where((lane % each == turn) & (turn < each), 1.0, 0.0).astype(BF16)
    return jnp.sum(
        jnp.where(where // each == line, dot_plain(values, pick), 0.0), axis=0, keepdims=True)


def prepare_body(w, heads, sm, wst, tile, sem):
    copies = [pltpu.make_async_copy(
        w.at[:, :, :, :, pl.ds(0, 16), pl.ds(384, 128)], tile, sem.at[0])]
    for t in range(2):
        for half in range(2):
            copies.append(pltpu.make_async_copy(
                w.at[t, :, :, :, pl.ds(16 * half, 16), pl.ds(2 * D, 128)],
                wst.at[t, :, :, :, :, pl.ds(128 * half, 128)], sem.at[1 + 2 * t + half]))
    for copy in copies:
        copy.start()
    sm[...] = jnp.zeros_like(sm)
    for t in range(2):
        sm[SM_BIAS:SM_BIAS + 1, 128 * t:128 * t + 128] = heads[t, 0:1, :]
        sm[SM_DEC:SM_DEC + 1, 128 * t:128 * t + 128] = heads[t, 1:2, :]
        for p in range(6):
            c = 768 * t + 128 * p
            lane = lax.broadcasted_iota(jnp.int32, (1, 128), 1)
            sm[SM_SKIP:SM_SKIP + 1, c:c + 128] = jnp.where(
                lane < HEAD, heads[t, 2:3, 2 * p:2 * p + 1], heads[t, 2:3, 2 * p + 1:2 * p + 2])
    copies[0].wait()
    lines = tile[...].reshape(64, 16, 128).astype(F32)

    def line(row, first):
        return pltpu.roll(lines[:, row, :], 128 - first, 1).astype(BF16)

    sm[SM_G1:SM_G1 + 1, 0:D] = spread(line(0, 12), 16, D)
    sm[SM_G2:SM_G2 + 1, 0:D] = spread(line(0, 28), 16, D)
    for k in range(4):
        sm[SM_CONV + k:SM_CONV + k + 1, :] = spread(line(1, 12 + 24 * k), 24, SM_COLS)
        sm[SM_CST + k:SM_CST + k + 1, 0:256] = spread(line(0, 44 + 4 * k), 4, 256)
    for copy in copies[1:]:
        copy.wait()


def prepare(w, all_heads):
    sm, wst = pl.pallas_call(
        prepare_body,
        out_shape=(jax.ShapeDtypeStruct((SM_ROWS, SM_COLS), F32),
                   jax.ShapeDtypeStruct((2, 4, 4, 2, 16, 256), BF16)),
        in_specs=[any_spec(), vmem_spec()],
        out_specs=(vmem_spec(), vmem_spec()),
        scratch_shapes=[pltpu.VMEM((2, 4, 4, 2, 16, 128), BF16), pltpu.SemaphoreType.DMA((5,))],
        compiler_params=pltpu.CompilerParams(vmem_limit_bytes=VMEM_LIMIT),
        name="prepare_small",
    )(w, all_heads)
    return sm, wst.reshape(D, 256)


def finish_body(at, red, small, coming, stayed, final, igrad, g1, g2, query, key, value, attn,
                gate, ssm, step, conv, state, cst, bias, dec, skip, ssm_out, ffn_gate, ffn_up,
                ffn_down):
    first, core, place = at[0], at[1], at[2]
    final[...] = jnp.where(first == 1, coming[...], stayed[...].astype(BF16))
    igrad[...] = jnp.where(first == 1, stayed[...], coming[...].astype(F32))
    query[0] = red[:, 0:256]
    kv = red[:, 256:384]
    key[0] = kv[:, 0:64]
    value[0] = pltpu.roll(kv, 64, 1)[:, 0:64]
    step[0] = red[:, 384:512][:, 0:12]
    gate[0] = red[:, 512:1280]
    ssm[0] = red[:, 1280:2048]
    state[0, :, 0:128] = red[0:16, 2 * D:W_OUT]
    state[0, :, 128:256] = red[16:32, 2 * D:W_OUT]
    attn[0] = red[:, W_OUT:W_OUT + 256]
    ssm_out[0] = red[:, W_OUT + 256:W_FFN]
    ffn_gate[0] = red[:, W_FFN:W_FFN + D]
    ffn_up[0] = red[:, W_FFN + D:W_DN]
    ffn_down[0] = red[:, W_DN:W_COLS]

    def mine(rows, cols, size):
        v = small[rows, pl.ds(pl.multiple_of(place * size // 128 * 128, 128), cols)]
        return pltpu.roll(v, (cols - place * size % 128) % cols, 1)

    for k, (ref, size) in enumerate(((g1, 16), (g2, 16))):
        ref[...] = mine(pl.ds(0, 8), 128, size)[k:k + 1, 0:size]
    pair = jnp.concatenate([small[0:8, :], jnp.zeros((8, 128), F32)], axis=1)
    turned = pltpu.roll(pair, (SM_COLS + 128 - place * 24) % (SM_COLS + 128), 1)
    conv[0] = turned[SM_CONV:SM_CONV + 4, 0:24]
    tail = small[:, 0:256]
    turned = pltpu.roll(tail, (256 - place * 4) % 256, 1)
    cst[0] = turned[SM_CST:SM_CST + 4, 0:4]
    for row, ref in ((SM_BIAS, bias), (SM_DEC, dec)):
        v = small[8:16, pl.ds(pl.multiple_of(core * 128, 128), 128)]
        ref[...] = v[row - 8:row - 7, 0:12]
    lane = lax.broadcasted_iota(jnp.int32, (8, 128), 1)
    sums = jnp.zeros((8, 128), F32)
    for p in range(6):
        v = small[8:16, pl.ds(pl.multiple_of(core * 768 + 128 * p, 128), 128)]
        even = jnp.sum(jnp.where(lane < HEAD, v, 0.0), axis=1, keepdims=True)
        odd = jnp.sum(jnp.where(lane < HEAD, 0.0, v), axis=1, keepdims=True)
        sums = jnp.where(lane == 2 * p, even, jnp.where(lane == 2 * p + 1, odd, sums))
    skip[...] = sums[SM_SKIP - 8:SM_SKIP - 7, 0:12]


def finish(at, red, small, coming, stayed):
    shapes = [((512, 512), BF16)] + [(shape, F32) for shape in (
        (512, 512), (1, 16), (1, 16), (1, 32, 256), (1, 32, 64), (1, 32, 64), (1, 32, 256),
        (1, 32, 768), (1, 32, 768), (1, 32, 12), (1, 4, 24), (1, 16, 256), (1, 4, 4), (1, 12),
        (1, 12), (1, 12), (1, 32, 768), (1, 32, 1024), (1, 32, 1024), (1, 32, 1024))]
    outs = pl.pallas_call(
        finish_body,
        out_shape=tuple(jax.ShapeDtypeStruct(*shape) for shape in shapes),
        in_specs=[smem_spec()] + [vmem_spec()] * 4,
        out_specs=tuple(vmem_spec() for _ in shapes),
        compiler_params=pltpu.CompilerParams(vmem_limit_bytes=VMEM_LIMIT),
        name="finish_outputs",
    )(at, red, small, coming, stayed)
    turned = (7, 17, 20)
    return tuple(v.swapaxes(1, 2) if k in turned else v for k, v in enumerate(outs))


def local(tokens, segments, cotangent, gain_one, gain_two, w_query, key_weight, value_weight,
          w_attn_out, w_gate_ssm, w_ssm_in, w_step, conv_ssm, w_state, conv_state, step_bias,
          decay_log, skip_gain, w_ssm_out, w_ffn_gate, w_ffn_up, w_ffn_down):
    core = lax.axis_index("tensor")
    place = core * lax.axis_size("dp") + lax.axis_index("dp")
    first = lax.axis_index("section") == 0
    first_i = first.astype(jnp.int32)

    state = w_state[0]
    spare = 116
    one = jnp.concatenate([gain_one[0], gain_two[0], conv_state[0].ravel()])
    two = conv_ssm[0].ravel()
    smalls = jnp.concatenate([
        jnp.pad(v, (0, spare - v.shape[0]))[None] for v in (one, two)], axis=0)
    smalls = jnp.pad(smalls, ((0, 30), (0, 0)))
    heads = jnp.pad(jnp.concatenate([step_bias, decay_log, skip_gain]), ((0, 5), (0, 116)))
    packed = jnp.concatenate([
        w_query[0], key_weight[0], value_weight[0], w_step[0], smalls,
        w_gate_ssm[0], w_ssm_in[0], jnp.concatenate([state[:, 0:128], state[:, 128:256]], axis=0),
        w_attn_out[0].T, w_ssm_out[0].T, w_ffn_gate[0], w_ffn_up[0], w_ffn_down[0].T], axis=1)
    tok = lax.dynamic_slice_in_dim(tokens, core * ROWS, ROWS)
    cot = lax.dynamic_slice_in_dim(cotangent, core * ROWS, ROWS)
    tab = tables_of(lax.dynamic_slice_in_dim(segments, core * ROWS, ROWS).reshape(2, SEQ))
    gathered, all_heads, cot, tab_late = gather_weights(packed, heads, cot, tab)
    tab = jnp.where(first, tab, tab_late)
    sm, wst = prepare(gathered, all_heads)
    weights = gathered.reshape(2, D, W_COLS)

    real_first = jnp.stack([jnp.where(first, 0, 1), first_i])
    real_second = jnp.stack([jnp.where(first, 1, 0), first_i])
    nothing = jnp.zeros((ROWS, D), BF16)
    out, *kept = fwd_call(real_first, tok, nothing, tab, sm, wst, weights, ())
    received = relay(out, 2)
    out, *kept = fwd_call(real_second, tok, received, tab, sm, wst, weights, kept)
    _, gin_b, *grads = bwd_call(real_second, cot, nothing, tab, sm, wst, weights, *kept, ())
    received = relay(gin_b, 3)
    gin, gin_b, *grads = bwd_call(real_first, cot, received, tab, sm, wst, weights, *kept, grads)

    red, small, coming, stayed = reduce_grads(kept[1], grads[0], grads[1], out, gin, gin_b)
    at = jnp.stack([first_i, core, place])
    return finish(at, red, small, coming, stayed)


def solution(mesh):
    rows = P("dp", None)
    flat = P("section", ("tensor", "dp"))
    split_in = P("section", "dp", "tensor")
    split_out = P("section", "tensor", "dp")
    kernel = P("section", None, ("tensor", "dp"))
    head = P("section", "tensor")
    state = P("section", ("tensor", "dp"), None)
    params = (flat, flat, split_in, split_in, split_in, split_out, split_in, split_in, split_in,
              kernel, state, kernel, head, head, head, split_out, split_in, split_in, split_out)
    halves = P("dp", "section")
    return jax.shard_map(
        local, mesh=mesh, in_specs=(rows, P("dp"), rows, *params),
        out_specs=(halves, halves, *params), check_vma=False)
```

```python
from functools import partial

import jax
import jax.numpy as jnp
from jax import lax
from jax.experimental import pallas as pl
from jax.experimental.pallas import tpu as pltpu
from jax.sharding import PartitionSpec as P

F32 = jnp.float32
BF16 = jnp.bfloat16
EPS = 1e-05
BASE = 10000.0
SCALE = 0.125
NEG = -1e30
SEQ = 128
ROWS = 256
D = 1024
HEAD = 64

W_OUT, W_FFN, W_DN, W_COLS = 2176, 3200, 5248, 6272
KF_X, KF_MID, KF_GATE, KF_SSM, KF_Y, KF_STEP, KF_STATE, KF_GU, KF_COLS = (
    0, 1024, 2048, 3584, 5120, 6656, 6912, 7168, 11264)
KB_N1, KB_N2, KB_Q, KB_KV, KB_AG, KB_HID, KB_COLS = 0, 1024, 2048, 2560, 2816, 4864, 6912
GB_OUT, GB_MID, GB_GU, GB_RAW, GB_ST, GB_COLS = 0, 1024, 2048, 6144, 10240, 10496
SM_G1, SM_G2, SM_CONV, SM_CST, SM_BIAS, SM_DEC, SM_SKIP = 0, 1, 2, 6, 10, 11, 12
SM_ROWS, SM_COLS = 16, 1536
VMEM_LIMIT = 60 * 1024 * 1024
AHEAD = 6


def dot_plain(left, right):
    return jnp.dot(left, right, preferred_element_type=F32)


def dot_left(left, right):
    return lax.dot_general(left, right, (((0,), (0,)), ((), ())), preferred_element_type=F32)


def dot_right(left, right):
    return lax.dot_general(left, right, (((1,), (1,)), ((), ())), preferred_element_type=F32)


def dot_exact(left, right, dims):
    return lax.dot_general(
        left, right, (dims, ((), ())), preferred_element_type=F32, precision=lax.Precision.HIGHEST
    )


def lanes():
    lane = lax.broadcasted_iota(jnp.int32, (SEQ, 128), 1)
    wide = lax.broadcasted_iota(jnp.int32, (ROWS, 128), 1)
    return lane, lane < HEAD, wide < HEAD, (wide & 32) == 0


def swap_halves(v, first_half):
    return jnp.where(first_half, pltpu.roll(v, 96, 1), pltpu.roll(v, 32, 1))


def both_halves(v, low):
    turned = pltpu.roll(v.astype(F32), HEAD, 1).astype(BF16)
    return jnp.where(low, v, turned), jnp.where(low, turned, v)


def head_rows(pairs, low):
    zero = jnp.zeros_like(pairs[0])
    rows = []
    for pair in pairs:
        rows += [jnp.where(low, pair, zero), jnp.where(low, zero, pair)]
    return jnp.concatenate(rows, axis=0)


def conv_of(u, kernel, keeps):
    total = u * kernel[3]
    for o in (1, 2, 3):
        total = total + pltpu.roll(u, o, 0) * keeps[o] * kernel[3 - o]
    return total


def conv_back(u, g, kernel, keeps):
    back = g * kernel[3]
    sums = [None, None, None, jnp.sum(u * g, axis=0, keepdims=True)]
    for o in (1, 2, 3):
        kept = g * keeps[o]
        back = back + pltpu.roll(kept, ROWS - o, 0) * kernel[3 - o]
        sums[3 - o] = jnp.sum(pltpu.roll(u, o, 0) * kept, axis=0, keepdims=True)
    return back, sums


def softplus(v):
    return jnp.maximum(v, 0.0) + jnp.log1p(jnp.exp(-jnp.abs(v)))


def keeps_of(masks):
    pos = jnp.concatenate([jnp.sum(mask, axis=1, keepdims=True) for mask in masks]) - 1.0
    return [None] + [jnp.where(pos >= o, 1.0, 0.0) for o in (1, 2, 3)]


def softmax_rows(scores, mask4):
    scores = jnp.where(mask4, scores, NEG)
    e = jnp.exp(scores - jnp.max(scores, axis=1, keepdims=True))
    return e / jnp.sum(e, axis=1, keepdims=True)


class Loads:
    def __init__(self, copies, ahead):
        self.copies, self.next, self.ahead = copies, 0, ahead
        self.start(ahead)

    def start(self, count):
        for copy in self.copies[self.next:self.next + count]:
            copy.start()
        self.next += count

    def wait(self, count=1):
        for _ in range(count):
            self.copies[self.next - self.ahead].wait()
            self.start(1)


def weight_loads(w_hbm, column, ref, sem):
    return [pltpu.make_async_copy(
        w_hbm.at[t, :, pl.ds(column, ref.shape[2])], ref.at[t], sem.at[t]) for t in range(2)]


def decay_of(running, turned, head, allowed):
    gap = running[:, head:head + 1] - turned[head:head + 1, :]
    return jnp.exp(jnp.where(allowed, gap, NEG))


def geometry(tab):
    cos, sin = tab[:, 0:128], tab[:, 128:256]
    masks = [tab[SEQ * s:SEQ * s + SEQ, 256:384] for s in range(2)]
    return cos, sin, masks, [mask > 0.5 for mask in masks], keeps_of(masks)


def per_sequence(v):
    return v[0:SEQ], v[SEQ:ROWS]


def fwd_body(sc, tok, recv, tab, sm, wst, w_hbm, out_ref, kf_hbm, kb_hbm,
             wmix, wout, wffn, wdn, kf, kb, wsem, osem):
    loads = Loads(
        weight_loads(w_hbm, 0, wmix, wsem) + weight_loads(w_hbm, W_OUT, wout, wsem.at[pl.ds(2, 2)])
        + weight_loads(w_hbm, W_FFN, wffn, wsem.at[pl.ds(4, 2)])
        + weight_loads(w_hbm, W_DN, wdn, wsem.at[pl.ds(6, 2)]), AHEAD)
    slot, first = sc[0], sc[1]
    _, low, low2, first_half = lanes()
    cos, sin, masks, allowed, keeps = geometry(tab)
    square = jnp.zeros((ROWS, 1), F32)
    for j in range(0, D, 256):
        x = jnp.where(first == 1, tok[:, j:j + 256], recv[:, j:j + 256]).astype(F32)
        kf[:, KF_X + j:KF_X + j + 256] = x
        square = square + jnp.sum(x * x, axis=1, keepdims=True)
    r = lax.rsqrt(square * (1.0 / D) + EPS)
    for j in range(0, D, 256):
        kb[:, KB_N1 + j:KB_N1 + j + 256] = (
            kf[:, KF_X + j:KF_X + j + 256] * r * sm[SM_G1:SM_G1 + 1, j:j + 256]).astype(BF16)
    n1 = kb[:, KB_N1:KB_N1 + D]

    state_raw = dot_plain(n1, wst[...])
    kf[:, KF_STATE:KF_STATE + 256] = state_raw
    pre = conv_of(state_raw, [sm[SM_CST + k:SM_CST + k + 1, 0:256] for k in range(4)], keeps)
    act = (pre * jax.nn.sigmoid(pre)).astype(BF16)
    inner = [dot_right(v[:, 128:256], v[:, 0:128]) for v in per_sequence(act)]

    for t in range(2):
        loads.wait()
        qs = []
        raw = dot_plain(kb[:, KB_N1:KB_N1 + D], wmix[t, :, 0:256])
        for p in range(2):
            v = raw[:, 128 * p:128 * p + 128]
            qs.append((v * cos + swap_halves(v, first_half) * sin).astype(BF16))
            c = KB_Q + t * 256 + 128 * p
            kb[:, c:c + 128] = qs[p]
        raw = dot_plain(kb[:, KB_N1:KB_N1 + D], wmix[t, :, 256:512])
        v = raw[:, 0:128]
        kv = jnp.where(low2, v * cos + swap_halves(v, first_half) * sin, v).astype(BF16)
        kb[:, KB_KV + t * 128:KB_KV + t * 128 + 128] = kv
        step_raw = raw[:, 128:256]
        kf[:, KF_STEP + t * 128:KF_STEP + t * 128 + 128] = step_raw
        kk, vv = both_halves(kv, low2)
        for s in range(2):
            at = slice(SEQ * s, SEQ * s + SEQ)
            mask4 = jnp.concatenate([masks[s]] * 4, axis=0) > 0.5
            scores = dot_right(head_rows([q[at] for q in qs], low), kk[at]) * SCALE
            heads = dot_plain(softmax_rows(scores, mask4).astype(BF16), vv[at])
            for p in range(2):
                c = KB_AG + t * D + 128 * p
                kb[at, c:c + 128] = jnp.where(
                    low, heads[256 * p:256 * p + 128], heads[256 * p + 128:256 * p + 256]
                ).astype(BF16)

        delta = softplus(step_raw + sm[SM_BIAS:SM_BIAS + 1, t * 128:t * 128 + 128])
        rate = -delta * jnp.exp(sm[SM_DEC:SM_DEC + 1, t * 128:t * 128 + 128])
        running = [dot_exact(mask, v, ((1,), (0,))) for mask, v in zip(masks, per_sequence(rate))]
        turned = [v.T for v in running]
        for b in range(3):
            c0 = t * 768 + 256 * b
            gate2 = dot_plain(kb[:, KB_N1:KB_N1 + D], wmix[t, :, 512 + 256 * b:768 + 256 * b])
            kf[:, KF_GATE + c0:KF_GATE + c0 + 256] = gate2
            ssm2 = dot_plain(kb[:, KB_N1:KB_N1 + D], wmix[t, :, 1280 + 256 * b:1536 + 256 * b])
            kf[:, KF_SSM + c0:KF_SSM + c0 + 256] = ssm2
            for q in range(2):
                c = c0 + 128 * q
                h = 4 * b + 2 * q
                u = ssm2[:, 128 * q:128 * q + 128]
                pre = conv_of(
                    u, [sm[SM_CONV + k:SM_CONV + k + 1, c:c + 128] for k in range(4)], keeps)
                conv = pre * jax.nn.sigmoid(pre)
                scaled = (conv * jnp.where(low2, delta[:, h:h + 1], delta[:, h + 1:h + 2])
                          ).astype(BF16)
                for s in range(2):
                    at = slice(SEQ * s, SEQ * s + SEQ)
                    mixed = jnp.concatenate(
                        [(inner[s] * decay_of(running[s], turned[s], h + e, allowed[s])
                          ).astype(BF16) for e in range(2)], axis=1)
                    ssm_y = dot_plain(mixed, head_rows([scaled[at]], low))
                    kf[at, KF_Y + c:KF_Y + c + 128] = ssm_y
                    total = ssm_y + sm[SM_SKIP:SM_SKIP + 1, c:c + 128] * conv[at]
                    gate = kf[at, KF_GATE + c:KF_GATE + c + 128]
                    g = KB_AG + t * D + 256 + 256 * b + 128 * q
                    kb[at, g:g + 128] = (total * (gate * jax.nn.sigmoid(gate))).astype(BF16)

    loads.wait(2)
    square = jnp.zeros((ROWS, 1), F32)
    for j in range(0, D, 256):
        part = dot_right(kb[:, KB_AG:KB_AG + D], wout[0, j:j + 256, :]) + dot_right(
            kb[:, KB_AG + D:KB_AG + 2 * D], wout[1, j:j + 256, :])
        mid = kf[:, KF_X + j:KF_X + j + 256] + part
        kf[:, KF_MID + j:KF_MID + j + 256] = mid
        square = square + jnp.sum(mid * mid, axis=1, keepdims=True)
    r = lax.rsqrt(square * (1.0 / D) + EPS)
    for j in range(0, D, 256):
        kb[:, KB_N2 + j:KB_N2 + j + 256] = (
            kf[:, KF_MID + j:KF_MID + j + 256] * r * sm[SM_G2:SM_G2 + 1, j:j + 256]).astype(BF16)
    for t in range(2):
        loads.wait()
        for j in range(0, D, 256):
            gate = dot_plain(kb[:, KB_N2:KB_N2 + D], wffn[t, :, j:j + 256])
            up = dot_plain(kb[:, KB_N2:KB_N2 + D], wffn[t, :, D + j:D + j + 256])
            c = KF_GU + t * 2 * D + j
            kf[:, c:c + 256] = gate
            kf[:, c + D:c + D + 256] = up
            c = KB_HID + t * D + j
            kb[:, c:c + 256] = (gate * jax.nn.sigmoid(gate) * up).astype(BF16)
    save_f = pltpu.make_async_copy(kf, kf_hbm.at[slot], osem.at[0])
    save_b = pltpu.make_async_copy(kb, kb_hbm.at[slot], osem.at[1])
    save_f.start()
    save_b.start()
    loads.wait(2)
    for j in range(0, D, 256):
        part = dot_right(kb[:, KB_HID:KB_HID + D], wdn[0, j:j + 256, :]) + dot_right(
            kb[:, KB_HID + D:KB_HID + 2 * D], wdn[1, j:j + 256, :])
        out_ref[:, j:j + 256] = (kf[:, KF_MID + j:KF_MID + j + 256] + part).astype(BF16)
    save_f.wait()
    save_b.wait()


def bwd_body(sc, cot, recv, tab, sm, wst, w_hbm, kf_hbm, kb_hbm, gin_ref, ginb_ref, gb_hbm, sg_hbm,
             wmix, wout, wffn, wdn, kf, kb, gb, sg, gn, gmid, colsum, wsem, isem, osem):
    slot, first = sc[0], sc[1]
    kept = [pltpu.make_async_copy(
        kf_hbm.at[slot, :, pl.ds(a, b - a)], kf.at[:, pl.ds(a, b - a)], isem.at[n])
        for n, (a, b) in enumerate(((KF_GU, KF_GU + 2 * D), (KF_GU + 2 * D, KF_COLS),
                                    (KF_X, KF_GATE), (KF_GATE, KF_GU)))]
    kept.append(pltpu.make_async_copy(kb_hbm.at[slot], kb, isem.at[4]))
    down = weight_loads(w_hbm, W_DN, wdn, wsem)
    ffn = weight_loads(w_hbm, W_FFN, wffn, wsem.at[pl.ds(2, 2)])
    outer = weight_loads(w_hbm, W_OUT, wout, wsem.at[pl.ds(4, 2)])
    mix = weight_loads(w_hbm, 0, wmix, wsem.at[pl.ds(6, 2)])
    loads = Loads([down[0], kept[0], down[1], kept[1], ffn[0], ffn[1], kept[2], outer[0], kept[4],
                   kept[3], outer[1], mix[0], mix[1]], AHEAD)

    lane, low, low2, first_half = lanes()
    cos, sin, masks, allowed, keeps = geometry(tab)
    sg[...] = jnp.zeros_like(sg)

    for j in range(0, D, 256):
        gout = jnp.where(first == 1, recv[:, j:j + 256], cot[:, j:j + 256])
        gmid[:, j:j + 256] = gout.astype(F32)
        gb[:, GB_OUT + j:GB_OUT + j + 256] = gout
    for t in range(2):
        loads.wait(2)
        for j in range(0, D, 256):
            gh = dot_plain(gb[:, GB_OUT:GB_OUT + D], wdn[t, :, j:j + 256])
            c = KF_GU + t * 2 * D + j
            gate, up = kf[:, c:c + 256], kf[:, c + D:c + D + 256]
            s = jax.nn.sigmoid(gate)
            c = GB_GU + t * 2 * D + j
            gb[:, c:c + 256] = (gh * up * (s * (1.0 + gate * (1.0 - s)))).astype(BF16)
            gb[:, c + D:c + D + 256] = (gh * (gate * s)).astype(BF16)
    loads.wait(2)

    def norm_back(v0, gain_row):
        square = jnp.zeros((ROWS, 1), F32)
        cross = jnp.zeros((ROWS, 1), F32)
        for j in range(0, D, 256):
            v = kf[:, v0 + j:v0 + j + 256]
            square = square + jnp.sum(v * v, axis=1, keepdims=True)
            cross = cross + jnp.sum(
                v * gn[:, j:j + 256] * sm[gain_row:gain_row + 1, j:j + 256], axis=1, keepdims=True)
        r = lax.rsqrt(square * (1.0 / D) + EPS)
        factor = cross * (1.0 / D) * r * r * r
        for j in range(0, D, 256):
            v = kf[:, v0 + j:v0 + j + 256]
            g = gn[:, j:j + 256]
            sg[gain_row:gain_row + 1, j:j + 256] = jnp.sum(g * (v * r), axis=0, keepdims=True)
            gmid[:, j:j + 256] = gmid[:, j:j + 256] + (
                g * sm[gain_row:gain_row + 1, j:j + 256] * r - v * factor)

    for j in range(0, D, 256):
        gn[:, j:j + 256] = dot_right(gb[:, GB_GU:GB_GU + 2 * D], wffn[0, j:j + 256, :]) + dot_right(
            gb[:, GB_GU + 2 * D:GB_GU + 4 * D], wffn[1, j:j + 256, :])
    loads.wait()
    norm_back(KF_MID, SM_G2)
    for j in range(0, D, 256):
        gb[:, GB_MID + j:GB_MID + j + 256] = gmid[:, j:j + 256].astype(BF16)

    loads.wait(3)
    state_raw = kf[:, KF_STATE:KF_STATE + 256]
    cst = [sm[SM_CST + k:SM_CST + k + 1, 0:256] for k in range(4)]
    state_pre = conv_of(state_raw, cst, keeps)
    act = (state_pre * jax.nn.sigmoid(state_pre)).astype(BF16)
    acts = per_sequence(act)
    inner = [dot_right(v[:, 128:256], v[:, 0:128]) for v in acts]
    ginner = [jnp.zeros((SEQ, 128), F32), jnp.zeros((SEQ, 128), F32)]

    for t in range(2):
        if t == 1:
            loads.wait()
        raw0 = GB_RAW + t * 2 * D
        gatt = dot_plain(gb[:, GB_MID:GB_MID + D], wout[t, :, 0:256]).astype(BF16)
        kk, vv = both_halves(kb[:, KB_KV + t * 128:KB_KV + t * 128 + 128], low2)
        for s in range(2):
            at = slice(SEQ * s, SEQ * s + SEQ)
            mask4 = jnp.concatenate([masks[s]] * 4, axis=0) > 0.5
            gheads = head_rows([gatt[at, 0:128], gatt[at, 128:256]], low)
            c = KB_Q + t * 256
            qheads = head_rows([kb[at, c:c + 128], kb[at, c + 128:c + 256]], low)
            probs = softmax_rows(dot_right(qheads, kk[at]) * SCALE, mask4)
            gprobs = dot_right(gheads, vv[at])
            gscores = (probs * (gprobs - jnp.sum(probs * gprobs, axis=1, keepdims=True))
                       ).astype(BF16)
            gq = dot_plain(gscores, kk[at]) * SCALE
            turn, half = (cos[at], sin[at]), first_half[at]
            for p in range(2):
                v = jnp.where(low, gq[256 * p:256 * p + 128], gq[256 * p + 128:256 * p + 256])
                gb[at, raw0 + 128 * p:raw0 + 128 * p + 128] = (
                    v * turn[0] - swap_halves(v, half) * turn[1]).astype(BF16)
            gk = dot_left(gscores, qheads) * SCALE
            gk = gk + pltpu.roll(gk, HEAD, 1)
            gv = dot_left(probs.astype(BF16), gheads)
            gv = gv + pltpu.roll(gv, HEAD, 1)
            gb[at, raw0 + 256:raw0 + 384] = jnp.where(
                low, gk * turn[0] - swap_halves(gk, half) * turn[1], gv).astype(BF16)

        bias = sm[SM_BIAS:SM_BIAS + 1, t * 128:t * 128 + 128]
        speed = jnp.exp(sm[SM_DEC:SM_DEC + 1, t * 128:t * 128 + 128])
        step = kf[:, KF_STEP + t * 128:KF_STEP + t * 128 + 128] + bias
        delta = softplus(step)
        rate = -delta * speed
        running = [dot_exact(mask, v, ((1,), (0,))) for mask, v in zip(masks, per_sequence(rate))]
        turned = [v.T for v in running]
        grun = [jnp.zeros((SEQ, 128), F32), jnp.zeros((SEQ, 128), F32)]
        gdelta = jnp.zeros((ROWS, 128), F32)
        lane2 = jnp.concatenate([lane, lane], axis=0)
        colsum[...] = jnp.zeros_like(colsum)
        for b in range(3):
            gn[:, 0:256] = dot_plain(
                gb[:, GB_MID:GB_MID + D], wout[t, :, 256 + 256 * b:512 + 256 * b])
            for q in range(2):
                c = t * 768 + 256 * b + 128 * q
                h = 4 * b + 2 * q
                gg = gn[:, 128 * q:128 * q + 128]
                gate = kf[:, KF_GATE + c:KF_GATE + c + 128]
                kernel = [sm[SM_CONV + k:SM_CONV + k + 1, c:c + 128] for k in range(4)]
                skip = sm[SM_SKIP:SM_SKIP + 1, c:c + 128]
                pre = conv_of(kf[:, KF_SSM + c:KF_SSM + c + 128], kernel, keeps)
                sp = jax.nn.sigmoid(pre)
                conv = pre * sp
                wide = jnp.where(low2, delta[:, h:h + 1], delta[:, h + 1:h + 2])
                scaled = (conv * wide).astype(BF16)
                s = jax.nn.sigmoid(gate)
                gtotal = gg * (gate * s)
                total = kf[:, KF_Y + c:KF_Y + c + 128] + skip * conv
                k = raw0 + 512 + 256 * b + 128 * q
                gb[:, k:k + 128] = (gg * total * (s * (1.0 + gate * (1.0 - s)))).astype(BF16)
                sg[SM_SKIP:SM_SKIP + 1, c:c + 128] = jnp.sum(gtotal * conv, axis=0, keepdims=True)
                gtotal_b = gtotal.astype(BF16)
                gscaled = []
                for n in range(2):
                    at = slice(SEQ * n, SEQ * n + SEQ)
                    gy = head_rows([gtotal_b[at]], low)
                    gmixed = dot_right(gy, scaled[at])
                    mixed = []
                    for e in range(2):
                        decay = decay_of(running[n], turned[n], h + e, allowed[n])
                        weight = inner[n] * decay
                        mixed.append(weight.astype(BF16))
                        gm = gmixed[128 * e:128 * e + 128]
                        ginner[n] = ginner[n] + gm * decay
                        ggap = gm * weight
                        grun[n] = jnp.where(
                            lane == h + e, jnp.sum(ggap, axis=1, keepdims=True), grun[n])
                        colsum[n, h + e:h + e + 1, :] = jnp.sum(ggap, axis=0, keepdims=True)
                    gscaled.append(dot_left(jnp.concatenate(mixed, axis=0), gy))
                gscaled = jnp.concatenate(gscaled, axis=0)
                prod = gscaled * conv
                even = jnp.sum(jnp.where(low2, prod, 0.0), axis=1, keepdims=True)
                odd = jnp.sum(jnp.where(low2, 0.0, prod), axis=1, keepdims=True)
                gdelta = jnp.where(lane2 == h, even, jnp.where(lane2 == h + 1, odd, gdelta))
                gconv = gscaled * wide + gtotal * skip
                gpre = gconv * (sp * (1.0 + pre * (1.0 - sp)))
                gu, sums = conv_back(kf[:, KF_SSM + c:KF_SSM + c + 128], gpre, kernel, keeps)
                for k in range(4):
                    sg[SM_CONV + k:SM_CONV + k + 1, c:c + 128] = sums[k]
                k = raw0 + 1280 + 256 * b + 128 * q
                gb[:, k:k + 128] = gu.astype(BF16)
        grate = jnp.concatenate([
            dot_exact(masks[n], grun[n] - colsum[n].T, ((0,), (0,))) for n in range(2)], axis=0)
        gstep = (gdelta - grate * speed) * jax.nn.sigmoid(step)
        gb[:, raw0 + 384:raw0 + 512] = gstep.astype(BF16)
        c = t * 128
        sg[SM_BIAS:SM_BIAS + 1, c:c + 128] = jnp.sum(gstep, axis=0, keepdims=True)
        sg[SM_DEC:SM_DEC + 1, c:c + 128] = jnp.sum(grate * rate, axis=0, keepdims=True)

    gacts = []
    for n in range(2):
        gi = ginner[n].astype(BF16)
        gacts.append(jnp.concatenate(
            [dot_left(gi, acts[n][:, 128:256]), dot_plain(gi, acts[n][:, 0:128])], axis=1))
    gact = jnp.concatenate(gacts, axis=0)
    s = jax.nn.sigmoid(state_pre)
    gpre = gact * (s * (1.0 + state_pre * (1.0 - s)))
    gstate, sums = conv_back(state_raw, gpre, cst, keeps)
    for k in range(4):
        sg[SM_CST + k:SM_CST + k + 1, 0:256] = sums[k]
    gb[:, GB_ST:GB_ST + 256] = gstate.astype(BF16)
    save_g = pltpu.make_async_copy(gb, gb_hbm.at[slot], osem.at[0])
    save_g.start()

    loads.wait(2)
    for j in range(0, D, 256):
        gn[:, j:j + 256] = (
            dot_right(gb[:, GB_RAW:GB_RAW + 2 * D], wmix[0, j:j + 256, :])
            + dot_right(gb[:, GB_RAW + 2 * D:GB_RAW + 4 * D], wmix[1, j:j + 256, :])
            + dot_right(gb[:, GB_ST:GB_ST + 256], wst[j:j + 256, :]))
    norm_back(KF_X, SM_G1)
    for j in range(0, D, 256):
        gin_ref[:, j:j + 256] = gmid[:, j:j + 256]
        ginb_ref[:, j:j + 256] = gmid[:, j:j + 256].astype(BF16)
    save_s = pltpu.make_async_copy(sg, sg_hbm.at[slot], osem.at[1])
    save_s.start()
    save_g.wait()
    save_s.wait()


def any_spec():
    return pl.BlockSpec(memory_space=pl.ANY)


def vmem_spec():
    return pl.BlockSpec(memory_space=pltpu.VMEM)


def smem_spec():
    return pl.BlockSpec(memory_space=pltpu.SMEM)


def weight_scratch():
    return [pltpu.VMEM((2, D, 2 * D), BF16), pltpu.VMEM((2, D, D), BF16),
            pltpu.VMEM((2, D, 2 * D), BF16), pltpu.VMEM((2, D, D), BF16)]


def fwd_call(sc, tok, recv, tab, sm, wst, w, kept):
    def body(*refs):
        ins, rest = refs[:7], refs[7 + len(kept):]
        fwd_body(*ins, *rest)

    return pl.pallas_call(
        body,
        out_shape=(jax.ShapeDtypeStruct((ROWS, D), BF16),
                   jax.ShapeDtypeStruct((2, ROWS, KF_COLS), F32),
                   jax.ShapeDtypeStruct((2, ROWS, KB_COLS), BF16)),
        in_specs=[smem_spec()] + [vmem_spec()] * 5 + [any_spec()] * (1 + len(kept)),
        out_specs=(vmem_spec(), any_spec(), any_spec()),
        scratch_shapes=weight_scratch() + [
            pltpu.VMEM((ROWS, KF_COLS), F32), pltpu.VMEM((ROWS, KB_COLS), BF16),
            pltpu.SemaphoreType.DMA((8,)), pltpu.SemaphoreType.DMA((2,))],
        input_output_aliases={7: 1, 8: 2} if kept else {},
        compiler_params=pltpu.CompilerParams(vmem_limit_bytes=VMEM_LIMIT),
        name="layer_forward",
    )(sc, tok, recv, tab, sm, wst, w, *kept)


def bwd_call(sc, cot, recv, tab, sm, wst, w, kf, kb, grads):
    def body(*refs):
        ins, rest = refs[:9], refs[9 + len(grads):]
        bwd_body(*ins, *rest)

    return pl.pallas_call(
        body,
        out_shape=(jax.ShapeDtypeStruct((ROWS, D), F32),
                   jax.ShapeDtypeStruct((ROWS, D), BF16),
                   jax.ShapeDtypeStruct((2, ROWS, GB_COLS), BF16),
                   jax.ShapeDtypeStruct((2, SM_ROWS, SM_COLS), F32)),
        in_specs=[smem_spec()] + [vmem_spec()] * 5 + [any_spec()] * (3 + len(grads)),
        out_specs=(vmem_spec(), vmem_spec(), any_spec(), any_spec()),
        scratch_shapes=weight_scratch() + [
            pltpu.VMEM((ROWS, KF_COLS), F32), pltpu.VMEM((ROWS, KB_COLS), BF16),
            pltpu.VMEM((ROWS, GB_COLS), BF16), pltpu.VMEM((SM_ROWS, SM_COLS), F32),
            pltpu.VMEM((ROWS, D), F32), pltpu.VMEM((ROWS, D), F32), pltpu.VMEM((2, SEQ, 128), F32),
            pltpu.SemaphoreType.DMA((8,)), pltpu.SemaphoreType.DMA((5,)),
            pltpu.SemaphoreType.DMA((2,))],
        input_output_aliases={9: 2, 10: 3} if grads else {},
        compiler_params=pltpu.CompilerParams(vmem_limit_bytes=VMEM_LIMIT),
        name="layer_backward",
    )(sc, cot, recv, tab, sm, wst, w, kf, kb, *grads)


def tables_of(segs):
    index = jnp.arange(SEQ, dtype=jnp.int32)
    same = segs[:, None, :] == segs[:, :, None]
    mask = same & (index[None, None, :] <= index[None, :, None])
    pos = jnp.sum(mask, axis=2).astype(F32) - 1.0
    lane = jnp.arange(128, dtype=jnp.int32)
    frequency = BASE ** (-2.0 * (lane % 32).astype(F32) / HEAD)
    angle = pos[:, :, None] * frequency[None, None, :]
    sign = jnp.where((lane & 32) == 0, -1.0, 1.0)
    return jnp.concatenate(
        [jnp.cos(angle), jnp.sin(angle) * sign, mask.astype(F32)], axis=2).reshape(ROWS, 384)


A_COLS, B_COLS = W_FFN, W_COLS - W_FFN
MESH = pl.DeviceIdType.MESH


def where_am_i():
    core, d = lax.axis_index("tensor"), lax.axis_index("dp")
    return core, d // 8, (d // 2) % 4, d % 2


def place_on_dp(y, z, h):
    return {"dp": y * 8 + z * 2 + h}


class Copies:
    def __init__(self, send_sem, recv_sem):
        self.send_sem, self.recv_sem, self.all = send_sem, recv_sem, []

    def send(self, src, dst, device):
        k = len(self.all)
        copy = pltpu.make_async_remote_copy(
            src_ref=src, dst_ref=dst, send_sem=self.send_sem.at[k], recv_sem=self.recv_sem.at[k],
            device_id=device, device_id_type=MESH)
        copy.start()
        self.all.append(copy)
        return copy

    def drain(self, done=()):
        assert len(self.all) == self.send_sem.shape[0]
        for copy in self.all:
            if not any(copy is other for other in done):
                copy.wait_send()


def greet(core, y, z, h, more=()):
    barrier = pltpu.get_barrier_semaphore()
    others = [place_on_dp((y + 1) % 4, z, h), place_on_dp((y + 3) % 4, z, h),
              place_on_dp(y, (z + 1) % 4, h), place_on_dp(y, (z + 3) % 4, h),
              place_on_dp(y, z, 1 - h), {"tensor": 1 - core}]
    for other in (*others, *more):
        pl.semaphore_signal(barrier, inc=1, device_id=other, device_id_type=MESH)
    pl.semaphore_wait(barrier, len(others) + len(more))
    return others


GATHER_COPIES = 73


def gather_body(p, heads, cot, tab, w, all_heads, cot_late, tab_late, send_sem, recv_sem, own_sem):
    core, y, z, h = where_am_i()
    yp, ym, zp, zm, across, sibling = greet(core, y, z, h)
    own = pltpu.make_async_copy(p, w.at[core, y, z, h], own_sem.at[0])
    own.start()
    own_heads = pltpu.make_async_copy(heads, all_heads.at[core], own_sem.at[1])
    own_heads.start()
    net = Copies(send_sem, recv_sem)
    beside = [net.send(heads, all_heads.at[core], sibling)]
    partner = [net.send(p.at[:, cols], w.at[core, y, z, h, :, cols], across)
               for cols in (pl.ds(0, W_OUT), pl.ds(A_COLS, 2 * D))]
    top, bottom = pl.ds(0, SEQ), pl.ds(SEQ, SEQ)
    tops = [pltpu.make_async_copy(src.at[top], dst.at[top], own_sem.at[2 + k])
            for k, (src, dst) in enumerate(((cot, cot_late), (tab, tab_late)))]
    for copy in tops:
        copy.start()
    bottoms = [net.send(src.at[bottom], dst.at[bottom], across)
               for src, dst in ((cot, cot_late), (tab, tab_late))]
    a, b = pl.ds(0, A_COLS), pl.ds(A_COLS, B_COLS)
    all_halves = ((a, pl.ds(0, 1664), pl.ds(1664, 1536), yp, ym, zp, zm),
                  (b, pl.ds(A_COLS, 1536), pl.ds(A_COLS + 1536, 1536), zp, zm, yp, ym))
    most = ((pl.ds(0, W_OUT), pl.ds(0, 1152), pl.ds(1152, 1024), yp, ym, zp, zm),
            (pl.ds(A_COLS, 2 * D), pl.ds(A_COLS, D), pl.ds(A_COLS + D, D), zp, zm, yp, ym))
    rest = (pl.ds(W_OUT, D), pl.ds(W_DN, D))
    crossing = []

    def cross(k, step):
        block = plane(k, step, h, rest[k])
        crossing.append((net.send(block, block, across), plane(k, step, 1 - h, rest[k])))

    def crossed(count):
        for copy, block in crossing[:count]:
            copy.wait_recv()
            beside.append(net.send(block, block, sibling))
        del crossing[:count]

    def ring_block(k, step, hh, cols):
        if k == 0:
            return w.at[core, (y + step) % 4, z, hh, :, cols]
        return w.at[core, y, (z + step) % 4, hh, :, cols]

    def plane(k, step, hh, cols):
        if k == 0:
            return w.at[core, :, (z + step) % 4, hh, :, cols]
        return w.at[core, (y + step) % 4, :, hh, :, cols]

    def ring_one(hh, mine):
        copies = []
        for k, (cols, _, _, up, down, _, _) in enumerate(all_halves if mine else most):
            block = ring_block(k, 0, hh, cols)
            src = p.at[:, cols] if mine else block
            copies.append((net.send(src, block, up), net.send(src, block, down)))
        return copies

    def ring_one_on(hh, copies, halves):
        onward = []
        for k, (_, one, two, up, down, _, _) in enumerate(halves):
            copies[k][0].wait_recv()
            block = ring_block(k, 3, hh, one)
            going_up = net.send(block, block, up)
            copies[k][1].wait_recv()
            block = ring_block(k, 1, hh, two)
            onward.append((going_up, net.send(block, block, down)))
        return onward

    def ring_two(hh, onward, halves):
        copies = []
        for k, (cols, _, _, _, _, up, down) in enumerate(halves):
            onward[k][0].wait_recv()
            onward[k][1].wait_recv()
            block = plane(k, 0, hh, cols)
            copies.append((net.send(block, block, up), net.send(block, block, down)))
            beside.append(net.send(block, block, sibling))
            if halves is all_halves:
                cross(k, 0)
        return copies

    def ring_two_on(hh, copies, halves):
        onward = []
        for k, (cols, one, two, _, _, up, down) in enumerate(halves):
            copies[k][0].wait_recv()
            block = plane(k, 3, hh, one)
            going_up = net.send(block, block, up)
            copies[k][1].wait_recv()
            block = plane(k, 1, hh, two)
            onward.append((going_up, net.send(block, block, down)))
            for step in (3, 1):
                block = plane(k, step, hh, cols)
                beside.append(net.send(block, block, sibling))
                if halves is all_halves:
                    cross(k, step)
        return onward

    def ring_two_end(hh, onward, halves):
        for k, (_, one, two, _, _, _, _) in enumerate(halves):
            for copy, cols in zip(onward[k], (one, two)):
                copy.wait_recv()
                block = plane(k, 2, hh, cols)
                beside.append(net.send(block, block, sibling))
            if halves is all_halves:
                cross(k, 2)

    mine = ring_one_on(h, ring_one(h, True), all_halves)
    own.wait()
    own_heads.wait()
    mine = ring_two(h, mine, all_halves)
    for copy in partner:
        copy.wait_recv()
    theirs = ring_one_on(1 - h, ring_one(1 - h, False), most)
    mine = ring_two_on(h, mine, all_halves)
    theirs = ring_two(1 - h, theirs, most)
    ring_two_end(h, mine, all_halves)
    crossed(2)
    theirs = ring_two_on(1 - h, theirs, most)
    crossed(4)
    ring_two_end(1 - h, theirs, most)
    crossed(2)
    for copy in beside + bottoms:
        copy.wait_recv()
    for copy in tops:
        copy.wait()
    net.drain()


def gather_weights(packed, heads, cot, tab):
    return pl.pallas_call(
        gather_body,
        out_shape=(jax.ShapeDtypeStruct((2, 4, 4, 2, 32, W_COLS), BF16),
                   jax.ShapeDtypeStruct((2, 8, 128), F32),
                   jax.ShapeDtypeStruct((ROWS, D), BF16),
                   jax.ShapeDtypeStruct((ROWS, 384), F32)),
        in_specs=[any_spec()] * 4,
        out_specs=(any_spec(),) * 4,
        scratch_shapes=[pltpu.SemaphoreType.DMA((GATHER_COPIES,)),
                        pltpu.SemaphoreType.DMA((GATHER_COPIES,)), pltpu.SemaphoreType.DMA((4,))],
        compiler_params=pltpu.CompilerParams(collective_id=0, has_side_effects=True),
        name="gather_weights",
    )(packed, heads, cot, tab)


def relay_body(src, dst, send_sem, recv_sem):
    core, y, z, h = where_am_i()
    other = 1 - lax.axis_index("section")
    here = {"section": other}
    there = {"section": other, **place_on_dp(y, z, 1 - h)}
    barrier = pltpu.get_barrier_semaphore()
    for device in (here, there):
        pl.semaphore_signal(barrier, inc=1, device_id=device, device_id_type=MESH)
    pl.semaphore_wait(barrier, 2)
    net = Copies(send_sem, recv_sem)
    for start, device in ((0, here), (SEQ, there)):
        rows = pl.ds(start, SEQ)
        net.send(src.at[rows], dst.at[rows], device)
    for copy in net.all:
        copy.wait_recv()
    net.drain()


def relay(rows, collective_id):
    return pl.pallas_call(
        relay_body,
        out_shape=jax.ShapeDtypeStruct((ROWS, D), BF16),
        in_specs=[any_spec()],
        out_specs=any_spec(),
        scratch_shapes=[pltpu.SemaphoreType.DMA((2,)), pltpu.SemaphoreType.DMA((2,))],
        compiler_params=pltpu.CompilerParams(collective_id=collective_id, has_side_effects=True),
        name="relay_sections",
    )(rows)


REDUCE_COPIES = 15 + 34
ORDER = (2, 1, 3, 0)
GROUPS = (((0, A_COLS),), ((0, B_COLS),))
PARTS = ((0, W_OUT), (0, 2 * D))


def reduce_body(kb_hbm, gb_hbm, sg_hbm, out_hbm, gin_hbm, ginb_hbm, red, small, coming, stayed,
                kb, gb, sg, by_y, by_z, by_h, by_core, leaving, leaving_too, staying, staying_too,
                swapped, n1t, midt, n2t, outt, st, sent_a, sent_b, held_a, held_b, x1_a, x1_b, x2_a, x2_b,
                y1_a, y1_b, y2_a, y2_b, last, send_sem, recv_sem, load_sem):
    core, y, z, h = where_am_i()
    section = lax.axis_index("section")

    def load(k, src, dst):
        copy = pltpu.make_async_copy(src, dst, load_sem.at[k])
        copy.start()
        return copy

    def columns(k, src, dst, start, stop):
        at = pl.ds(start, stop - start)
        return load(k, src.at[0, :, at], dst.at[:, at])

    load_norms = columns(0, kb_hbm, kb, KB_N1, KB_Q)
    load_raw = columns(1, gb_hbm, gb, GB_GU, GB_COLS)
    load_s = load(2, sg_hbm.at[0], sg)
    load_rest = [columns(3, kb_hbm, kb, KB_Q, KB_COLS), columns(4, gb_hbm, gb, GB_OUT, GB_GU)]
    near, far_half = pl.ds(0, 512), pl.ds(512, 512)
    load_moved = [load(5, out_hbm.at[:, near], leaving), load(6, ginb_hbm.at[:, far_half], leaving_too),
                  load(7, gin_hbm.at[:, near], staying), load(8, out_hbm.at[:, far_half], staying_too)]
    yp, ym, zp, zm, across, sibling = greet(
        core, y, z, h, (place_on_dp((y + 2) % 4, z, h), place_on_dp(y, (z + 2) % 4, h),
                        *[{"section": 1 - section, "tensor": c, **place_on_dp(y, z, hh)}
                          for c in (core, 1 - core) for hh in (h, 1 - h)]))
    net = Copies(send_sem, recv_sem)

    def both(ref, c, n):
        return ref[:, pl.ds(c, n)]

    def turn(ref, c, to):
        for j in range(0, D, 256):
            v = both(ref, c + j, 256).T
            to[j // 256] = v.reshape(4, 64, 256)

    small_groups = (
        (by_y, y, [place_on_dp((y + k) % 4, z, h) for k in (1, 2, 3)]),
        (by_z, z, [place_on_dp(y, (z + k) % 4, h) for k in (1, 2, 3)]),
        (by_h, h, [across]), (by_core, core, [sibling]))

    def small_send(n, total):
        ref, at, others = small_groups[n]
        ref[at] = total
        return [net.send(ref.at[at], ref.at[at], other) for other in others]

    def small_sum(n, copies):
        for copy in copies:
            copy.wait_recv()
        ref = small_groups[n][0]
        total = ref[0] + ref[1]
        for k in range(2, ref.shape[0]):
            total = total + ref[k]
        return total

    load_s.wait()
    small_copies = small_send(0, sg[...])
    load_norms.wait()
    turn(kb, KB_N1, n1t)
    turn(kb, KB_N2, n2t)
    load_raw.wait()
    for j in range(4):
        v = dot_plain(n1t[j].reshape(256, 256), both(gb, GB_ST, 256)).astype(BF16)
        t, y0 = j // 2, 2 * (j % 2)
        v = v.reshape(2, 4, 2, 16, 256)
        st[t, y0] = v[0]
        st[t, y0 + 1] = v[1]
    for copy in load_rest:
        copy.wait()
    turn(gb, GB_MID, midt)
    turn(gb, GB_OUT, outt)

    def move_outputs():
        for copy in load_moved:
            copy.wait()
        first = section == 0
        leaving[...] = jnp.where(first, leaving_too[...], leaving[...])
        staying[...] = jnp.where(first, staying[...], staying_too[...].astype(F32))
        back = place_on_dp(y, z, h + section * (1 - 2 * h))
        copies = [net.send(staying.at[bottom], swapped, across)]
        for half, rows, place in ((top, rows_top, place_on_dp(y, z, h)),
                                  (bottom, rows_bottom, back)):
            for c in (core, 1 - core):
                copies.append(net.send(leaving.at[half], coming.at[rows],
                                       {"section": 1 - section, "tensor": c, **place}))
        copies.append(net.send(staying.at[top], stayed.at[rows_top], sibling))
        return copies

    def settle_outputs(copies):
        copies[0].wait_recv()
        copies[0].wait_send()
        staying[bottom, :] = jnp.where(section == 0, staying[bottom, :], swapped[...])
        copies.append(net.send(staying.at[bottom], stayed.at[rows_bottom], sibling))
        return load(9, staying, stayed.at[pl.ds(pl.multiple_of(core * 256, 256), 256)])

    top, bottom = pl.ds(0, SEQ), pl.ds(SEQ, SEQ)
    rows_top = pl.ds(pl.multiple_of(core * 256, 128), SEQ)
    rows_bottom = pl.ds(pl.multiple_of(core * 256 + SEQ, 128), SEQ)

    def wide(base, t, count, j, size):
        return pl.multiple_of(base + t * count + j * size, 128)

    def tiles(n, step):
        pl.loop(0, n)(step)

    def chunk(g, i, k, t, ref, add):
        def put(v, c, n):
            where = (i, slice(None), pl.ds(c, n))
            ref[where] = (v + ref[where].astype(F32) if add else v).astype(BF16)

        if k == 0:
            at = (z + ORDER[i]) % 4
            left = (n1t, midt)[g][:, at].reshape(256, 256)
        else:
            at = (y + ORDER[i]) % 4
            left = (n2t, outt)[g][at].reshape(256, 256)
        right, base = ((gb, GB_RAW), (kb, KB_AG), (gb, GB_GU), (kb, KB_HID))[2 * k + g]
        start, count = PARTS[k][g], 2 * D if g == 0 else D

        def step(j):
            put(dot_plain(left, both(right, wide(base, t, count, j, 512), 512)),
                pl.multiple_of(start + j * 512, 128), 512)

        tiles(count // 512, step)
        if k == 0 and g == 0:
            v = st[t, :, at].astype(F32)
            v = jnp.concatenate([v[..., 0:128], v[..., 128:256]], axis=2).reshape(256, 128)
            put(v, 2 * D, 128)

    def add_rows(ref, other, rows):
        def step(j):
            at = pl.ds(pl.multiple_of(j * 32, 32), 32)
            ref[at, :] = (ref[at, :].astype(F32) + other[at, :].astype(F32)).astype(BF16)
        pl.loop(0, rows // 32)(step)

    def add_two(ref, one, two, rows):
        def step(j):
            at = pl.ds(pl.multiple_of(j * 32, 32), 32)
            ref[at, :] = (ref[at, :].astype(F32) + one[at, :].astype(F32)
                          + two[at, :].astype(F32)).astype(BF16)
        pl.loop(0, rows // 32)(step)

    halves = ((sent_a, held_a, x1_a, x2_a, zp, zm), (sent_b, held_b, x1_b, x2_b, yp, ym))
    low, high = pl.ds(0, 128), pl.ds(128, 128)
    cols = [[pl.ds(*span) for span in spans] for spans in GROUPS]
    beside, far, near = {}, {}, {}

    def for_sibling(g, i, k):
        sent, held = halves[k][:2]
        chunk(0, i, k, 1 - core, sent, False)
        chunk(1, i, k, 1 - core, sent, False)
        at = cols[k][g]
        beside[g, i, k] = net.send(sent.at[i, :, at], held.at[i, :, at], sibling)

    steps = [(0, i, k) for i in range(4) for k in range(2)]
    for_sibling(*steps[0])
    for n, (g, i, k) in enumerate(steps):
        if n + 1 < len(steps):
            for_sibling(*steps[n + 1])
        _, held, x1, x2, up, down = halves[k]
        at = cols[k][g]
        beside[g, i, k].wait_recv()
        chunk(0, i, k, core, held, True)
        chunk(1, i, k, core, held, True)
        if n < 3:
            small_copies = small_send(n + 1, small_sum(n, small_copies))
        if n == 3:
            small[...] = small_sum(3, small_copies)
        if i == 0:
            far[g, k] = (net.send(held.at[0, low, at], x1.at[0, :, at], up),
                         net.send(held.at[0, high, at], x1.at[1, :, at], down))
        if i == 1:
            near[g, k] = [net.send(held.at[1, high, at], x2.at[0, high, at], up)]
        if i == 2:
            near[g, k].append(net.send(held.at[2, low, at], x2.at[1, low, at], down))
        if n == 1:
            moved = move_outputs()
        if n == 7:
            kept_here = settle_outputs(moved)
    for g in range(len(GROUPS[0])):
        for k in range(2):
            _, held, x1, x2, up, down = halves[k]
            at = cols[k][g]
            far[g, k][0].wait_recv()
            add_rows(held.at[1, low, at], x1.at[0, :, at], 128)
            near[g, k].append(net.send(held.at[1, low, at], x2.at[0, low, at], up))
            far[g, k][1].wait_recv()
            add_rows(held.at[2, high, at], x1.at[1, :, at], 128)
            near[g, k].append(net.send(held.at[2, high, at], x2.at[1, high, at], down))

    rings = ((held_a, y1_a, y2_a, yp, ym, y), (held_b, y1_b, y2_b, zp, zm, z))
    far, close, final = {}, {}, {}

    def rows_of(g, k, step, part):
        held, place = rings[k][0], rings[k][5]
        start = pl.multiple_of(((place + step) % 4) * 64 + part * 32, 32)
        return held.at[3, pl.ds(start, 32), cols[k][g]]

    for g in range(len(GROUPS[0])):
        for k in range(2):
            _, held, x1, x2, _, _ = halves[k]
            _, y1, y2, up, down, _ = rings[k]
            at = cols[k][g]
            for copy in near[g, k]:
                copy.wait_recv()
            add_two(held.at[3, :, at], x2.at[0, :, at], x2.at[1, :, at], 256)
            far[g, k] = (net.send(rows_of(g, k, 2, 0), y1.at[0, :, at], up),
                         net.send(rows_of(g, k, 2, 1), y1.at[1, :, at], down))
            close[g, k] = [net.send(rows_of(g, k, 1, 1), y2.at[0, 1, :, at], up),
                           net.send(rows_of(g, k, 3, 0), y2.at[1, 0, :, at], down)]
    for g in range(len(GROUPS[0])):
        for k in range(2):
            _, y1, y2, up, down, _ = rings[k]
            at = cols[k][g]
            far[g, k][0].wait_recv()
            add_rows(rows_of(g, k, 1, 0), y1.at[0, :, at], 32)
            close[g, k].append(net.send(rows_of(g, k, 1, 0), y2.at[0, 0, :, at], up))
            far[g, k][1].wait_recv()
            add_rows(rows_of(g, k, 3, 1), y1.at[1, :, at], 32)
            close[g, k].append(net.send(rows_of(g, k, 3, 1), y2.at[1, 1, :, at], down))
    for g in range(len(GROUPS[0])):
        for k in range(2):
            y2 = rings[k][2]
            at = cols[k][g]
            for copy in close[g, k]:
                copy.wait_recv()
            for part in range(2):
                add_two(rows_of(g, k, 0, part), y2.at[0, part, :, at], y2.at[1, part, :, at], 32)
            start, size = GROUPS[k][g]
            whole = pl.ds(start + k * A_COLS, size)
            final[g, k] = whole, net.send(rows_of(g, k, 0, 1 - h), last.at[:, whole], across)
    for g in range(len(GROUPS[0])):
        for k in range(2):
            whole, copy = final[g, k]
            copy.wait_recv()
            red[:, whole] = rows_of(g, k, 0, h)[...].astype(F32) + last[:, whole].astype(F32)
    kept_here.wait()
    for copy in moved[1:]:
        copy.wait_recv()
    net.drain(moved[:1])


def reduce_grads(kb, gb, sg, out, gin, gin_b):
    def pair(cols, rows, count=2):
        return pltpu.VMEM((count, rows, cols), BF16)

    return pl.pallas_call(
        reduce_body,
        out_shape=(jax.ShapeDtypeStruct((32, W_COLS), F32),
                   jax.ShapeDtypeStruct((SM_ROWS, SM_COLS), F32),
                   jax.ShapeDtypeStruct((512, 512), BF16),
                   jax.ShapeDtypeStruct((512, 512), F32)),
        in_specs=[any_spec()] * 6,
        out_specs=(vmem_spec(), vmem_spec(), any_spec(), any_spec()),
        scratch_shapes=[
            pltpu.VMEM((ROWS, KB_COLS), BF16), pltpu.VMEM((ROWS, GB_COLS), BF16),
            pltpu.VMEM((SM_ROWS, SM_COLS), F32),
            *[pltpu.VMEM((n, SM_ROWS, SM_COLS), F32) for n in (4, 4, 2, 2)],
            *[pltpu.VMEM((256, 512), kind) for kind in (BF16, BF16, F32, BF16)],
            pltpu.VMEM((SEQ, 512), F32),
            *[pltpu.VMEM((4, 4, 64, 256), BF16)] * 4, pltpu.VMEM((2, 4, 4, 2, 16, 256), BF16),
            pair(A_COLS, 256, 4), pair(B_COLS, 256, 4), pair(A_COLS, 256, 4), pair(B_COLS, 256, 4),
            pair(A_COLS, 128), pair(B_COLS, 128), pair(A_COLS, 256), pair(B_COLS, 256),
            pair(A_COLS, 32), pair(B_COLS, 32),
            pltpu.VMEM((2, 2, 32, A_COLS), BF16), pltpu.VMEM((2, 2, 32, B_COLS), BF16),
            pltpu.VMEM((32, W_COLS), BF16),
            pltpu.SemaphoreType.DMA((REDUCE_COPIES,)), pltpu.SemaphoreType.DMA((REDUCE_COPIES,)),
            pltpu.SemaphoreType.DMA((10,))],
        compiler_params=pltpu.CompilerParams(
            collective_id=1, has_side_effects=True, vmem_limit_bytes=VMEM_LIMIT),
        name="reduce_grads",
    )(kb, gb, sg, out, gin, gin_b)


def spread(values, each, whole):
    turn = lax.broadcasted_iota(jnp.int32, (128, whole), 0)
    lane = lax.broadcasted_iota(jnp.int32, (128, whole), 1)
    line = lax.broadcasted_iota(jnp.int32, (64, whole), 0)
    where = lax.broadcasted_iota(jnp.int32, (64, whole), 1)
    pick = jnp.where((lane % each == turn) & (turn < each), 1.0, 0.0).astype(BF16)
    return jnp.sum(
        jnp.where(where // each == line, dot_plain(values, pick), 0.0), axis=0, keepdims=True)


def prepare_body(w, heads, sm, wst, tile, sem):
    copies = [pltpu.make_async_copy(
        w.at[:, :, :, :, pl.ds(0, 16), pl.ds(384, 128)], tile, sem.at[0])]
    for t in range(2):
        for half in range(2):
            copies.append(pltpu.make_async_copy(
                w.at[t, :, :, :, pl.ds(16 * half, 16), pl.ds(2 * D, 128)],
                wst.at[t, :, :, :, :, pl.ds(128 * half, 128)], sem.at[1 + 2 * t + half]))
    for copy in copies:
        copy.start()
    sm[...] = jnp.zeros_like(sm)
    for t in range(2):
        sm[SM_BIAS:SM_BIAS + 1, 128 * t:128 * t + 128] = heads[t, 0:1, :]
        sm[SM_DEC:SM_DEC + 1, 128 * t:128 * t + 128] = heads[t, 1:2, :]
        for p in range(6):
            c = 768 * t + 128 * p
            lane = lax.broadcasted_iota(jnp.int32, (1, 128), 1)
            sm[SM_SKIP:SM_SKIP + 1, c:c + 128] = jnp.where(
                lane < HEAD, heads[t, 2:3, 2 * p:2 * p + 1], heads[t, 2:3, 2 * p + 1:2 * p + 2])
    copies[0].wait()
    lines = tile[...].reshape(64, 16, 128).astype(F32)

    def line(row, first):
        return pltpu.roll(lines[:, row, :], 128 - first, 1).astype(BF16)

    sm[SM_G1:SM_G1 + 1, 0:D] = spread(line(0, 12), 16, D)
    sm[SM_G2:SM_G2 + 1, 0:D] = spread(line(0, 28), 16, D)
    for k in range(4):
        sm[SM_CONV + k:SM_CONV + k + 1, :] = spread(line(1, 12 + 24 * k), 24, SM_COLS)
        sm[SM_CST + k:SM_CST + k + 1, 0:256] = spread(line(0, 44 + 4 * k), 4, 256)
    for copy in copies[1:]:
        copy.wait()


def prepare(w, all_heads):
    sm, wst = pl.pallas_call(
        prepare_body,
        out_shape=(jax.ShapeDtypeStruct((SM_ROWS, SM_COLS), F32),
                   jax.ShapeDtypeStruct((2, 4, 4, 2, 16, 256), BF16)),
        in_specs=[any_spec(), vmem_spec()],
        out_specs=(vmem_spec(), vmem_spec()),
        scratch_shapes=[pltpu.VMEM((2, 4, 4, 2, 16, 128), BF16), pltpu.SemaphoreType.DMA((5,))],
        compiler_params=pltpu.CompilerParams(vmem_limit_bytes=VMEM_LIMIT),
        name="prepare_small",
    )(w, all_heads)
    return sm, wst.reshape(D, 256)


def finish_body(at, red, small, coming, stayed, final, igrad, g1, g2, query, key, value, attn,
                gate, ssm, step, conv, state, cst, bias, dec, skip, ssm_out, ffn_gate, ffn_up,
                ffn_down):
    first, core, place = at[0], at[1], at[2]
    final[...] = jnp.where(first == 1, coming[...], stayed[...].astype(BF16))
    igrad[...] = jnp.where(first == 1, stayed[...], coming[...].astype(F32))
    query[0] = red[:, 0:256]
    kv = red[:, 256:384]
    key[0] = kv[:, 0:64]
    value[0] = pltpu.roll(kv, 64, 1)[:, 0:64]
    step[0] = red[:, 384:512][:, 0:12]
    gate[0] = red[:, 512:1280]
    ssm[0] = red[:, 1280:2048]
    state[0, :, 0:128] = red[0:16, 2 * D:W_OUT]
    state[0, :, 128:256] = red[16:32, 2 * D:W_OUT]
    attn[0] = red[:, W_OUT:W_OUT + 256]
    ssm_out[0] = red[:, W_OUT + 256:W_FFN]
    ffn_gate[0] = red[:, W_FFN:W_FFN + D]
    ffn_up[0] = red[:, W_FFN + D:W_DN]
    ffn_down[0] = red[:, W_DN:W_COLS]

    def mine(rows, cols, size):
        v = small[rows, pl.ds(pl.multiple_of(place * size // 128 * 128, 128), cols)]
        return pltpu.roll(v, (cols - place * size % 128) % cols, 1)

    for k, (ref, size) in enumerate(((g1, 16), (g2, 16))):
        ref[...] = mine(pl.ds(0, 8), 128, size)[k:k + 1, 0:size]
    pair = jnp.concatenate([small[0:8, :], jnp.zeros((8, 128), F32)], axis=1)
    turned = pltpu.roll(pair, (SM_COLS + 128 - place * 24) % (SM_COLS + 128), 1)
    conv[0] = turned[SM_CONV:SM_CONV + 4, 0:24]
    tail = small[:, 0:256]
    turned = pltpu.roll(tail, (256 - place * 4) % 256, 1)
    cst[0] = turned[SM_CST:SM_CST + 4, 0:4]
    for row, ref in ((SM_BIAS, bias), (SM_DEC, dec)):
        v = small[8:16, pl.ds(pl.multiple_of(core * 128, 128), 128)]
        ref[...] = v[row - 8:row - 7, 0:12]
    lane = lax.broadcasted_iota(jnp.int32, (8, 128), 1)
    sums = jnp.zeros((8, 128), F32)
    for p in range(6):
        v = small[8:16, pl.ds(pl.multiple_of(core * 768 + 128 * p, 128), 128)]
        even = jnp.sum(jnp.where(lane < HEAD, v, 0.0), axis=1, keepdims=True)
        odd = jnp.sum(jnp.where(lane < HEAD, 0.0, v), axis=1, keepdims=True)
        sums = jnp.where(lane == 2 * p, even, jnp.where(lane == 2 * p + 1, odd, sums))
    skip[...] = sums[SM_SKIP - 8:SM_SKIP - 7, 0:12]


def finish(at, red, small, coming, stayed):
    shapes = [((512, 512), BF16)] + [(shape, F32) for shape in (
        (512, 512), (1, 16), (1, 16), (1, 32, 256), (1, 32, 64), (1, 32, 64), (1, 32, 256),
        (1, 32, 768), (1, 32, 768), (1, 32, 12), (1, 4, 24), (1, 16, 256), (1, 4, 4), (1, 12),
        (1, 12), (1, 12), (1, 32, 768), (1, 32, 1024), (1, 32, 1024), (1, 32, 1024))]
    outs = pl.pallas_call(
        finish_body,
        out_shape=tuple(jax.ShapeDtypeStruct(*shape) for shape in shapes),
        in_specs=[smem_spec()] + [vmem_spec()] * 4,
        out_specs=tuple(vmem_spec() for _ in shapes),
        compiler_params=pltpu.CompilerParams(vmem_limit_bytes=VMEM_LIMIT),
        name="finish_outputs",
    )(at, red, small, coming, stayed)
    turned = (7, 17, 20)
    return tuple(v.swapaxes(1, 2) if k in turned else v for k, v in enumerate(outs))


def local(tokens, segments, cotangent, gain_one, gain_two, w_query, key_weight, value_weight,
          w_attn_out, w_gate_ssm, w_ssm_in, w_step, conv_ssm, w_state, conv_state, step_bias,
          decay_log, skip_gain, w_ssm_out, w_ffn_gate, w_ffn_up, w_ffn_down):
    core = lax.axis_index("tensor")
    place = core * lax.axis_size("dp") + lax.axis_index("dp")
    first = lax.axis_index("section") == 0
    first_i = first.astype(jnp.int32)

    state = w_state[0]
    spare = 116
    one = jnp.concatenate([gain_one[0], gain_two[0], conv_state[0].ravel()])
    two = conv_ssm[0].ravel()
    smalls = jnp.concatenate([
        jnp.pad(v, (0, spare - v.shape[0]))[None] for v in (one, two)], axis=0)
    smalls = jnp.pad(smalls, ((0, 30), (0, 0)))
    heads = jnp.pad(jnp.concatenate([step_bias, decay_log, skip_gain]), ((0, 5), (0, 116)))
    packed = jnp.concatenate([
        w_query[0], key_weight[0], value_weight[0], w_step[0], smalls,
        w_gate_ssm[0], w_ssm_in[0], jnp.concatenate([state[:, 0:128], state[:, 128:256]], axis=0),
        w_attn_out[0].T, w_ssm_out[0].T, w_ffn_gate[0], w_ffn_up[0], w_ffn_down[0].T], axis=1)
    tok = lax.dynamic_slice_in_dim(tokens, core * ROWS, ROWS)
    cot = lax.dynamic_slice_in_dim(cotangent, core * ROWS, ROWS)
    tab = tables_of(lax.dynamic_slice_in_dim(segments, core * ROWS, ROWS).reshape(2, SEQ))
    gathered, all_heads, cot, tab_late = gather_weights(packed, heads, cot, tab)
    tab = jnp.where(first, tab, tab_late)
    sm, wst = prepare(gathered, all_heads)
    weights = gathered.reshape(2, D, W_COLS)

    real_first = jnp.stack([jnp.where(first, 0, 1), first_i])
    real_second = jnp.stack([jnp.where(first, 1, 0), first_i])
    nothing = jnp.zeros((ROWS, D), BF16)
    out, *kept = fwd_call(real_first, tok, nothing, tab, sm, wst, weights, ())
    received = relay(out, 2)
    out, *kept = fwd_call(real_second, tok, received, tab, sm, wst, weights, kept)
    _, gin_b, *grads = bwd_call(real_second, cot, nothing, tab, sm, wst, weights, *kept, ())
    received = relay(gin_b, 3)
    gin, gin_b, *grads = bwd_call(real_first, cot, received, tab, sm, wst, weights, *kept, grads)

    red, small, coming, stayed = reduce_grads(kept[1], grads[0], grads[1], out, gin, gin_b)
    at = jnp.stack([first_i, core, place])
    return finish(at, red, small, coming, stayed)


def solution(mesh):
    rows = P("dp", None)
    flat = P("section", ("tensor", "dp"))
    split_in = P("section", "dp", "tensor")
    split_out = P("section", "tensor", "dp")
    kernel = P("section", None, ("tensor", "dp"))
    head = P("section", "tensor")
    state = P("section", ("tensor", "dp"), None)
    params = (flat, flat, split_in, split_in, split_in, split_out, split_in, split_in, split_in,
              kernel, state, kernel, head, head, head, split_out, split_in, split_in, split_out)
    halves = P("dp", "section")
    return jax.shard_map(
        local, mesh=mesh, in_specs=(rows, P("dp"), rows, *params),
        out_specs=(halves, halves, *params), check_vma=False)
```
